128 devices in a mesh: dp: 8 (over z, y_lo), tensor: 16 (over y_hi, x, core).
Axes of the slice: x: 4, y: 4 (y_hi: 2, y_lo: 2; y = y_hi * 2 + y_lo), z: 4, core: 2. Of those that a mesh axis runs over, the one named last changes fastest.
Arguments:
- x_rows: bfloat16 [2048, 4096], P('dp'), may hold values from -6 to 6
- lengths: int32 [16], P('dp'), may hold values from 1 to 128, 1280 in all
- routes: int32 [2048, 2], P('dp'), may hold values from 0 to 7, all different within a row; in each aligned block of 256 rows (0 to 255, 256 to 511, ...) at most 96 rows name the same one
- conv_state: bfloat16 [16, 3, 8192], P('dp', None, 'tensor'), may hold values from -6 to 6
- ssm_state: float32 [16, 16, 8192], P('dp', None, 'tensor'), may hold values from -6 to 6
- norm1_gain: float32 [4096], replicated, may hold values from 0.5 to 1.5
- in_x: bfloat16 [4096, 8192], P('dp', 'tensor'), may hold values from -0.09375 to 0.09375
- in_z: bfloat16 [4096, 8192], P('dp', 'tensor'), may hold values from -0.09375 to 0.09375
- conv_w: float32 [4, 8192], P(None, 'tensor'), may hold values from -3 to 3
- conv_b: float32 [8192], P('tensor'), may hold values from -3 to 3
- x_dt: bfloat16 [8192, 512], P('tensor'), may hold values from -0.0625 to 0.0625
- x_bc: bfloat16 [8192, 32], P('tensor'), may hold values from -0.0625 to 0.0625
- dt_proj: bfloat16 [512, 8192], P(None, 'tensor'), may hold values from -0.25 to 0.25
- dt_bias: float32 [8192], P('tensor'), may hold values from -5 to -2
- decay_rate: float32 [16, 8192], P(None, 'tensor'), may hold values from 0.05 to 4
- skip: float32 [8192], P('tensor'), may hold values from 0.5 to 1.5
- out_w: bfloat16 [8192, 4096], P('tensor', 'dp'), may hold values from -0.0625 to 0.0625
- norm2_gain: float32 [4096], replicated, may hold values from 0.5 to 1.5
- router: bfloat16 [4096, 8], replicated, may hold values from -0.09375 to 0.09375
- w_gate: bfloat16 [8, 4096, 12288], P('dp', None, 'tensor'), may hold values from -0.09375 to 0.09375
- w_up: bfloat16 [8, 4096, 12288], P('dp', None, 'tensor'), may hold values from -0.09375 to 0.09375
- w_down: bfloat16 [8, 12288, 4096], P('dp', 'tensor'), may hold values from -0.0546875 to 0.0546875
Outputs:
- out_rows: bfloat16 [2048, 4096], P('dp')
- ssm_final: float32 [16, 16, 8192], P('dp', None, 'tensor')
The draws below stay inside these ranges and needn't reach their ends.
Inputs may be any that keep to these rules, and one draw needn't show every extreme that they name: `lengths`: every request has at least one valid token, and some request has all 128. `routes`: a token's 2 experts differ; in each aligned block of 256 rows (the tokens of one request group) no expert is named by more than 96 rows, and some block names some expert exactly 96 times.
All inputs are finite; a program needn't handle non-finite values. No bound on the sum of `lengths` on one device may be relied on, other than what follows from the above.
Results may differ from the reference program's by a relative error of at most 0.023.
Values may be sent and summed in bfloat16 or wider, within the bound.
No kernel may reach another device: no remote copies, remote signals or barrier semaphores. Data moves between devices by JAX's collectives and lax.ppermute only.
A program may use at most 128 MiB of HBM per device.

```python
import math
import jax
import jax.numpy as jnp
import numpy as np
from jax import lax

D = 4096
DI = 8192
STATE = 16
RANK = 512
CONV = 4
EXPERTS = 8
TOP = 2
FF = 12288
SPAN = 128
REQUESTS = 16
TOKEN_COUNT = 2048
ROWS = 256
CAP = 96
N_TENSOR = 16


def level_of(stream_key, extent, pieces, least, top_value):
    loudness, own = 1.0, jax.random.fold_in(stream_key, 6)
    for axis_at, shards_of in pieces:
        heights = jnp.exp(jax.random.uniform(jax.random.fold_in(own, axis_at), (shards_of,), jnp.float32, least / len(pieces), top_value / len(pieces)))
        loudness = loudness * jnp.repeat(heights, extent[axis_at] // shards_of).reshape([-1 if axis == axis_at else 1 for axis in range(len(extent))])
    return loudness


def split_up(amount, total, reach, lean):
    weights = [(1 << 20) // math.isqrt(rank ** lean) + 1 for rank in range(2, amount + 1)]
    rest, holding = total - reach - (amount - 1), [1] * (amount - 1)
    while rest > 0:
        movable = [i for i in range(amount - 1) if holding[i] < reach]
        pool, budget = sum([weights[i] for i in movable]), rest
        for i in movable:
            more = min(reach - holding[i], max(1, budget * weights[i] // pool), rest)
            holding[i] = holding[i] + more
            rest = rest - more
    return np.array([reach] + holding)


def ragged_sizes(rng, count, total, reach, lean):
    if count == 2:
        one = jax.random.randint(rng, (), max(1, total - reach), min(reach, total - 1) + 1)
        return jnp.stack([one, total - one])
    sizes = jnp.asarray(split_up(count, total, reach, lean), jnp.int32)
    twos = (count - 1) // 2
    donor, sink = sizes[1:1 + 2 * twos:2], sizes[2:2 + 2 * twos:2]
    room = jnp.minimum(donor - 1, reach - sink)
    moved = jax.random.randint(jax.random.fold_in(rng, 1), (twos,), 0, 1 << 20) % (room + 1)
    sizes = sizes.at[1:1 + 2 * twos:2].set(donor - moved).at[2:2 + 2 * twos:2].set(sink + moved)
    return sizes[jax.random.permutation(jax.random.fold_in(rng, 2), count)]


def routed_block(stream_key, own, number, rows, amount, top, most, slope):
    ranking = jax.random.permutation(stream_key, amount)
    packed, usual = portions_of(amount, rows * top, most, slope, True), portions_of(amount, rows * top, most, slope, False)
    places = jnp.arange(amount)

    def named(tallies, rotation):
        used = int((tallies > 0).sum())
        fixed = max(1, used // 4)
        shifted = fixed + (places - fixed + rotation * (used - fixed)) % max(1, amount - fixed)
        return jnp.zeros((amount,), jnp.int32).at[ranking[jnp.where(places < fixed, places, shifted)]].set(jnp.asarray(tallies, jnp.int32))

    tallies = jnp.where(number % 4 == 0, named(packed, number // 4), named(usual, number - number // 4 - 1))
    mixed = jax.random.permutation(jax.random.fold_in(own, 3), amount)
    source_of, receiver = mixed[0:amount // 2 * 2:2], mixed[1:amount // 2 * 2:2]
    slack = jnp.minimum(tallies[source_of] - 1, most - tallies[receiver]) // 2
    slack = jnp.where((source_of == ranking[0]) | (receiver == ranking[0]) | (tallies[receiver] == 0), 0, jnp.maximum(slack, 0))
    shifted = jax.random.randint(jax.random.fold_in(own, 4), (amount // 2,), 0, 1 << 20) % (slack + 1)
    tallies = tallies.at[source_of].add(-shifted).at[receiver].add(shifted)
    members = jnp.searchsorted(jnp.cumsum(tallies), jnp.arange(rows * top), side="right").astype(jnp.int32)
    grid = members.reshape(top, rows).T
    grid = grid[jax.random.permutation(jax.random.fold_in(own, 1), rows)]
    rotation = jax.random.randint(jax.random.fold_in(own, 2), (rows, 1), 0, top)
    return jnp.take_along_axis(grid, (jnp.arange(top)[None, :] + rotation) % top, axis=1)


def portions_of(number_of, total, reach, slope, full):
    portions = [(1 << 20) // math.isqrt(rank ** slope) + 1 for rank in range(1, number_of + 1)]
    largest = reach if full else min(reach, max(-(-total // number_of), total * portions[0] // sum(portions)))
    least = 1 if total - largest >= number_of - 1 else 0
    holding, spare = [largest] + [least] * (number_of - 1), total - largest - least * (number_of - 1)
    while spare > 0:
        candidates = [i for i in range(1, number_of) if holding[i] < largest] or [i for i in range(1, number_of) if holding[i] < reach]
        mass, budget = sum([portions[i] for i in candidates]), spare
        for i in candidates:
            extra = min(reach - holding[i], max(1, budget * portions[i] // mass), spare)
            holding[i] = holding[i] + extra
            spare = spare - extra
    return np.array(holding)


def bell_draw(rng, extent, deviation, most, shards=(), kind=jnp.bfloat16):
    result = jax.random.normal(rng, extent, jnp.float32) * deviation
    if len(shards) > 0:
        result = level_of(rng, extent, shards, -0.22, 0.18) * result
    return jnp.clip(result, min=-most, max=most).astype(kind)


def setup_inputs(seed: int = 0) -> dict:
    streams_of = jax.random.split(jax.random.key(seed), 23)
    x_rows = bell_draw(streams_of[0], (TOKEN_COUNT, D), 1.0, 6.0, ((0, 8),))
    lengths = ragged_sizes(streams_of[1], REQUESTS, REQUESTS * SPAN * 5 // 8, SPAN, 2).astype(jnp.int32)
    routes_keys = jax.random.split(jax.random.fold_in(streams_of[2], 1), TOKEN_COUNT // ROWS)
    routes_turns = jax.random.permutation(jax.random.fold_in(streams_of[2], 3), TOKEN_COUNT // ROWS)
    routes = jax.vmap(lambda own, number: routed_block(jax.random.fold_in(streams_of[2], 2), own, number, ROWS, EXPERTS, TOP, CAP, 2))(routes_keys, routes_turns).reshape((TOKEN_COUNT, TOP))
    conv_state = bell_draw(streams_of[3], (REQUESTS, CONV - 1, DI), 1.0, 6.0, ((0, 8), (2, 16)))
    ssm_state = bell_draw(streams_of[4], (REQUESTS, STATE, DI), 1.0, 6.0, ((0, 8), (2, 16)), jnp.float32)
    norm1_gain = jnp.clip(jax.random.uniform(streams_of[5], (D,), jnp.float32, 0.5, 1.5), 0.5, 1.5)
    in_x = bell_draw(streams_of[6], (D, DI), D ** -0.5, 0.09375, ((0, 8), (1, 16)))
    in_z = bell_draw(streams_of[7], (D, DI), D ** -0.5, 0.09375, ((0, 8), (1, 16)))
    conv_w = bell_draw(streams_of[8], (CONV, DI), 0.5, 3.0, ((1, 16),), jnp.float32)
    conv_b = bell_draw(streams_of[9], (DI,), 0.5, 3.0, ((0, 16),), jnp.float32)
    x_dt = bell_draw(streams_of[10], (DI, RANK), DI ** -0.5, 0.0625, ((0, 16),))
    x_bc = bell_draw(streams_of[11], (DI, 2 * STATE), DI ** -0.5, 0.0625, ((0, 16),))
    dt_proj = bell_draw(streams_of[12], (RANK, DI), RANK ** -0.5, 0.25, ((1, 16),))
    dt_bias = jnp.clip(-5.0 + 3.0 * jax.random.uniform(streams_of[13], (DI,), jnp.float32) ** level_of(streams_of[13], (DI,), ((0, 16),), -0.2, 0.2), -5.0, -2.0)
    decay_rate = jnp.clip(jnp.exp(math.log(4.0) - 4.3820266 * jax.random.uniform(streams_of[14], (STATE, DI), jnp.float32) ** level_of(streams_of[14], (STATE, DI), ((1, 16),), -0.2, 0.2)), 0.05, 4.0)
    skip = jnp.clip(0.5 + 1.0 * jax.random.uniform(streams_of[15], (DI,), jnp.float32) ** level_of(streams_of[15], (DI,), ((0, 16),), -0.2, 0.2), 0.5, 1.5)
    out_w = bell_draw(streams_of[16], (DI, D), DI ** -0.5, 0.0625, ((0, 16), (1, 8)))
    norm2_gain = jnp.clip(jax.random.uniform(streams_of[17], (D,), jnp.float32, 0.5, 1.5), 0.5, 1.5)
    router = bell_draw(streams_of[18], (D, EXPERTS), D ** -0.5, 0.09375)
    w_gate = bell_draw(streams_of[19], (EXPERTS, D, FF), D ** -0.5, 0.09375, ((0, 8), (2, 16)))
    w_up = bell_draw(streams_of[20], (EXPERTS, D, FF), D ** -0.5, 0.09375, ((0, 8), (2, 16)))
    w_down = bell_draw(streams_of[21], (EXPERTS, FF, D), FF ** -0.5, 0.0546875, ((0, 8), (1, 16)))
    return {"x_rows": x_rows, "lengths": lengths, "routes": routes, "conv_state": conv_state, "ssm_state": ssm_state, "norm1_gain": norm1_gain, "in_x": in_x, "in_z": in_z, "conv_w": conv_w, "conv_b": conv_b, "x_dt": x_dt, "x_bc": x_bc, "dt_proj": dt_proj, "dt_bias": dt_bias, "decay_rate": decay_rate, "skip": skip, "out_w": out_w, "norm2_gain": norm2_gain, "router": router, "w_gate": w_gate, "w_up": w_up, "w_down": w_down}


def norm_rows(values, gain):
    values = values.astype(jnp.float32)
    mean_square = lax.optimization_barrier(jnp.mean(values * values, axis=-1, keepdims=True))
    return values * lax.rsqrt(mean_square + 1e-05) * gain

def expert_pass(unit, routes, w_gate, w_up, w_down):
    capacity_total = TOKEN_COUNT // ROWS * CAP
    flat_routes = routes.reshape(-1)
    token_of = (jnp.arange(TOKEN_COUNT * TOP, dtype=jnp.int32) // TOP).astype(jnp.int32)
    block_width = FF // N_TENSOR

    def one_expert(accumulated, inputs):
        expert_id, gate_w, up_w, down_w = inputs
        hit_flag = (flat_routes == expert_id).astype(jnp.int32)
        rank_of = (jnp.cumsum(hit_flag) - hit_flag).astype(jnp.int32)
        target = jnp.where(hit_flag > 0, rank_of, capacity_total).astype(jnp.int32)
        group_members = jnp.zeros((capacity_total,), jnp.int32).at[target].set(token_of, mode='drop')
        inputs_rows = unit[group_members]
        gate_part = jnp.dot(inputs_rows, gate_w, preferred_element_type=jnp.float32)
        up_part = jnp.dot(inputs_rows, up_w, preferred_element_type=jnp.float32)
        active = (jax.nn.silu(gate_part) * up_part).astype(jnp.bfloat16)
        block_list = active.reshape(capacity_total, N_TENSOR, block_width).astype(jnp.float32)
        down_projection_blocks = down_w.reshape(N_TENSOR, block_width, D).astype(jnp.float32)
        partial_value_sum = jnp.einsum('mzp,zph->zmh', block_list, down_projection_blocks).astype(jnp.bfloat16)
        partial_value_sum = lax.optimization_barrier(partial_value_sum)
        layer_output = lax.optimization_barrier(jnp.sum(partial_value_sum.astype(jnp.float32), axis=0)).astype(jnp.bfloat16)
        picked = layer_output[jnp.minimum(rank_of, capacity_total - 1)].astype(jnp.float32)
        return (accumulated + jnp.where(hit_flag[:, None] > 0, picked, 0.0), None)
    initial = jnp.zeros((TOKEN_COUNT * TOP, D), jnp.float32)
    accumulated, _ = lax.scan(one_expert, initial, (jnp.arange(EXPERTS, dtype=jnp.int32), w_gate, w_up, w_down))
    return accumulated.reshape(TOKEN_COUNT, TOP, D)

def reference(x_rows, lengths, routes, conv_state, ssm_state, norm1_gain, in_x, in_z, conv_w, conv_b, x_dt, x_bc, dt_proj, dt_bias, decay_rate, skip, out_w, norm2_gain, router, w_gate, w_up, w_down):
    normed = norm_rows(x_rows, norm1_gain).astype(jnp.bfloat16)
    x_inner = jnp.dot(normed, in_x, preferred_element_type=jnp.float32).astype(jnp.bfloat16)
    z_gate = jnp.dot(normed, in_z, preferred_element_type=jnp.float32).astype(jnp.bfloat16)
    history = jnp.concatenate([conv_state, x_inner.reshape(REQUESTS, SPAN, DI)], axis=1).astype(jnp.float32)
    conv_sum = conv_b + sum((conv_w[shift_index] * history[:, shift_index:shift_index + SPAN] for shift_index in range(CONV)))
    conv_out = jax.nn.silu(conv_sum).astype(jnp.bfloat16).reshape(TOKEN_COUNT, DI)
    step_low = jnp.dot(conv_out, x_dt, preferred_element_type=jnp.float32).astype(jnp.bfloat16)
    bc_sum = jnp.dot(conv_out, x_bc, preferred_element_type=jnp.float32)
    valid_mask = (jnp.arange(SPAN, dtype=jnp.int32)[None, :] < lengths[:, None]).astype(jnp.float32)
    step_size = jax.nn.softplus(jnp.dot(step_low, dt_proj, preferred_element_type=jnp.float32) + dt_bias)
    step_size = step_size.reshape(REQUESTS, SPAN, DI) * valid_mask[:, :, None]
    entry_gain = bc_sum[:, :STATE].reshape(REQUESTS, SPAN, STATE)
    read_gain = bc_sum[:, STATE:].reshape(REQUESTS, SPAN, STATE)
    signal = conv_out.reshape(REQUESTS, SPAN, DI).astype(jnp.float32)

    def advance(state, inputs):
        step_now, signal_now, entry_now, read_now = inputs
        state = jnp.exp(-step_now[:, None, :] * decay_rate) * state + (step_now * signal_now)[:, None, :] * entry_now[:, :, None]
        return (state, lax.optimization_barrier(jnp.sum(read_now[:, :, None] * state, axis=1)))
    ssm_final, mixer_out = lax.scan(advance, ssm_state, (jnp.swapaxes(step_size, 0, 1), jnp.swapaxes(signal, 0, 1), jnp.swapaxes(entry_gain, 0, 1), jnp.swapaxes(read_gain, 0, 1)))
    mixer_y = jnp.swapaxes(mixer_out, 0, 1) + skip * signal
    gate_act = jax.nn.silu(z_gate.reshape(REQUESTS, SPAN, DI).astype(jnp.float32))
    gated = (mixer_y * gate_act * valid_mask[:, :, None]).astype(jnp.bfloat16).reshape(TOKEN_COUNT, DI)
    hidden = (x_rows.astype(jnp.float32) + jnp.dot(gated, out_w, preferred_element_type=jnp.float32)).astype(jnp.bfloat16)
    unit = norm_rows(hidden, norm2_gain).astype(jnp.bfloat16)
    logits = jnp.dot(unit, router, preferred_element_type=jnp.float32)
    chosen = routes[:, :, None] == jnp.arange(EXPERTS, dtype=jnp.int32)
    gates = lax.optimization_barrier(jnp.sum(jnp.where(chosen, jax.nn.sigmoid(logits)[:, None, :], 0.0), axis=-1))
    expert_out = expert_pass(unit, routes, w_gate, w_up, w_down)
    out_rows = (hidden.astype(jnp.float32) + lax.optimization_barrier(jnp.sum(gates[:, :, None] * expert_out, axis=1))).astype(jnp.bfloat16)
    return (out_rows, ssm_final)
```

```python
import jax
import jax.numpy as jnp
from jax import lax
from jax.sharding import Mesh
from jax.sharding import PartitionSpec as P
from jax.experimental import pallas as pl
from jax.experimental.pallas import tpu as pltpu

F32 = jnp.float32
BF16 = jnp.bfloat16
DP = ("z", "ylo")
TENSOR = ("yhi", "x", "core")
CHIPS = ("yhi", "x")
EPS = 1e-05
LOG2E = 1.4426950408889634


def params(megabytes=48):
    return pltpu.CompilerParams(vmem_limit_bytes=megabytes << 20)


def call(body, scalars, grid, in_specs, out_specs, out_shape, scratch=(), cost=None):
    spec = pltpu.PrefetchScalarGridSpec(
        num_scalar_prefetch=len(scalars),
        grid=grid,
        in_specs=in_specs,
        out_specs=out_specs,
        scratch_shapes=scratch,
    )
    return pl.pallas_call(
        body, grid_spec=spec, out_shape=out_shape, compiler_params=params(), cost_estimate=cost
    )


def exchange(value, axes):
    return lax.all_to_all(value, axes, split_axis=0, concat_axis=0, tiled=True)


def spread(value):
    return exchange(jnp.broadcast_to(value[None], (8,) + value.shape), CHIPS)


def swap_core(value):
    return lax.ppermute(value, "core", [(0, 1), (1, 0)])


def sigmoid(value):
    return 1.0 / (1.0 + jnp.exp(-value))


def silu(value):
    return value * sigmoid(value)


def norm_split(core, x_rows, gain):
    def body(core_ref, x_ref, gain_ref, out_ref):
        values = x_ref[...].astype(F32)
        scale = lax.rsqrt(jnp.mean(values * values, axis=-1, keepdims=True) + EPS)
        normed = (values * scale * gain_ref[...]).astype(BF16)
        for piece in range(8):
            out_ref[piece] = normed[:, piece * 512 : piece * 512 + 512]

    return call(
        body,
        (core,),
        (1,),
        [
            pl.BlockSpec((128, 4096), lambda i, c: (c[0], 0)),
            pl.BlockSpec((1, 4096), lambda i, c: (0, 0)),
        ],
        pl.BlockSpec((8, 128, 512), lambda i, c: (0, 0, 0)),
        jax.ShapeDtypeStruct((8, 128, 512), BF16),
    )(core, x_rows, gain)


def partial_product(own, other, weight):
    def body(own_ref, other_ref, w_ref, out_ref):
        weight_now = w_ref[...]
        for slot, rows_ref in enumerate((own_ref, other_ref)):
            out_ref[:, slot] = (
                jnp.dot(rows_ref[...].reshape(512, 512), weight_now, preferred_element_type=F32)
                .astype(BF16)
                .reshape(4, 128, 512)
            )

    rows = pl.BlockSpec((4, 128, 512), lambda i: (i, 0, 0))
    return call(
        body,
        (),
        (2,),
        [rows, rows, pl.BlockSpec((512, 512), lambda i: (0, 0))],
        pl.BlockSpec((4, 2, 128, 512), lambda i: (i, 0, 0, 0)),
        jax.ShapeDtypeStruct((8, 2, 128, 512), BF16),
    )(own, other, weight)


def conv_project(core, parts, history, conv_w, conv_b, weight):
    def body(core_ref, parts_ref, hist_ref, cw_ref, cb_ref, w_ref, conv_ref, low_ref, line):
        x_inner = jnp.sum(parts_ref[:, 0].astype(F32), axis=0).astype(BF16).astype(F32)
        line[0:8] = hist_ref[0]
        line[8:136] = x_inner
        total = cb_ref[...] + cw_ref[3:4] * x_inner
        for tap in range(3):
            total = total + cw_ref[tap : tap + 1] * line[5 + tap : 133 + tap]
        conv = silu(total).astype(BF16)
        conv_ref[0] = conv
        low_ref[0] = jnp.dot(conv, w_ref[...], preferred_element_type=F32).astype(BF16)

    return call(
        body,
        (core,),
        (2,),
        [
            pl.BlockSpec((8, 1, 128, 512), lambda r, c: (0, r ^ c[0], 0, 0)),
            pl.BlockSpec((1, 8, 512), lambda r, c: (r, 0, 0)),
            pl.BlockSpec((4, 512), lambda r, c: (0, 0)),
            pl.BlockSpec((1, 512), lambda r, c: (0, 0)),
            pl.BlockSpec((512, 640), lambda r, c: (0, 0)),
        ],
        [
            pl.BlockSpec((1, 128, 512), lambda r, c: (r, 0, 0)),
            pl.BlockSpec((1, 128, 640), lambda r, c: (r ^ c[0], 0, 0)),
        ],
        [
            jax.ShapeDtypeStruct((2, 128, 512), BF16),
            jax.ShapeDtypeStruct((2, 128, 640), BF16),
        ],
        (pltpu.VMEM((136, 512), F32),),
    )(core, parts, history, conv_w, conv_b, weight)


def scan_gate(core, lengths, low_own, low_other, z_parts, conv, dt_proj, dt_bias, decay, skip, state):
    def body(
        core_ref,
        len_ref,
        own_ref,
        other_ref,
        z_ref,
        conv_ref,
        dtp_ref,
        dtb_ref,
        decay_ref,
        skip_ref,
        state_ref,
        gated_ref,
        final_ref,
        step_s,
        drive_s,
        trail_s,
        dec_s,
    ):
        dec_s[...] = decay_ref[...] * (-LOG2E)
        lane = lax.broadcasted_iota(jnp.int32, (128, 128), 1)
        row = lax.broadcasted_iota(jnp.int32, (128, 128), 0)
        pick_entry = (row == lane % 16).astype(BF16)
        pick_read = (row == 16 + lane % 16).astype(BF16)
        diagonal = ((lane // 16) == (row % 8)).astype(F32)
        position = lax.broadcasted_iota(jnp.int32, (128, 512), 0)
        reads = []
        for slot, low_ref in enumerate((own_ref, other_ref)):
            request = core_ref[0] ^ slot
            mask = (position < len_ref[request]).astype(F32)
            raw = jnp.dot(low_ref[:, 0:512], dtp_ref[...], preferred_element_type=F32) + dtb_ref[...]
            step = (jnp.maximum(raw, 0.0) + jnp.log(1.0 + jnp.exp(-jnp.abs(raw)))) * mask
            step_s[slot] = step
            drive = (step * conv_ref[request].astype(F32)).astype(BF16)
            tail = low_ref[:, 512:640]
            entry = (jnp.dot(tail, pick_entry, preferred_element_type=F32) * diagonal).astype(BF16)
            reads.append(
                (jnp.dot(tail, pick_read, preferred_element_type=F32) * diagonal).astype(BF16)
            )
            for piece in range(8):
                for half in range(2):
                    at = piece * 16 + half * 8
                    keep = (
                        lax.broadcasted_iota(jnp.int32, (16, 128), 0) // 8 == half
                    ).astype(BF16)
                    drive_s[slot, at * 16 : at * 16 + 128] = lax.dot_general(
                        entry[piece * 16 : piece * 16 + 16] * keep,
                        drive[piece * 16 : piece * 16 + 16],
                        (((0,), (0,)), ((), ())),
                        preferred_element_type=F32,
                    )

        def advance(block, held):
            held = list(held)
            base = pl.multiple_of(block * 8, 8)
            for slot in range(2):
                steps = step_s[slot, pl.ds(base, 8)]
                now = held[slot]
                for offset in range(8):
                    rows = pl.ds(pl.multiple_of(block * 128 + offset * 16, 16), 16)
                    now = jnp.exp2(steps[offset : offset + 1] * dec_s[...]) * now + drive_s[slot, rows]
                    trail_s[slot, rows] = now.astype(BF16)
                held[slot] = now
            return tuple(held)

        first = tuple(state_ref[core_ref[0] ^ slot] for slot in range(2))
        last = lax.fori_loop(0, 16, advance, first)
        for slot in range(2):
            request = core_ref[0] ^ slot
            final_ref[request] = last[slot]
            outs = []
            for piece in range(16):
                outs.append(
                    jnp.dot(
                        reads[slot][piece * 8 : piece * 8 + 8],
                        trail_s[slot, piece * 128 : piece * 128 + 128],
                        preferred_element_type=F32,
                    )
                )
            mask = (position < len_ref[request]).astype(F32)
            mixed = jnp.concatenate(outs, axis=0) + skip_ref[...] * conv_ref[request].astype(F32)
            z_gate = jnp.sum(z_ref[:, slot].astype(F32), axis=0).astype(BF16).astype(F32)
            gated_ref[request] = (mixed * silu(z_gate) * mask).astype(BF16)

    def whole(*shape):
        return pl.BlockSpec(shape, lambda i, c, n: (0,) * len(shape))

    return call(
        body,
        (core, lengths),
        (1,),
        [
            whole(128, 640),
            whole(128, 640),
            whole(8, 2, 128, 512),
            whole(2, 128, 512),
            whole(512, 512),
            whole(1, 512),
            whole(16, 512),
            whole(1, 512),
            whole(2, 16, 512),
        ],
        [whole(2, 128, 512), whole(2, 16, 512)],
        [
            jax.ShapeDtypeStruct((2, 128, 512), BF16),
            jax.ShapeDtypeStruct((2, 16, 512), F32),
        ],
        (
            pltpu.VMEM((2, 128, 512), F32),
            pltpu.VMEM((2, 2048, 512), F32),
            pltpu.VMEM((2, 2048, 512), BF16),
            pltpu.VMEM((16, 512), F32),
        ),
    )(core, lengths, low_own, low_other, z_parts, conv, dt_proj, dt_bias, decay, skip, state)


def half_product(target, rows, weight, weight_spec, received=None):
    row_count, depth = rows.shape

    def body(target_ref, rows_ref, w_ref, *refs):
        out_ref = refs[-1]
        product = jnp.dot(
            rows_ref[...], w_ref[...].reshape(depth, 512), preferred_element_type=F32
        )
        for side in range(2):
            value = product[:, side * 256 : side * 256 + 256]
            if received is not None:
                value = value + refs[0][side].astype(F32)
            out_ref[side] = value.astype(BF16)

    blocks = pl.BlockSpec((2, row_count, 256), lambda i, t: (i, 0, 0))
    operands = (target, rows, weight) + (() if received is None else (received,))
    return call(
        body,
        (target,),
        (4,),
        [pl.BlockSpec((row_count, depth), lambda i, t: (0, 0)), weight_spec]
        + ([] if received is None else [blocks]),
        blocks,
        jax.ShapeDtypeStruct((8, row_count, 256), BF16),
    )(*operands)


def tables_of(routes_t):
    expert = lax.broadcasted_iota(jnp.int32, (8, 256), 0)
    picks = [(expert == routes_t[k : k + 1]) for k in range(2)]
    counts = (picks[0] | picks[1]).astype(BF16)
    earlier = (
        lax.broadcasted_iota(jnp.int32, (256, 256), 0)
        < lax.broadcasted_iota(jnp.int32, (256, 256), 1)
    ).astype(BF16)
    before = jnp.dot(counts, earlier, preferred_element_type=F32)
    place = before + 96.0 * expert.astype(F32)
    slot_row = lax.broadcasted_iota(jnp.int32, (768, 256), 0)
    hit = None
    for pick in picks:
        slot = jnp.sum(jnp.where(pick, place, 0.0), axis=0, keepdims=True).astype(jnp.int32)
        mine = slot_row == slot
        hit = mine if hit is None else hit | mine
    return hit.astype(BF16)


def hidden_dispatch(block, parts, x_rows, routes_t):
    def body(block_ref, parts_ref, x_ref, routes_ref, hidden_ref, out_ref):
        mixer = jnp.sum(parts_ref[...].astype(F32), axis=0)
        hidden = (x_ref[...].astype(F32) + mixer).astype(BF16)
        hidden_ref[...] = hidden
        out_ref[...] = jnp.dot(
            tables_of(routes_ref[...]), hidden, preferred_element_type=F32
        ).astype(BF16)

    return call(
        body,
        (block,),
        (1,),
        [
            pl.BlockSpec((8, 256, 256), lambda i, b: (0, 0, 0)),
            pl.BlockSpec((256, 256), lambda i, b: (0, b[0])),
            pl.BlockSpec((2, 256), lambda i, b: (0, 0)),
        ],
        [
            pl.BlockSpec((256, 256), lambda i, b: (0, 0)),
            pl.BlockSpec((768, 256), lambda i, b: (0, 0)),
        ],
        [
            jax.ShapeDtypeStruct((256, 256), BF16),
            jax.ShapeDtypeStruct((768, 256), BF16),
        ],
    )(block, parts, x_rows, routes_t)


def gate_up(core, own, other, gain, router_row, w_gate, w_up):
    def body(core_ref, own_ref, other_ref, gain_ref, router_ref, wg_ref, wu_ref, out_ref, g_s, u_s, sq_s, lo_s):
        step = pl.program_id(0)

        def work(rows_ref):
            scaled, squares, logits = [], None, None
            for piece in range(4):
                at = slice(piece * 256, piece * 256 + 256)
                value = rows_ref[piece].astype(F32)
                square = value * value
                square = square[:, 0:128] + square[:, 128:256]
                squares = square if squares is None else squares + square
                times = (value * gain_ref[:, at]).astype(BF16)
                scaled.append(times)
                logit = times.astype(F32) * router_ref[:, at]
                logit = logit[:, 0:128] + logit[:, 128:256]
                logits = logit if logits is None else logits + logit
            units = jnp.concatenate(scaled, axis=1)
            gate = jnp.dot(units, wg_ref[...], preferred_element_type=F32)
            up = jnp.dot(units, wu_ref[...], preferred_element_type=F32)

            @pl.when(step == 0)
            def _():
                g_s[...] = gate
                u_s[...] = up
                sq_s[...] = squares
                lo_s[...] = logits

            @pl.when(step > 0)
            def _():
                g_s[...] += gate
                u_s[...] += up
                sq_s[...] += squares
                lo_s[...] += logits

        @pl.when(step < 2)
        def _():
            work(own_ref)

        @pl.when(step >= 2)
        def _():
            work(other_ref)

        @pl.when(step == 3)
        def _():
            scale = lax.rsqrt(jnp.sum(sq_s[...], axis=1, keepdims=True) * (1.0 / 4096.0) + EPS)
            weight = sigmoid(jnp.sum(lo_s[...], axis=1, keepdims=True) * scale)
            out_ref[...] = (silu(g_s[...] * scale) * (u_s[...] * (scale * weight))).astype(BF16)

    def at(i, c):
        return jnp.where(i < 2, c[0] * 2 + i, (1 - c[0]) * 2 + i - 2)

    return call(
        body,
        (core,),
        (4,),
        [
            pl.BlockSpec((4, 768, 256), lambda i, c: (jnp.minimum(i, 1), 0, 0)),
            pl.BlockSpec((4, 768, 256), lambda i, c: (jnp.maximum(i - 2, 0), 0, 0)),
            pl.BlockSpec((1, 1024), lambda i, c: (0, at(i, c))),
            pl.BlockSpec((1, 1024), lambda i, c: (0, at(i, c))),
            pl.BlockSpec((1024, 768), lambda i, c: (at(i, c), 0)),
            pl.BlockSpec((1024, 768), lambda i, c: (at(i, c), 0)),
        ],
        pl.BlockSpec((768, 768), lambda i, c: (0, 0)),
        jax.ShapeDtypeStruct((768, 768), BF16),
        (
            pltpu.VMEM((768, 768), F32),
            pltpu.VMEM((768, 768), F32),
            pltpu.VMEM((768, 128), F32),
            pltpu.VMEM((768, 128), F32),
        ),
    )(core, own, other, gain, router_row, w_gate, w_up)


def sum_parts(parts):
    def body(parts_ref, out_ref):
        out_ref[...] = jnp.sum(parts_ref[...].astype(F32), axis=0).astype(BF16)

    return call(
        body,
        (),
        (4,),
        [pl.BlockSpec((8, 192, 256), lambda i: (0, i, 0))],
        pl.BlockSpec((192, 256), lambda i: (i, 0)),
        jax.ShapeDtypeStruct((768, 256), BF16),
    )(parts)


def combine(hidden, back, routes_t):
    def body(hidden_ref, back_ref, routes_ref, out_ref):
        mixed = lax.dot_general(
            tables_of(routes_ref[...]),
            back_ref[...],
            (((0,), (0,)), ((), ())),
            preferred_element_type=F32,
        )
        out_ref[...] = (hidden_ref[...].astype(F32) + mixed).astype(BF16)

    return call(
        body,
        (),
        (1,),
        [
            pl.BlockSpec((256, 256), lambda i: (0, 0)),
            pl.BlockSpec((768, 256), lambda i: (0, 0)),
            pl.BlockSpec((2, 256), lambda i: (0, 0)),
        ],
        pl.BlockSpec((256, 256), lambda i: (0, 0)),
        jax.ShapeDtypeStruct((256, 256), BF16),
    )(hidden, back, routes_t)


def assemble(core, own, other):
    def body(core_ref, own_ref, other_ref, out_ref):
        for side, ref in enumerate((own_ref, other_ref)):

            @pl.when(pl.program_id(0) == side)
            def _():
                for piece in range(4):
                    out_ref[:, piece * 256 : piece * 256 + 256] = ref[piece]

    return call(
        body,
        (core,),
        (2, 2),
        [
            pl.BlockSpec((4, 256, 256), lambda s, i, c: (jnp.where(s == 0, i, 1), 0, 0)),
            pl.BlockSpec((4, 256, 256), lambda s, i, c: (jnp.where(s == 0, 0, i), 0, 0)),
        ],
        pl.BlockSpec((256, 1024), lambda s, i, c: (0, (c[0] ^ s) * 2 + i)),
        jax.ShapeDtypeStruct((256, 4096), BF16),
    )(core, own, other)


def per_device(
    x_rows,
    lengths,
    routes,
    conv_state,
    ssm_state,
    norm1_gain,
    in_x,
    in_z,
    conv_w,
    conv_b,
    x_dt,
    x_bc,
    dt_proj,
    dt_bias,
    decay_rate,
    skip,
    out_w,
    norm2_gain,
    router,
    w_gate,
    w_up,
    w_down,
):
    core_at = lax.axis_index("core").astype(jnp.int32)
    core = core_at.reshape(1)
    away = (1 - core_at).reshape(1)
    chip_at = lax.axis_index(CHIPS).astype(jnp.int32)
    block = (core_at * 8 + chip_at).reshape(1)
    expert_at = lax.axis_index(DP).astype(jnp.int32)

    out_full = lax.all_gather(out_w, DP, axis=0, tiled=True).reshape(8, 512, 512)
    low_weight = jnp.concatenate([x_dt, x_bc, jnp.zeros((512, 96), BF16)], axis=1)
    history = jnp.pad(conv_state.astype(F32), ((0, 0), (5, 0), (0, 0)))
    routes_t = routes.T
    router_row = lax.dynamic_slice(router, (0, expert_at), (4096, 1)).astype(F32).reshape(1, 4096)

    own = exchange(norm_split(core, x_rows, norm1_gain.reshape(1, 4096)), DP)
    other = swap_core(own)
    x_parts = exchange(partial_product(own, other, in_x), DP)
    z_parts = exchange(partial_product(own, other, in_z), DP)
    conv, low = conv_project(core, x_parts, history, conv_w, conv_b.reshape(1, 512), low_weight)
    low_pair = (low[0].astype(F32) + swap_core(low[1]).astype(F32)).astype(BF16)
    low_sum = jnp.sum(exchange(low_pair.reshape(8, 16, 640), CHIPS).astype(F32), axis=0).astype(BF16)
    low_own = spread(low_sum).reshape(128, 640)
    low_other = swap_core(low_own)
    gated, final = scan_gate(
        core,
        lengths,
        low_own,
        low_other,
        z_parts,
        conv,
        dt_proj,
        dt_bias.reshape(1, 512),
        decay_rate,
        skip.reshape(1, 512),
        ssm_state,
    )
    gated = gated.reshape(256, 512)
    out_spec = pl.BlockSpec((1, 512, 512), lambda i, t: (t[0] * 4 + i, 0, 0))
    far = swap_core(half_product(away, gated, out_full, out_spec))
    mixer_parts = exchange(half_product(core, gated, out_full, out_spec, far), CHIPS)
    hidden, outgoing = hidden_dispatch(block, mixer_parts, x_rows, routes_t)
    arriving = exchange(outgoing.reshape(8, 96, 256), DP).reshape(768, 256)
    rows_own = spread(arriving)
    rows_other = swap_core(rows_own)
    active = gate_up(
        core, rows_own, rows_other, norm2_gain.reshape(1, 4096), router_row, w_gate[0], w_up[0]
    )
    down_spec = pl.BlockSpec((768, 512), lambda i, t: (0, t[0] * 4 + i))
    far_down = swap_core(half_product(away, active, w_down[0], down_spec))
    down_parts = exchange(half_product(core, active, w_down[0], down_spec, far_down), CHIPS)
    back = exchange(sum_parts(down_parts).reshape(8, 96, 256), DP).reshape(768, 256)
    out_own = spread(combine(hidden, back, routes_t))
    out_other = swap_core(out_own)
    return (assemble(core, out_own, out_other), final)


def solution(mesh):
    wide = Mesh(mesh.devices.reshape(4, 2, 2, 4, 2), ("z", "ylo", "yhi", "x", "core"))
    return jax.shard_map(
        per_device,
        mesh=wide,
        in_specs=(
            P(DP, None),
            P(DP),
            P(DP, None),
            P(DP, None, TENSOR),
            P(DP, None, TENSOR),
            P(),
            P(DP, TENSOR),
            P(DP, TENSOR),
            P(None, TENSOR),
            P(TENSOR),
            P(TENSOR, None),
            P(TENSOR, None),
            P(None, TENSOR),
            P(TENSOR),
            P(None, TENSOR),
            P(TENSOR),
            P(TENSOR, DP),
            P(),
            P(),
            P(DP, None, TENSOR),
            P(DP, None, TENSOR),
            P(DP, TENSOR, None),
        ),
        out_specs=(P(DP, None), P(DP, None, TENSOR)),
        check_vma=False,
    )
```

```python
import jax
import jax.numpy as jnp
from jax import lax
from jax.sharding import Mesh
from jax.sharding import PartitionSpec as P
from jax.experimental import pallas as pl
from jax.experimental.pallas import tpu as pltpu

F32 = jnp.float32
BF16 = jnp.bfloat16
DP = ("z", "ylo")
TENSOR = ("yhi", "x", "core")
CHIPS = ("yhi", "x")
EPS = 1e-05
LOG2E = 1.4426950408889634


def params(megabytes=48):
    return pltpu.CompilerParams(vmem_limit_bytes=megabytes << 20)


def call(body, scalars, grid, in_specs, out_specs, out_shape, scratch=(), cost=None):
    spec = pltpu.PrefetchScalarGridSpec(
        num_scalar_prefetch=len(scalars),
        grid=grid,
        in_specs=in_specs,
        out_specs=out_specs,
        scratch_shapes=scratch,
    )
    return pl.pallas_call(
        body, grid_spec=spec, out_shape=out_shape, compiler_params=params(), cost_estimate=cost
    )


def exchange(value, axes):
    return lax.all_to_all(value, axes, split_axis=0, concat_axis=0, tiled=True)


def spread(value):
    return exchange(jnp.broadcast_to(value[None], (8,) + value.shape), CHIPS)


def swap_core(value):
    return lax.ppermute(value, "core", [(0, 1), (1, 0)])


def sigmoid(value):
    return 1.0 / (1.0 + jnp.exp(-value))


def silu(value):
    return value * sigmoid(value)


RING = (0, 3, 1, 2)


def from_below(value):
    return lax.ppermute(value, "z", [(i, (i + 1) % 4) for i in range(4)])


def from_above(value):
    return lax.ppermute(value, "z", [(i, (i - 1) % 4) for i in range(4)])


def after(value, *earlier):
    return lax.optimization_barrier((value,) + earlier)[0]


def swap_pair(value):
    return lax.ppermute(value, "ylo", [(0, 1), (1, 0)])


def gather_ring(block, below, above, halves):
    return block, below, above, from_below(halves[0]), from_above(halves[1])


def second_round(below, above, pair):
    return (
        jnp.concatenate([below[:256], pair[:256]]),
        jnp.concatenate([above[256:], pair[256:]]),
        jnp.concatenate([above[:256], below[256:]]),
    )


def third_round(first, second, third):
    return (
        from_below(first[256:384]),
        from_above(third[128:256]),
        swap_pair(second[:256]),
    )


def norm_split(place, x_rows, gain):
    def body(place_ref, x_ref, gain_ref, own_ref, send_ref):
        request = pl.ds(pl.multiple_of(place_ref[0] * 128, 128), 128)
        for rows, out_ref, member in (
            (slice(0, 256), own_ref, place_ref[2]),
            (request, send_ref, 1 - place_ref[2]),
        ):
            values = x_ref[rows, :].astype(F32)
            scale = lax.rsqrt(jnp.mean(values * values, axis=-1, keepdims=True) + EPS)
            for piece, shift in enumerate(RING):
                at = ((place_ref[1] + shift) % 4) * 2 + member
                columns = pl.ds(pl.multiple_of(at * 512, 512), 512)
                part = x_ref[rows, columns].astype(F32)
                out_ref[piece] = (part * scale * gain_ref[:, columns]).astype(BF16)

    return call(
        body,
        (place,),
        (1,),
        [
            pl.BlockSpec((256, 4096), lambda i, c: (0, 0)),
            pl.BlockSpec((1, 4096), lambda i, c: (0, 0)),
        ],
        [
            pl.BlockSpec((4, 256, 512), lambda i, c: (0, 0, 0)),
            pl.BlockSpec((4, 128, 512), lambda i, c: (0, 0, 0)),
        ],
        [
            jax.ShapeDtypeStruct((4, 256, 512), BF16),
            jax.ShapeDtypeStruct((4, 128, 512), BF16),
        ],
    )(place, x_rows, gain)


def ring_product(rows_ref, blocks):
    total = None
    for piece in range(3):
        term = jnp.dot(rows_ref[piece], blocks[piece][...], preferred_element_type=F32)
        total = term if total is None else total + term
    total = total + jnp.dot(rows_ref[3, :, 0:256], blocks[3][...], preferred_element_type=F32)
    return total + jnp.dot(rows_ref[3, :, 256:512], blocks[4][...], preferred_element_type=F32)


RING_SPECS = [pl.BlockSpec((512, 512), lambda *_: (0, 0))] * 3 + [
    pl.BlockSpec((256, 512), lambda *_: (0, 0))
] * 2


def pair_product(place, own, other, blocks):
    def body(place_ref, own_ref, other_ref, *refs):
        for slot, rows_ref in enumerate((own_ref, other_ref)):
            refs[5][place_ref[0] ^ slot] = ring_product(rows_ref, refs[:5]).astype(BF16)

    return call(
        body,
        (place,),
        (1,),
        [pl.BlockSpec((4, 128, 512), lambda i, c: (0, 0, 0))] * 2 + RING_SPECS,
        pl.BlockSpec((2, 128, 512), lambda i, c: (0, 0, 0)),
        jax.ShapeDtypeStruct((2, 128, 512), BF16),
    )(place, own, other, *blocks)


def own_product(rows, blocks):
    def body(rows_ref, *refs):
        refs[5][...] = ring_product(rows_ref, refs[:5]).reshape(2, 128, 512)

    return call(
        body,
        (),
        (1,),
        [pl.BlockSpec((4, 256, 512), lambda i: (0, 0, 0))] + RING_SPECS,
        pl.BlockSpec((2, 128, 512), lambda i: (0, 0, 0)),
        jax.ShapeDtypeStruct((2, 128, 512), F32),
    )(rows, *blocks)


def conv_project(core, near, far, history, conv_w, conv_b, weight):
    def body(core_ref, near_ref, far_ref, hist_ref, cw_ref, cb_ref, w_ref, conv_ref, low_ref, line):
        x_inner = (near_ref[0] + far_ref[0].astype(F32)).astype(BF16).astype(F32)
        line[0:8] = hist_ref[0]
        line[8:136] = x_inner
        total = cb_ref[...] + cw_ref[3:4] * x_inner
        for tap in range(3):
            total = total + cw_ref[tap : tap + 1] * line[5 + tap : 133 + tap]
        conv = silu(total).astype(BF16)
        conv_ref[0] = conv
        low_ref[0] = jnp.dot(conv, w_ref[...], preferred_element_type=F32).astype(BF16)

    return call(
        body,
        (core,),
        (2,),
        [
            pl.BlockSpec((1, 128, 512), lambda r, c: (r, 0, 0)),
            pl.BlockSpec((1, 128, 512), lambda r, c: (r, 0, 0)),
            pl.BlockSpec((1, 8, 512), lambda r, c: (r, 0, 0)),
            pl.BlockSpec((4, 512), lambda r, c: (0, 0)),
            pl.BlockSpec((1, 512), lambda r, c: (0, 0)),
            pl.BlockSpec((512, 640), lambda r, c: (0, 0)),
        ],
        [
            pl.BlockSpec((1, 128, 512), lambda r, c: (r, 0, 0)),
            pl.BlockSpec((1, 128, 640), lambda r, c: (r ^ c[0], 0, 0)),
        ],
        [
            jax.ShapeDtypeStruct((2, 128, 512), BF16),
            jax.ShapeDtypeStruct((2, 128, 640), BF16),
        ],
        (pltpu.VMEM((136, 512), F32),),
    )(core, near, far, history, conv_w, conv_b, weight)


def scan_gate(
    core, lengths, low_own, low_other, z_near, z_far, conv, dt_proj, dt_bias, decay, skip, state
):
    def body(
        core_ref,
        len_ref,
        own_ref,
        other_ref,
        zn_ref,
        zf_ref,
        conv_ref,
        dtp_ref,
        dtb_ref,
        decay_ref,
        skip_ref,
        state_ref,
        gated_ref,
        final_ref,
        step_s,
        drive_s,
        trail_s,
        dec_s,
    ):
        dec_s[...] = decay_ref[...] * (-LOG2E)
        lane = lax.broadcasted_iota(jnp.int32, (128, 128), 1)
        row = lax.broadcasted_iota(jnp.int32, (128, 128), 0)
        pick_entry = (row == lane % 16).astype(BF16)
        pick_read = (row == 16 + lane % 16).astype(BF16)
        diagonal = ((lane // 16) == (row % 8)).astype(F32)
        position = lax.broadcasted_iota(jnp.int32, (128, 512), 0)
        reads = []
        for slot, low_ref in enumerate((own_ref, other_ref)):
            request = core_ref[0] ^ slot
            mask = (position < len_ref[request]).astype(F32)
            raw = jnp.dot(low_ref[:, 0:512], dtp_ref[...], preferred_element_type=F32) + dtb_ref[...]
            step = (jnp.maximum(raw, 0.0) + jnp.log(1.0 + jnp.exp(-jnp.abs(raw)))) * mask
            step_s[slot] = step
            drive = (step * conv_ref[request].astype(F32)).astype(BF16)
            tail = low_ref[:, 512:640]
            entry = (jnp.dot(tail, pick_entry, preferred_element_type=F32) * diagonal).astype(BF16)
            reads.append(
                (jnp.dot(tail, pick_read, preferred_element_type=F32) * diagonal).astype(BF16)
            )
            for piece in range(8):
                for half in range(2):
                    at = piece * 16 + half * 8
                    keep = (
                        lax.broadcasted_iota(jnp.int32, (16, 128), 0) // 8 == half
                    ).astype(BF16)
                    drive_s[slot, at * 16 : at * 16 + 128] = lax.dot_general(
                        entry[piece * 16 : piece * 16 + 16] * keep,
                        drive[piece * 16 : piece * 16 + 16],
                        (((0,), (0,)), ((), ())),
                        preferred_element_type=F32,
                    )

        def advance(block, held):
            held = list(held)
            base = pl.multiple_of(block * 8, 8)
            for slot in range(2):
                steps = step_s[slot, pl.ds(base, 8)]
                now = held[slot]
                for offset in range(8):
                    rows = pl.ds(pl.multiple_of(block * 128 + offset * 16, 16), 16)
                    now = jnp.exp2(steps[offset : offset + 1] * dec_s[...]) * now + drive_s[slot, rows]
                    trail_s[slot, rows] = now.astype(BF16)
                held[slot] = now
            return tuple(held)

        first = tuple(state_ref[core_ref[0] ^ slot] for slot in range(2))
        last = lax.fori_loop(0, 16, advance, first)
        for slot in range(2):
            request = core_ref[0] ^ slot
            final_ref[request] = last[slot]
            outs = []
            for piece in range(16):
                outs.append(
                    jnp.dot(
                        reads[slot][piece * 8 : piece * 8 + 8],
                        trail_s[slot, piece * 128 : piece * 128 + 128],
                        preferred_element_type=F32,
                    )
                )
            mask = (position < len_ref[request]).astype(F32)
            mixed = jnp.concatenate(outs, axis=0) + skip_ref[...] * conv_ref[request].astype(F32)
            z_gate = (zn_ref[request] + zf_ref[request].astype(F32)).astype(BF16).astype(F32)
            gated_ref[request] = (mixed * silu(z_gate) * mask).astype(BF16)

    def whole(*shape):
        return pl.BlockSpec(shape, lambda i, c, n: (0,) * len(shape))

    return call(
        body,
        (core, lengths),
        (1,),
        [
            whole(128, 640),
            whole(128, 640),
            whole(2, 128, 512),
            whole(2, 128, 512),
            whole(2, 128, 512),
            whole(512, 512),
            whole(1, 512),
            whole(16, 512),
            whole(1, 512),
            whole(2, 16, 512),
        ],
        [whole(2, 128, 512), whole(2, 16, 512)],
        [
            jax.ShapeDtypeStruct((2, 128, 512), BF16),
            jax.ShapeDtypeStruct((2, 16, 512), F32),
        ],
        (
            pltpu.VMEM((2, 128, 512), F32),
            pltpu.VMEM((2, 2048, 512), F32),
            pltpu.VMEM((2, 2048, 512), BF16),
            pltpu.VMEM((16, 512), F32),
        ),
    )(
        core,
        lengths,
        low_own,
        low_other,
        z_near,
        z_far,
        conv,
        dt_proj,
        dt_bias,
        decay,
        skip,
        state,
    )


def mixer_product(place, gated, blocks):
    def body(place_ref, rows_ref, *refs):
        own, below, above, pair, first, second, third, low, mid, high = refs[:10]
        own_ref, other_ref = refs[10:]

        def times(begin, end, ref, at):
            return jnp.dot(
                rows_ref[:, begin:end], ref[at : at + end - begin], preferred_element_type=F32
            )

        sums = (
            lambda: times(0, 512, own, 0),
            lambda: times(0, 512, below, 0),
            lambda: times(0, 512, above, 0),
            lambda: times(0, 256, first, 0) + times(256, 512, second, 0),
            lambda: times(0, 512, pair, 0),
            lambda: times(0, 256, first, 256) + times(256, 512, third, 256),
            lambda: times(0, 256, third, 0) + times(256, 512, second, 256),
            lambda: times(0, 128, low, 0) + times(128, 256, mid, 0) + times(256, 512, high, 0),
        )
        for index, make in enumerate(sums):
            value = make().astype(BF16)
            part = ((place_ref[1] + RING[index % 4]) % 4) * 2 + (place_ref[2] ^ (index // 4))

            @pl.when(part // 4 == place_ref[0])
            def _():
                own_ref[part % 4, 0] = value[:, 0:256]
                own_ref[part % 4, 1] = value[:, 256:512]

            @pl.when(part // 4 != place_ref[0])
            def _():
                other_ref[part % 4, 0] = value[:, 0:256]
                other_ref[part % 4, 1] = value[:, 256:512]

    def whole(*shape):
        return pl.BlockSpec(shape, lambda i, c: (0,) * len(shape))

    return call(
        body,
        (place,),
        (1,),
        [whole(256, 512)] + [whole(*block.shape) for block in blocks],
        [whole(4, 2, 256, 256)] * 2,
        [jax.ShapeDtypeStruct((4, 2, 256, 256), BF16)] * 2,
    )(place, gated, *blocks)


def half_product(target, rows, weight, weight_spec, received=None):
    row_count, depth = rows.shape

    def body(target_ref, rows_ref, w_ref, *refs):
        out_ref = refs[-1]
        product = jnp.dot(
            rows_ref[...], w_ref[...].reshape(depth, 512), preferred_element_type=F32
        )
        for side in range(2):
            value = product[:, side * 256 : side * 256 + 256]
            if received is not None:
                value = value + refs[0][side].astype(F32)
            out_ref[side] = value.astype(BF16)

    blocks = pl.BlockSpec((2, row_count, 256), lambda i, t: (i, 0, 0))
    operands = (target, rows, weight) + (() if received is None else (received,))
    return call(
        body,
        (target,),
        (4,),
        [pl.BlockSpec((row_count, depth), lambda i, t: (0, 0)), weight_spec]
        + ([] if received is None else [blocks]),
        blocks,
        jax.ShapeDtypeStruct((8, row_count, 256), BF16),
    )(*operands)


def tables_of(routes_t):
    expert = lax.broadcasted_iota(jnp.int32, (8, 256), 0)
    picks = [(expert == routes_t[k : k + 1]) for k in range(2)]
    counts = (picks[0] | picks[1]).astype(BF16)
    earlier = (
        lax.broadcasted_iota(jnp.int32, (256, 256), 0)
        < lax.broadcasted_iota(jnp.int32, (256, 256), 1)
    ).astype(BF16)
    before = jnp.dot(counts, earlier, preferred_element_type=F32)
    place = before + 96.0 * expert.astype(F32)
    slot_row = lax.broadcasted_iota(jnp.int32, (768, 256), 0)
    hit = None
    for pick in picks:
        slot = jnp.sum(jnp.where(pick, place, 0.0), axis=0, keepdims=True).astype(jnp.int32)
        mine = slot_row == slot
        hit = mine if hit is None else hit | mine
    return hit.astype(BF16)


def hidden_dispatch(block, parts, x_rows, routes_t):
    def body(block_ref, parts_ref, x_ref, routes_ref, hidden_ref, out_ref):
        mixer = jnp.sum(parts_ref[...].astype(F32), axis=0)
        hidden = (x_ref[...].astype(F32) + mixer).astype(BF16)
        hidden_ref[...] = hidden
        out_ref[...] = jnp.dot(
            tables_of(routes_ref[...]), hidden, preferred_element_type=F32
        ).astype(BF16)

    return call(
        body,
        (block,),
        (1,),
        [
            pl.BlockSpec((8, 256, 256), lambda i, b: (0, 0, 0)),
            pl.BlockSpec((256, 256), lambda i, b: (0, b[0])),
            pl.BlockSpec((2, 256), lambda i, b: (0, 0)),
        ],
        [
            pl.BlockSpec((256, 256), lambda i, b: (0, 0)),
            pl.BlockSpec((768, 256), lambda i, b: (0, 0)),
        ],
        [
            jax.ShapeDtypeStruct((256, 256), BF16),
            jax.ShapeDtypeStruct((768, 256), BF16),
        ],
    )(block, parts, x_rows, routes_t)


def gate_up(core, own, other, gain, router_row, w_gate, w_up):
    def body(core_ref, own_ref, other_ref, gain_ref, router_ref, wg_ref, wu_ref, out_ref, g_s, u_s, sq_s, lo_s):
        step = pl.program_id(0)

        def work(rows_ref):
            scaled, squares, logits = [], None, None
            for piece in range(4):
                at = slice(piece * 256, piece * 256 + 256)
                value = rows_ref[piece].astype(F32)
                square = value * value
                square = square[:, 0:128] + square[:, 128:256]
                squares = square if squares is None else squares + square
                times = (value * gain_ref[:, at]).astype(BF16)
                scaled.append(times)
                logit = times.astype(F32) * router_ref[:, at]
                logit = logit[:, 0:128] + logit[:, 128:256]
                logits = logit if logits is None else logits + logit
            units = jnp.concatenate(scaled, axis=1)
            gate = jnp.dot(units, wg_ref[...], preferred_element_type=F32)
            up = jnp.dot(units, wu_ref[...], preferred_element_type=F32)

            @pl.when(step == 0)
            def _():
                g_s[...] = gate
                u_s[...] = up
                sq_s[...] = squares
                lo_s[...] = logits

            @pl.when(step > 0)
            def _():
                g_s[...] += gate
                u_s[...] += up
                sq_s[...] += squares
                lo_s[...] += logits

        @pl.when(step < 2)
        def _():
            work(own_ref)

        @pl.when(step >= 2)
        def _():
            work(other_ref)

        @pl.when(step == 3)
        def _():
            scale = lax.rsqrt(jnp.sum(sq_s[...], axis=1, keepdims=True) * (1.0 / 4096.0) + EPS)
            weight = sigmoid(jnp.sum(lo_s[...], axis=1, keepdims=True) * scale)
            out_ref[...] = (silu(g_s[...] * scale) * (u_s[...] * (scale * weight))).astype(BF16)

    def at(i, c):
        return jnp.where(i < 2, c[0] * 2 + i, (1 - c[0]) * 2 + i - 2)

    return call(
        body,
        (core,),
        (4,),
        [
            pl.BlockSpec((4, 768, 256), lambda i, c: (jnp.minimum(i, 1), 0, 0)),
            pl.BlockSpec((4, 768, 256), lambda i, c: (jnp.maximum(i - 2, 0), 0, 0)),
            pl.BlockSpec((1, 1024), lambda i, c: (0, at(i, c))),
            pl.BlockSpec((1, 1024), lambda i, c: (0, at(i, c))),
            pl.BlockSpec((1024, 768), lambda i, c: (at(i, c), 0)),
            pl.BlockSpec((1024, 768), lambda i, c: (at(i, c), 0)),
        ],
        pl.BlockSpec((768, 768), lambda i, c: (0, 0)),
        jax.ShapeDtypeStruct((768, 768), BF16),
        (
            pltpu.VMEM((768, 768), F32),
            pltpu.VMEM((768, 768), F32),
            pltpu.VMEM((768, 128), F32),
            pltpu.VMEM((768, 128), F32),
        ),
    )(core, own, other, gain, router_row, w_gate, w_up)


def sum_parts(parts):
    def body(parts_ref, out_ref):
        out_ref[...] = jnp.sum(parts_ref[...].astype(F32), axis=0).astype(BF16)

    return call(
        body,
        (),
        (4,),
        [pl.BlockSpec((8, 192, 256), lambda i: (0, i, 0))],
        pl.BlockSpec((192, 256), lambda i: (i, 0)),
        jax.ShapeDtypeStruct((768, 256), BF16),
    )(parts)


def combine(hidden, back, routes_t):
    def body(hidden_ref, back_ref, routes_ref, out_ref):
        mixed = lax.dot_general(
            tables_of(routes_ref[...]),
            back_ref[...],
            (((0,), (0,)), ((), ())),
            preferred_element_type=F32,
        )
        out_ref[...] = (hidden_ref[...].astype(F32) + mixed).astype(BF16)

    return call(
        body,
        (),
        (1,),
        [
            pl.BlockSpec((256, 256), lambda i: (0, 0)),
            pl.BlockSpec((768, 256), lambda i: (0, 0)),
            pl.BlockSpec((2, 256), lambda i: (0, 0)),
        ],
        pl.BlockSpec((256, 256), lambda i: (0, 0)),
        jax.ShapeDtypeStruct((256, 256), BF16),
    )(hidden, back, routes_t)


def assemble(core, own, other):
    def body(core_ref, own_ref, other_ref, out_ref):
        for side, ref in enumerate((own_ref, other_ref)):

            @pl.when(pl.program_id(0) == side)
            def _():
                for piece in range(4):
                    out_ref[:, piece * 256 : piece * 256 + 256] = ref[piece]

    return call(
        body,
        (core,),
        (2, 2),
        [
            pl.BlockSpec((4, 256, 256), lambda s, i, c: (jnp.where(s == 0, i, 1), 0, 0)),
            pl.BlockSpec((4, 256, 256), lambda s, i, c: (jnp.where(s == 0, 0, i), 0, 0)),
        ],
        pl.BlockSpec((256, 1024), lambda s, i, c: (0, (c[0] ^ s) * 2 + i)),
        jax.ShapeDtypeStruct((256, 4096), BF16),
    )(core, own, other)


def per_device(
    x_rows,
    lengths,
    routes,
    conv_state,
    ssm_state,
    norm1_gain,
    in_x,
    in_z,
    conv_w,
    conv_b,
    x_dt,
    x_bc,
    dt_proj,
    dt_bias,
    decay_rate,
    skip,
    out_w,
    norm2_gain,
    router,
    w_gate,
    w_up,
    w_down,
):
    core_at = lax.axis_index("core").astype(jnp.int32)
    core = core_at.reshape(1)
    away = (1 - core_at).reshape(1)
    chip_at = lax.axis_index(CHIPS).astype(jnp.int32)
    block = (core_at * 8 + chip_at).reshape(1)
    expert_at = lax.axis_index(DP).astype(jnp.int32)

    place = jnp.stack(
        [core_at, lax.axis_index("z").astype(jnp.int32), lax.axis_index("ylo").astype(jnp.int32)]
    )
    low_weight = jnp.concatenate([x_dt, x_bc, jnp.zeros((512, 96), BF16)], axis=1)
    history = jnp.pad(conv_state.astype(F32), ((0, 0), (5, 0), (0, 0)))
    routes_t = routes.T
    router_row = lax.dynamic_slice(router, (0, expert_at), (4096, 1)).astype(F32).reshape(1, 4096)

    rows_mine, rows_send = norm_split(place, x_rows, norm1_gain.reshape(1, 4096))
    pair_own = swap_pair(rows_send)
    x_below, x_above = from_below(in_x), from_above(in_x)
    x_halves = (x_below[:256], x_above[256:])
    x_blocks = gather_ring(in_x, x_below, x_above, x_halves)
    pair_other = swap_core(pair_own)
    z_block = after(in_z, pair_other, *x_halves)
    z_below, z_above = from_below(z_block), from_above(z_block)
    x_far = swap_pair(pair_product(place, pair_own, pair_other, x_blocks))
    z_halves = (z_below[:256], z_above[256:])
    z_blocks = gather_ring(z_block, z_below, z_above, z_halves)
    x_near = after(own_product(rows_mine, x_blocks), *z_halves)
    conv, low = conv_project(
        core, x_near, x_far, history, conv_w, conv_b.reshape(1, 512), low_weight
    )
    low_far = swap_core(low[1])
    out_block = after(out_w, low[1])
    out_pair, out_below, out_above = (
        swap_pair(out_block),
        from_below(out_block),
        from_above(out_block),
    )
    low_pair = (low[0].astype(F32) + low_far.astype(F32)).astype(BF16)
    low_parts = exchange(low_pair.reshape(8, 16, 640), CHIPS)
    low_sum = jnp.sum(low_parts.astype(F32), axis=0).astype(BF16)
    z_send = pair_product(place, pair_own, after(pair_other, low_parts), z_blocks)
    out_sends = second_round(
        after(out_below, z_send), after(out_above, z_send), after(out_pair, z_send)
    )
    low_sum = after(low_sum, z_send, *out_sends)
    z_far = swap_pair(z_send)
    z_near = own_product(rows_mine, z_blocks)
    out_seconds = (from_below(out_sends[0]), from_above(out_sends[1]), swap_pair(out_sends[2]))
    low_own = spread(low_sum).reshape(128, 640)
    out_seconds = tuple(after(block, low_own) for block in out_seconds)
    out_blocks = (
        (out_block, out_below, out_above, out_pair) + out_seconds + third_round(*out_seconds)
    )
    low_other = swap_core(low_own)
    gated, final = scan_gate(
        core,
        lengths,
        low_own,
        low_other,
        z_near,
        z_far,
        conv,
        dt_proj,
        dt_bias.reshape(1, 512),
        decay_rate,
        skip.reshape(1, 512),
        ssm_state,
    )
    gated = gated.reshape(256, 512)
    mixer_own, mixer_other = mixer_product(place, gated, out_blocks)
    mixer_pair = (mixer_own.astype(F32) + swap_core(mixer_other).astype(F32)).astype(BF16)
    mixer_parts = exchange(mixer_pair.reshape(8, 256, 256), CHIPS)
    hidden, outgoing = hidden_dispatch(block, mixer_parts, x_rows, routes_t)
    arriving = exchange(outgoing.reshape(8, 96, 256), DP).reshape(768, 256)
    rows_own = spread(arriving)
    rows_other = swap_core(rows_own)
    active = gate_up(
        core, rows_own, rows_other, norm2_gain.reshape(1, 4096), router_row, w_gate[0], w_up[0]
    )
    down_spec = pl.BlockSpec((768, 512), lambda i, t: (0, t[0] * 4 + i))
    far_down = swap_core(half_product(away, active, w_down[0], down_spec))
    down_parts = exchange(half_product(core, active, w_down[0], down_spec, far_down), CHIPS)
    back = exchange(sum_parts(down_parts).reshape(8, 96, 256), DP).reshape(768, 256)
    out_own = spread(combine(hidden, back, routes_t))
    out_other = swap_core(out_own)
    return (assemble(core, out_own, out_other), final)


def solution(mesh):
    wide = Mesh(mesh.devices.reshape(4, 2, 2, 4, 2), ("z", "ylo", "yhi", "x", "core"))
    return jax.shard_map(
        per_device,
        mesh=wide,
        in_specs=(
            P(DP, None),
            P(DP),
            P(DP, None),
            P(DP, None, TENSOR),
            P(DP, None, TENSOR),
            P(),
            P(DP, TENSOR),
            P(DP, TENSOR),
            P(None, TENSOR),
            P(TENSOR),
            P(TENSOR, None),
            P(TENSOR, None),
            P(None, TENSOR),
            P(TENSOR),
            P(None, TENSOR),
            P(TENSOR),
            P(TENSOR, DP),
            P(),
            P(),
            P(DP, None, TENSOR),
            P(DP, None, TENSOR),
            P(DP, TENSOR, None),
        ),
        out_specs=(P(DP, None), P(DP, None, TENSOR)),
        check_vma=False,
    )
```

```python
import jax
import jax.numpy as jnp
from jax import lax
from jax.sharding import Mesh
from jax.sharding import PartitionSpec as P
from jax.experimental import pallas as pl
from jax.experimental.pallas import tpu as pltpu

F32 = jnp.float32
BF16 = jnp.bfloat16
DP = ("z", "ylo")
TENSOR = ("yhi", "x", "core")
CHIPS = ("yhi", "x")
EPS = 1e-05
LOG2E = 1.4426950408889634


def params(megabytes=48):
    return pltpu.CompilerParams(vmem_limit_bytes=megabytes << 20)


def call(body, scalars, grid, in_specs, out_specs, out_shape, scratch=(), cost=None):
    spec = pltpu.PrefetchScalarGridSpec(
        num_scalar_prefetch=len(scalars),
        grid=grid,
        in_specs=in_specs,
        out_specs=out_specs,
        scratch_shapes=scratch,
    )
    return pl.pallas_call(
        body, grid_spec=spec, out_shape=out_shape, compiler_params=params(), cost_estimate=cost
    )


def exchange(value, axes):
    return lax.all_to_all(value, axes, split_axis=0, concat_axis=0, tiled=True)


def spread(value):
    return exchange(jnp.broadcast_to(value[None], (8,) + value.shape), CHIPS)


def from_left(value):
    return lax.ppermute(value, "x", [(i, (i + 1) % 4) for i in range(4)])


def from_right(value):
    return lax.ppermute(value, "x", [(i, (i - 1) % 4) for i in range(4)])


def swap_far(value):
    return lax.ppermute(value, "yhi", [(0, 1), (1, 0)])


def add_half(value, received):
    return (value.astype(F32) + received.astype(F32)).astype(BF16)


def swap_core(value):
    return lax.ppermute(value, "core", [(0, 1), (1, 0)])


def sigmoid(value):
    return 1.0 / (1.0 + jnp.exp(-value))


def silu(value):
    return value * sigmoid(value)


RING = (0, 3, 1, 2)


def from_below(value):
    return lax.ppermute(value, "z", [(i, (i + 1) % 4) for i in range(4)])


def from_above(value):
    return lax.ppermute(value, "z", [(i, (i - 1) % 4) for i in range(4)])


def after(value, *earlier):
    return lax.optimization_barrier((value,) + earlier)[0]


def swap_pair(value):
    return lax.ppermute(value, "ylo", [(0, 1), (1, 0)])


def gather_ring(block, below, above, halves):
    return block, below, above, from_below(halves[0]), from_above(halves[1])


def second_round(below, above, pair):
    return (
        jnp.concatenate([below[:256], pair[:256]]),
        jnp.concatenate([above[256:], pair[256:]]),
        jnp.concatenate([above[:256], below[256:]]),
    )


def third_round(first, second, third):
    return (
        from_below(first[256:384]),
        from_above(third[128:256]),
        swap_pair(second[:256]),
    )


def norm_split(place, x_rows, gain):
    def body(place_ref, x_ref, gain_ref, own_ref, send_ref):
        request = pl.ds(pl.multiple_of(place_ref[0] * 128, 128), 128)
        for rows, out_ref, member in (
            (slice(0, 256), own_ref, place_ref[2]),
            (request, send_ref, 1 - place_ref[2]),
        ):
            values = x_ref[rows, :].astype(F32)
            scale = lax.rsqrt(jnp.mean(values * values, axis=-1, keepdims=True) + EPS)
            for piece, shift in enumerate(RING):
                at = ((place_ref[1] + shift) % 4) * 2 + member
                columns = pl.ds(pl.multiple_of(at * 512, 512), 512)
                part = x_ref[rows, columns].astype(F32)
                out_ref[piece] = (part * scale * gain_ref[:, columns]).astype(BF16)

    return call(
        body,
        (place,),
        (1,),
        [
            pl.BlockSpec((256, 4096), lambda i, c: (0, 0)),
            pl.BlockSpec((1, 4096), lambda i, c: (0, 0)),
        ],
        [
            pl.BlockSpec((4, 256, 512), lambda i, c: (0, 0, 0)),
            pl.BlockSpec((4, 128, 512), lambda i, c: (0, 0, 0)),
        ],
        [
            jax.ShapeDtypeStruct((4, 256, 512), BF16),
            jax.ShapeDtypeStruct((4, 128, 512), BF16),
        ],
    )(place, x_rows, gain)


def ring_product(rows_ref, blocks):
    total = None
    for piece in range(3):
        term = jnp.dot(rows_ref[piece], blocks[piece][...], preferred_element_type=F32)
        total = term if total is None else total + term
    total = total + jnp.dot(rows_ref[3, :, 0:256], blocks[3][...], preferred_element_type=F32)
    return total + jnp.dot(rows_ref[3, :, 256:512], blocks[4][...], preferred_element_type=F32)


RING_SPECS = [pl.BlockSpec((512, 512), lambda *_: (0, 0))] * 3 + [
    pl.BlockSpec((256, 512), lambda *_: (0, 0))
] * 2


def pair_product(place, own, other, blocks):
    def body(place_ref, own_ref, other_ref, *refs):
        for slot, rows_ref in enumerate((own_ref, other_ref)):
            refs[5][place_ref[0] ^ slot] = ring_product(rows_ref, refs[:5]).astype(BF16)

    return call(
        body,
        (place,),
        (1,),
        [pl.BlockSpec((4, 128, 512), lambda i, c: (0, 0, 0))] * 2 + RING_SPECS,
        pl.BlockSpec((2, 128, 512), lambda i, c: (0, 0, 0)),
        jax.ShapeDtypeStruct((2, 128, 512), BF16),
    )(place, own, other, *blocks)


def own_product(rows, blocks):
    def body(rows_ref, *refs):
        refs[5][...] = ring_product(rows_ref, refs[:5]).reshape(2, 128, 512)

    return call(
        body,
        (),
        (1,),
        [pl.BlockSpec((4, 256, 512), lambda i: (0, 0, 0))] + RING_SPECS,
        pl.BlockSpec((2, 128, 512), lambda i: (0, 0, 0)),
        jax.ShapeDtypeStruct((2, 128, 512), F32),
    )(rows, *blocks)


def conv_project(core, near, far, history, conv_w, conv_b, weight):
    def body(core_ref, near_ref, far_ref, hist_ref, cw_ref, cb_ref, w_ref, conv_ref, low_ref, line):
        x_inner = (near_ref[0] + far_ref[0].astype(F32)).astype(BF16).astype(F32)
        line[0:8] = hist_ref[0]
        line[8:136] = x_inner
        total = cb_ref[...] + cw_ref[3:4] * x_inner
        for tap in range(3):
            total = total + cw_ref[tap : tap + 1] * line[5 + tap : 133 + tap]
        conv = silu(total).astype(BF16)
        conv_ref[0] = conv
        low_ref[0] = jnp.dot(conv, w_ref[...], preferred_element_type=F32).astype(BF16)

    return call(
        body,
        (core,),
        (2,),
        [
            pl.BlockSpec((1, 128, 512), lambda r, c: (r, 0, 0)),
            pl.BlockSpec((1, 128, 512), lambda r, c: (r, 0, 0)),
            pl.BlockSpec((1, 8, 512), lambda r, c: (r, 0, 0)),
            pl.BlockSpec((4, 512), lambda r, c: (0, 0)),
            pl.BlockSpec((1, 512), lambda r, c: (0, 0)),
            pl.BlockSpec((512, 640), lambda r, c: (0, 0)),
        ],
        [
            pl.BlockSpec((1, 128, 512), lambda r, c: (r, 0, 0)),
            pl.BlockSpec((1, 128, 640), lambda r, c: (r ^ c[0], 0, 0)),
        ],
        [
            jax.ShapeDtypeStruct((2, 128, 512), BF16),
            jax.ShapeDtypeStruct((2, 128, 640), BF16),
        ],
        (pltpu.VMEM((136, 512), F32),),
    )(core, near, far, history, conv_w, conv_b, weight)


def scan_gate(
    core, lengths, low_own, low_other, z_near, z_far, conv, dt_proj, dt_bias, decay, skip, state
):
    def body(
        core_ref,
        len_ref,
        own_ref,
        other_ref,
        zn_ref,
        zf_ref,
        conv_ref,
        dtp_ref,
        dtb_ref,
        decay_ref,
        skip_ref,
        state_ref,
        gated_ref,
        final_ref,
        step_s,
        drive_s,
        trail_s,
        dec_s,
    ):
        dec_s[...] = decay_ref[...] * (-LOG2E)
        lane = lax.broadcasted_iota(jnp.int32, (128, 128), 1)
        row = lax.broadcasted_iota(jnp.int32, (128, 128), 0)
        pick_entry = (row == lane % 16).astype(BF16)
        pick_read = (row == 16 + lane % 16).astype(BF16)
        diagonal = ((lane // 16) == (row % 8)).astype(F32)
        position = lax.broadcasted_iota(jnp.int32, (128, 512), 0)
        reads = []
        for slot, low_ref in enumerate((own_ref, other_ref)):
            request = core_ref[0] ^ slot
            mask = (position < len_ref[request]).astype(F32)
            raw = jnp.dot(low_ref[:, 0:512], dtp_ref[...], preferred_element_type=F32) + dtb_ref[...]
            step = (jnp.maximum(raw, 0.0) + jnp.log(1.0 + jnp.exp(-jnp.abs(raw)))) * mask
            step_s[slot] = step
            drive = (step * conv_ref[request].astype(F32)).astype(BF16)
            tail = low_ref[:, 512:640]
            entry = (jnp.dot(tail, pick_entry, preferred_element_type=F32) * diagonal).astype(BF16)
            reads.append(
                (jnp.dot(tail, pick_read, preferred_element_type=F32) * diagonal).astype(BF16)
            )
            for piece in range(8):
                for half in range(2):
                    at = piece * 16 + half * 8
                    keep = (
                        lax.broadcasted_iota(jnp.int32, (16, 128), 0) // 8 == half
                    ).astype(BF16)
                    drive_s[slot, at * 16 : at * 16 + 128] = lax.dot_general(
                        entry[piece * 16 : piece * 16 + 16] * keep,
                        drive[piece * 16 : piece * 16 + 16],
                        (((0,), (0,)), ((), ())),
                        preferred_element_type=F32,
                    )

        def advance(block, held):
            held = list(held)
            base = pl.multiple_of(block * 8, 8)
            for slot in range(2):
                steps = step_s[slot, pl.ds(base, 8)]
                now = held[slot]
                for offset in range(8):
                    rows = pl.ds(pl.multiple_of(block * 128 + offset * 16, 16), 16)
                    now = jnp.exp2(steps[offset : offset + 1] * dec_s[...]) * now + drive_s[slot, rows]
                    trail_s[slot, rows] = now.astype(BF16)
                held[slot] = now
            return tuple(held)

        first = tuple(state_ref[core_ref[0] ^ slot] for slot in range(2))
        last = lax.fori_loop(0, 16, advance, first)
        for slot in range(2):
            request = core_ref[0] ^ slot
            final_ref[request] = last[slot]
            outs = []
            for piece in range(16):
                outs.append(
                    jnp.dot(
                        reads[slot][piece * 8 : piece * 8 + 8],
                        trail_s[slot, piece * 128 : piece * 128 + 128],
                        preferred_element_type=F32,
                    )
                )
            mask = (position < len_ref[request]).astype(F32)
            mixed = jnp.concatenate(outs, axis=0) + skip_ref[...] * conv_ref[request].astype(F32)
            z_gate = (zn_ref[request] + zf_ref[request].astype(F32)).astype(BF16).astype(F32)
            gated_ref[request] = (mixed * silu(z_gate) * mask).astype(BF16)

    def whole(*shape):
        return pl.BlockSpec(shape, lambda i, c, n: (0,) * len(shape))

    return call(
        body,
        (core, lengths),
        (1,),
        [
            whole(128, 640),
            whole(128, 640),
            whole(2, 128, 512),
            whole(2, 128, 512),
            whole(2, 128, 512),
            whole(512, 512),
            whole(1, 512),
            whole(16, 512),
            whole(1, 512),
            whole(2, 16, 512),
        ],
        [whole(2, 128, 512), whole(2, 16, 512)],
        [
            jax.ShapeDtypeStruct((2, 128, 512), BF16),
            jax.ShapeDtypeStruct((2, 16, 512), F32),
        ],
        (
            pltpu.VMEM((2, 128, 512), F32),
            pltpu.VMEM((2, 2048, 512), F32),
            pltpu.VMEM((2, 2048, 512), BF16),
            pltpu.VMEM((16, 512), F32),
        ),
    )(
        core,
        lengths,
        low_own,
        low_other,
        z_near,
        z_far,
        conv,
        dt_proj,
        dt_bias,
        decay,
        skip,
        state,
    )


def mixer_product(place, gated, blocks):
    def body(place_ref, rows_ref, *refs):
        own, below, above, pair, first, second, third, low, mid, high = refs[:10]
        own_ref, other_ref = refs[10:]

        def times(begin, end, ref, at):
            return jnp.dot(
                rows_ref[:, begin:end], ref[at : at + end - begin], preferred_element_type=F32
            )

        sums = (
            lambda: times(0, 512, own, 0),
            lambda: times(0, 512, below, 0),
            lambda: times(0, 512, above, 0),
            lambda: times(0, 256, first, 0) + times(256, 512, second, 0),
            lambda: times(0, 512, pair, 0),
            lambda: times(0, 256, first, 256) + times(256, 512, third, 256),
            lambda: times(0, 256, third, 0) + times(256, 512, second, 256),
            lambda: times(0, 128, low, 0) + times(128, 256, mid, 0) + times(256, 512, high, 0),
        )
        for index, make in enumerate(sums):
            value = make().astype(BF16)
            part = ((place_ref[1] + RING[index % 4]) % 4) * 2 + (place_ref[2] ^ (index // 4))

            @pl.when(part // 4 == place_ref[0])
            def _():
                own_ref[part % 4, 0] = value[:, 0:256]
                own_ref[part % 4, 1] = value[:, 256:512]

            @pl.when(part // 4 != place_ref[0])
            def _():
                other_ref[part % 4, 0] = value[:, 0:256]
                other_ref[part % 4, 1] = value[:, 256:512]

    def whole(*shape):
        return pl.BlockSpec(shape, lambda i, c: (0,) * len(shape))

    return call(
        body,
        (place,),
        (1,),
        [whole(256, 512)] + [whole(*block.shape) for block in blocks],
        [whole(4, 2, 256, 256)] * 2,
        [jax.ShapeDtypeStruct((4, 2, 256, 256), BF16)] * 2,
    )(place, gated, *blocks)


def tables_of(routes_t):
    expert = lax.broadcasted_iota(jnp.int32, (8, 256), 0)
    picks = [(expert == routes_t[k : k + 1]) for k in range(2)]
    counts = (picks[0] | picks[1]).astype(BF16)
    earlier = (
        lax.broadcasted_iota(jnp.int32, (256, 256), 0)
        < lax.broadcasted_iota(jnp.int32, (256, 256), 1)
    ).astype(BF16)
    before = jnp.dot(counts, earlier, preferred_element_type=F32)
    place = before + 96.0 * expert.astype(F32)
    slot_row = lax.broadcasted_iota(jnp.int32, (768, 256), 0)
    hit = None
    for pick in picks:
        slot = jnp.sum(jnp.where(pick, place, 0.0), axis=0, keepdims=True).astype(jnp.int32)
        mine = slot_row == slot
        hit = mine if hit is None else hit | mine
    return hit.astype(BF16)


def hidden_dispatch(block, parts, x_rows, gain, routes_t):
    def body(block_ref, parts_ref, x_ref, gain_ref, routes_ref, hidden_ref, out_ref):
        mixer = jnp.sum(parts_ref[...].astype(F32), axis=0)
        hidden = (x_ref[...].astype(F32) + mixer).astype(BF16)
        hidden_ref[...] = hidden
        scaled = (hidden.astype(F32) * gain_ref[...]).astype(BF16)
        out_ref[...] = jnp.dot(
            tables_of(routes_ref[...]), scaled, preferred_element_type=F32
        ).astype(BF16)

    return call(
        body,
        (block,),
        (1,),
        [
            pl.BlockSpec((8, 256, 256), lambda i, b: (0, 0, 0)),
            pl.BlockSpec((256, 256), lambda i, b: (0, b[0])),
            pl.BlockSpec((1, 256), lambda i, b: (0, b[0])),
            pl.BlockSpec((2, 256), lambda i, b: (0, 0)),
        ],
        [
            pl.BlockSpec((256, 256), lambda i, b: (0, 0)),
            pl.BlockSpec((768, 256), lambda i, b: (0, 0)),
        ],
        [
            jax.ShapeDtypeStruct((256, 256), BF16),
            jax.ShapeDtypeStruct((768, 256), BF16),
        ],
    )(block, parts, x_rows, gain, routes_t)


def block_places(core_at, x_at, far_at):
    near = [far_at * 4 + (x_at + step) % 4 for step in (0, 3, 1)]
    cross = [(1 - far_at) * 4 + (x_at + step) % 4 for step in (0, 3, 1, 2)]
    two = far_at * 4 + (x_at + 2) % 4
    order = near + cross[0:1] + [two] + cross[1:4]
    return jnp.stack([core_at * 8 + at for at in order] + [(1 - core_at) * 8 + at for at in order])


def gate_up(places, first, own, other, inverse, router_row, w_gate, w_up, held=None):
    def body(places_ref, *refs):
        step = pl.program_id(0)
        own_ref, other_ref = refs[0:4], refs[4:8]
        inverse_refs, router_refs = refs[8:12], refs[12:16]
        gate_refs, up_refs = refs[16:20], refs[20:24]
        held_refs, outs = refs[24:-4], refs[-4:]
        g_s, u_s, sq_s, lo_s = outs

        def work(rows_refs):
            units = jnp.concatenate([ref[...] for ref in rows_refs], axis=1)
            squares, logits = None, None
            for piece in range(4):
                value = rows_refs[piece][...].astype(F32)
                square = value * inverse_refs[piece][...]
                square = square * square
                square = square[:, 0:128] + square[:, 128:256]
                squares = square if squares is None else squares + square
                logit = value * router_refs[piece][...]
                logit = logit[:, 0:128] + logit[:, 128:256]
                logits = logit if logits is None else logits + logit
            gate = jnp.dot(
                units,
                jnp.concatenate([ref[...] for ref in gate_refs], axis=0),
                preferred_element_type=F32,
            )
            up = jnp.dot(
                units,
                jnp.concatenate([ref[...] for ref in up_refs], axis=0),
                preferred_element_type=F32,
            )
            return gate, up, squares, logits

        @pl.when(step == 0)
        def _():
            found = work(own_ref)
            for index, value in enumerate(found):
                if held is None:
                    outs[index][...] = value
                else:
                    outs[index][...] = held_refs[index][...] + value

        @pl.when(step == 1)
        def _():
            found = work(other_ref)
            for index, value in enumerate(found):
                outs[index][...] += value

    def at(piece):
        return lambda i, p: p[first + piece + 8 * i]

    def row_spec(piece):
        return pl.BlockSpec((1, 256), lambda i, p, f=at(piece): (0, f(i, p)))

    def weight_spec(piece):
        return pl.BlockSpec((256, 768), lambda i, p, f=at(piece): (f(i, p), 0))

    def whole(*shape):
        return pl.BlockSpec(shape, lambda i, p: (0, 0))

    kept = [whole(768, 768)] * 2 + [whole(768, 128)] * 2
    shapes = [jax.ShapeDtypeStruct((768, 768), F32)] * 2 + [
        jax.ShapeDtypeStruct((768, 128), F32)
    ] * 2
    return call(
        body,
        (places,),
        (2,),
        [whole(768, 256)] * 8
        + [row_spec(piece) for piece in range(4)] * 2
        + [weight_spec(piece) for piece in range(4)] * 2
        + ([] if held is None else kept),
        kept,
        shapes,
        cost=pl.CostEstimate(flops=2 * 768 * 2048 * 1536, bytes_accessed=20 << 20, transcendentals=0),
    )(
        places,
        *own,
        *other,
        *([inverse] * 4),
        *([router_row] * 4),
        *([w_gate] * 4),
        *([w_up] * 4),
        *(() if held is None else held),
    )


def activate(gate, up, squares, logits):
    def body(g_ref, u_ref, sq_ref, lo_ref, out_ref):
        scale = lax.rsqrt(jnp.sum(sq_ref[...], axis=1, keepdims=True) * (1.0 / 4096.0) + EPS)
        weight = sigmoid(jnp.sum(lo_ref[...], axis=1, keepdims=True) * scale)
        out_ref[...] = (silu(g_ref[...] * scale) * (u_ref[...] * (scale * weight))).astype(BF16)

    return call(
        body,
        (),
        (4,),
        [pl.BlockSpec((192, 768), lambda i: (i, 0))] * 2
        + [pl.BlockSpec((192, 128), lambda i: (i, 0))] * 2,
        pl.BlockSpec((192, 768), lambda i: (i, 0)),
        jax.ShapeDtypeStruct((768, 768), BF16),
    )(gate, up, squares, logits)


def down_product(places, first, active, w_down, received=None):
    def body(places_ref, rows_ref, *refs):
        out_ref = refs[-1]
        for side in range(2):
            value = jnp.dot(rows_ref[...], refs[side][...], preferred_element_type=F32)
            if received is not None:
                value = value + refs[2][side].astype(F32)
            out_ref[side] = value.astype(BF16)

    def weight_spec(side):
        return pl.BlockSpec((768, 256), lambda i, p: (0, p[first + 2 * i + side]))

    blocks = pl.BlockSpec((2, 768, 256), lambda i, p: (i, 0, 0))
    return call(
        body,
        (places,),
        (2,),
        [pl.BlockSpec((768, 768), lambda i, p: (0, 0)), weight_spec(0), weight_spec(1)]
        + ([] if received is None else [blocks]),
        blocks,
        jax.ShapeDtypeStruct((4, 768, 256), BF16),
        cost=pl.CostEstimate(flops=2 * 768 * 768 * 1024, bytes_accessed=5 << 20, transcendentals=0),
    )(places, active, w_down, w_down, *(() if received is None else (received,)))


def whole_call(body, shapes, operands):
    def spec(shape):
        return pl.BlockSpec(shape, lambda i: (0,) * len(shape))

    outs = [jax.ShapeDtypeStruct(shape, BF16) for shape in shapes]
    return call(
        body,
        (),
        (1,),
        [spec(value.shape) for value in operands],
        [spec(shape) for shape in shapes],
        outs,
    )(*operands)


def fold_far(far, corner):
    def body(far_ref, low_ref, mid_ref, high_ref, up_ref, down_ref, cross_ref):
        def add(block, begin, end, ref, at):
            return (
                far_ref[block, begin:end].astype(F32) + ref[at : at + end - begin].astype(F32)
            ).astype(BF16)

        up_ref[0:384] = far_ref[0, 0:384]
        up_ref[384:640] = add(2, 0, 256, low_ref, 0)
        up_ref[640:768] = far_ref[2, 256:384]
        down_ref[0:128] = far_ref[0, 384:512]
        down_ref[128:384] = add(0, 512, 768, high_ref, 0)
        down_ref[384:512] = add(1, 384, 512, mid_ref, 128)
        down_ref[512:768] = far_ref[1, 512:768]
        cross_ref[0:384] = far_ref[2, 384:768]
        cross_ref[384:640] = far_ref[1, 0:256]
        cross_ref[640:768] = add(1, 256, 384, mid_ref, 0)

    return whole_call(body, [(768, 256)] * 3, (far,) + corner)


def fold_near(near, up, down, cross):
    def body(near_ref, up_ref, down_ref, cross_ref, left_ref, right_ref, row_ref):
        for out_ref, block, top, bottom in (
            (right_ref, 2, up_ref[0:384], cross_ref[0:384]),
            (left_ref, 1, cross_ref[384:768], down_ref[0:384]),
            (row_ref, 3, up_ref[384:768], down_ref[384:768]),
        ):
            out_ref[0:384] = (near_ref[block, 0:384].astype(F32) + top.astype(F32)).astype(BF16)
            out_ref[384:768] = (near_ref[block, 384:768].astype(F32) + bottom.astype(F32)).astype(
                BF16
            )

    return whole_call(body, [(768, 256)] * 3, (near, up, down, cross))


def fold_own(near, parts):
    def body(near_ref, a_ref, b_ref, c_ref, out_ref):
        total = near_ref[0].astype(F32) + a_ref[...].astype(F32)
        out_ref[...] = (total + b_ref[...].astype(F32) + c_ref[...].astype(F32)).astype(BF16)

    return whole_call(body, [(768, 256)], (near,) + parts)[0]


def combine(hidden, back, routes_t):
    def body(hidden_ref, back_ref, routes_ref, out_ref):
        mixed = lax.dot_general(
            tables_of(routes_ref[...]),
            back_ref[...],
            (((0,), (0,)), ((), ())),
            preferred_element_type=F32,
        )
        out_ref[...] = (hidden_ref[...].astype(F32) + mixed).astype(BF16)

    return call(
        body,
        (),
        (1,),
        [
            pl.BlockSpec((256, 256), lambda i: (0, 0)),
            pl.BlockSpec((768, 256), lambda i: (0, 0)),
            pl.BlockSpec((2, 256), lambda i: (0, 0)),
        ],
        pl.BlockSpec((256, 256), lambda i: (0, 0)),
        jax.ShapeDtypeStruct((256, 256), BF16),
    )(hidden, back, routes_t)


def assemble(core, own, other):
    def body(core_ref, own_ref, other_ref, out_ref):
        for side, ref in enumerate((own_ref, other_ref)):

            @pl.when(pl.program_id(0) == side)
            def _():
                for piece in range(4):
                    out_ref[:, piece * 256 : piece * 256 + 256] = ref[piece]

    return call(
        body,
        (core,),
        (2, 2),
        [
            pl.BlockSpec((4, 256, 256), lambda s, i, c: (jnp.where(s == 0, i, 1), 0, 0)),
            pl.BlockSpec((4, 256, 256), lambda s, i, c: (jnp.where(s == 0, 0, i), 0, 0)),
        ],
        pl.BlockSpec((256, 1024), lambda s, i, c: (0, (c[0] ^ s) * 2 + i)),
        jax.ShapeDtypeStruct((256, 4096), BF16),
    )(core, own, other)


def per_device(
    x_rows,
    lengths,
    routes,
    conv_state,
    ssm_state,
    norm1_gain,
    in_x,
    in_z,
    conv_w,
    conv_b,
    x_dt,
    x_bc,
    dt_proj,
    dt_bias,
    decay_rate,
    skip,
    out_w,
    norm2_gain,
    router,
    w_gate,
    w_up,
    w_down,
):
    core_at = lax.axis_index("core").astype(jnp.int32)
    core = core_at.reshape(1)
    chip_at = lax.axis_index(CHIPS).astype(jnp.int32)
    block = (core_at * 8 + chip_at).reshape(1)
    expert_at = lax.axis_index(DP).astype(jnp.int32)

    place = jnp.stack(
        [core_at, lax.axis_index("z").astype(jnp.int32), lax.axis_index("ylo").astype(jnp.int32)]
    )
    low_weight = jnp.concatenate([x_dt, x_bc, jnp.zeros((512, 96), BF16)], axis=1)
    history = jnp.pad(conv_state.astype(F32), ((0, 0), (5, 0), (0, 0)))
    routes_t = routes.T
    router_row = lax.dynamic_slice(router, (0, expert_at), (4096, 1)).astype(F32).reshape(1, 4096)

    rows_mine, rows_send = norm_split(place, x_rows, norm1_gain.reshape(1, 4096))
    pair_own = swap_pair(rows_send)
    x_below, x_above = from_below(in_x), from_above(in_x)
    x_halves = (x_below[:256], x_above[256:])
    x_blocks = gather_ring(in_x, x_below, x_above, x_halves)
    pair_other = swap_core(after(pair_own, *x_halves))
    z_block = after(in_z, pair_other, *x_halves)
    z_below, z_above = from_below(z_block), from_above(z_block)
    x_far = swap_pair(pair_product(place, pair_own, pair_other, x_blocks))
    z_halves = (z_below[:256], z_above[256:])
    z_blocks = gather_ring(z_block, z_below, z_above, z_halves)
    x_near = after(own_product(rows_mine, x_blocks), *z_halves)
    conv, low = conv_project(
        core, x_near, x_far, history, conv_w, conv_b.reshape(1, 512), low_weight
    )
    low_far = swap_core(low[1])
    out_block = after(out_w, low[1])
    out_pair, out_below, out_above = (
        swap_pair(out_block),
        from_below(out_block),
        from_above(out_block),
    )
    low_pair = add_half(low[0], low_far)
    low_four = add_half(low_pair, lax.ppermute(low_pair, "x", [(i, i ^ 1) for i in range(4)]))
    low_four = after(low_four, *z_blocks[3:5])
    low_line = add_half(low_four, lax.ppermute(low_four, "x", [(i, i ^ 2) for i in range(4)]))
    z_send = pair_product(place, pair_own, after(pair_other, low_four), z_blocks)
    low_line = after(low_line, z_send)
    z_far = swap_pair(z_send)
    low_own = add_half(low_line, swap_far(low_line))
    out_sends = second_round(
        after(out_below, low_line), after(out_above, low_line), after(out_pair, low_line)
    )
    low_own = after(low_own, *out_sends)
    z_near = own_product(rows_mine, z_blocks)
    out_seconds = (from_below(out_sends[0]), from_above(out_sends[1]), swap_pair(out_sends[2]))
    low_other = swap_core(low_own)
    gated, final = scan_gate(
        core,
        lengths,
        low_own,
        low_other,
        z_near,
        z_far,
        conv,
        dt_proj,
        dt_bias.reshape(1, 512),
        decay_rate,
        skip.reshape(1, 512),
        ssm_state,
    )
    out_seconds = tuple(after(block, gated) for block in out_seconds)
    out_blocks = (
        (out_block, out_below, out_above, out_pair) + out_seconds + third_round(*out_seconds)
    )
    gated = gated.reshape(256, 512)
    mixer_own, mixer_other = mixer_product(place, gated, out_blocks)
    mixer_pair = (mixer_own.astype(F32) + swap_core(mixer_other).astype(F32)).astype(BF16)
    mixer_parts = exchange(mixer_pair.reshape(8, 256, 256), CHIPS)
    places = block_places(
        core_at, lax.axis_index("x").astype(jnp.int32), lax.axis_index("yhi").astype(jnp.int32)
    )
    gain = norm2_gain.reshape(1, 4096)
    hidden, outgoing = hidden_dispatch(block, mixer_parts, x_rows, gain, routes_t)
    rows = exchange(outgoing.reshape(8, 96, 256), DP).reshape(768, 256)
    left, right, cross = from_left(rows), from_right(rows), swap_far(rows)
    near = (rows, left, right, cross)
    near_other = tuple(swap_core(value) for value in near)
    top, bottom = slice(0, 384), slice(384, 768)
    up = from_left(jnp.concatenate([left[top], cross[top]]))
    down = from_right(jnp.concatenate([right[bottom], cross[bottom]]))
    over = swap_far(jnp.concatenate([right[top], left[bottom]]))
    inverse = 1.0 / gain
    held = gate_up(places, 0, near, near_other, inverse, router_row, w_gate[0], w_up[0])
    up, down, over = (after(value, held[2]) for value in (up, down, over))
    two = jnp.concatenate([up[top], down[top]])
    cross_left = jnp.concatenate([up[bottom], over[bottom]])
    cross_right = jnp.concatenate([over[top], down[bottom]])
    cross_two = jnp.concatenate(
        [from_left(cross_left[0:256]), from_right(cross_right[256:512]), swap_far(two[512:768])]
    )
    far = (two, cross_left, cross_right, cross_two)
    far_other = tuple(swap_core(value) for value in far)
    held = gate_up(places, 4, far, far_other, inverse, router_row, w_gate[0], w_up[0], held)
    active = activate(*held)
    far_sent = swap_core(down_product(places, 12, active, w_down[0]))
    near_sent = swap_core(down_product(places, 8, active, w_down[0]))
    far_sum = down_product(places, 4, active, w_down[0], far_sent)
    corner = (
        from_left(far_sum[3, 0:256]),
        from_right(far_sum[3, 256:512]),
        swap_far(far_sum[3, 512:768]),
    )
    near_sum = down_product(places, 0, active, w_down[0], near_sent)
    up_send, down_send, cross_send = fold_far(far_sum, corner)
    to_left, to_right, to_row = fold_near(
        near_sum, from_left(up_send), from_right(down_send), swap_far(cross_send)
    )
    total = fold_own(near_sum, (from_left(to_right), from_right(to_left), swap_far(to_row)))
    back = exchange(total.reshape(8, 96, 256), DP).reshape(768, 256)
    out_own = spread(combine(hidden, back, routes_t))
    out_other = swap_core(out_own)
    return (assemble(core, out_own, out_other), final)


def solution(mesh):
    wide = Mesh(mesh.devices.reshape(4, 2, 2, 4, 2), ("z", "ylo", "yhi", "x", "core"))
    return jax.shard_map(
        per_device,
        mesh=wide,
        in_specs=(
            P(DP, None),
            P(DP),
            P(DP, None),
            P(DP, None, TENSOR),
            P(DP, None, TENSOR),
            P(),
            P(DP, TENSOR),
            P(DP, TENSOR),
            P(None, TENSOR),
            P(TENSOR),
            P(TENSOR, None),
            P(TENSOR, None),
            P(None, TENSOR),
            P(TENSOR),
            P(None, TENSOR),
            P(TENSOR),
            P(TENSOR, DP),
            P(),
            P(),
            P(DP, None, TENSOR),
            P(DP, None, TENSOR),
            P(DP, TENSOR, None),
        ),
        out_specs=(P(DP, None), P(DP, None, TENSOR)),
        check_vma=False,
    )
```

```python
import jax
import jax.numpy as jnp
from jax import lax
from jax.sharding import Mesh
from jax.sharding import PartitionSpec as P
from jax.experimental import pallas as pl
from jax.experimental.pallas import tpu as pltpu

F32 = jnp.float32
BF16 = jnp.bfloat16
DP = ("z", "ylo")
TENSOR = ("yhi", "x", "core")
CHIPS = ("yhi", "x")
EPS = 1e-05
LOG2E = 1.4426950408889634


def params(megabytes=48):
    return pltpu.CompilerParams(vmem_limit_bytes=megabytes << 20)


def call(body, scalars, grid, in_specs, out_specs, out_shape, scratch=(), cost=None):
    if cost is None:
        cost = pl.CostEstimate(flops=1 << 20, bytes_accessed=1 << 16, transcendentals=0)
    spec = pltpu.PrefetchScalarGridSpec(
        num_scalar_prefetch=len(scalars),
        grid=grid,
        in_specs=in_specs,
        out_specs=out_specs,
        scratch_shapes=scratch,
    )
    return pl.pallas_call(
        body, grid_spec=spec, out_shape=out_shape, compiler_params=params(), cost_estimate=cost
    )


def exchange(value, axes):
    return lax.all_to_all(value, axes, split_axis=0, concat_axis=0, tiled=True)


def spread(value):
    return exchange(jnp.broadcast_to(value[None], (8,) + value.shape), CHIPS)


def from_left(value):
    return lax.ppermute(value, "x", [(i, (i + 1) % 4) for i in range(4)])


def from_right(value):
    return lax.ppermute(value, "x", [(i, (i - 1) % 4) for i in range(4)])


def swap_far(value):
    return lax.ppermute(value, "yhi", [(0, 1), (1, 0)])


def add_half(value, received):
    return (value.astype(F32) + received.astype(F32)).astype(BF16)


def swap_core(value):
    return lax.ppermute(value, "core", [(0, 1), (1, 0)])


def sigmoid(value):
    return 1.0 / (1.0 + jnp.exp(-value))


def silu(value):
    return value * sigmoid(value)


RING = (0, 3, 1, 2)


def from_below(value):
    return lax.ppermute(value, "z", [(i, (i + 1) % 4) for i in range(4)])


def from_above(value):
    return lax.ppermute(value, "z", [(i, (i - 1) % 4) for i in range(4)])


def after(value, *earlier):
    return lax.optimization_barrier((value,) + earlier)[0]


def swap_pair(value):
    return lax.ppermute(value, "ylo", [(0, 1), (1, 0)])


def gather_ring(block, below, above, halves):
    return block, below, above, from_below(halves[0]), from_above(halves[1])


def second_round(below, above, pair):
    return (
        jnp.concatenate([below[0:256], below[512:768], pair[0:256]]),
        jnp.concatenate([above[256:512], above[768:1024], pair[256:512]]),
        jnp.concatenate([above[512:768], below[768:1024]]),
    )


def third_round(up, down, over):
    return from_below(up[512:640]), from_above(over[128:256]), swap_pair(down[256:512])


def norm_split(place, x_rows, gain):
    def body(place_ref, x_ref, gain_ref, own_ref, send_ref):
        request = pl.ds(pl.multiple_of(place_ref[0] * 128, 128), 128)
        for rows, out_ref, member in (
            (slice(0, 256), own_ref, place_ref[2]),
            (request, send_ref, 1 - place_ref[2]),
        ):
            values = x_ref[rows, :].astype(F32)
            scale = lax.rsqrt(jnp.mean(values * values, axis=-1, keepdims=True) + EPS)
            for piece, shift in enumerate(RING):
                at = ((place_ref[1] + shift) % 4) * 2 + member
                columns = pl.ds(pl.multiple_of(at * 512, 512), 512)
                part = x_ref[rows, columns].astype(F32)
                out_ref[piece] = (part * scale * gain_ref[:, columns]).astype(BF16)

    return call(
        body,
        (place,),
        (1,),
        [
            pl.BlockSpec((256, 4096), lambda i, c: (0, 0)),
            pl.BlockSpec((1, 4096), lambda i, c: (0, 0)),
        ],
        [
            pl.BlockSpec((4, 256, 512), lambda i, c: (0, 0, 0)),
            pl.BlockSpec((4, 128, 512), lambda i, c: (0, 0, 0)),
        ],
        [
            jax.ShapeDtypeStruct((4, 256, 512), BF16),
            jax.ShapeDtypeStruct((4, 128, 512), BF16),
        ],
    )(place, x_rows, gain)


def ring_product(rows_ref, blocks):
    total = None
    for piece in range(3):
        term = jnp.dot(rows_ref[piece], blocks[piece][...], preferred_element_type=F32)
        total = term if total is None else total + term
    total = total + jnp.dot(rows_ref[3, :, 0:256], blocks[3][...], preferred_element_type=F32)
    return total + jnp.dot(rows_ref[3, :, 256:512], blocks[4][...], preferred_element_type=F32)


RING_SPECS = [pl.BlockSpec((512, 512), lambda *_: (0, 0))] * 3 + [
    pl.BlockSpec((256, 512), lambda *_: (0, 0))
] * 2


def pair_product(place, own, other, blocks):
    def body(place_ref, own_ref, other_ref, *refs):
        for slot, rows_ref in enumerate((own_ref, other_ref)):
            refs[5][place_ref[0] ^ slot] = ring_product(rows_ref, refs[:5]).astype(BF16)

    return call(
        body,
        (place,),
        (1,),
        [pl.BlockSpec((4, 128, 512), lambda i, c: (0, 0, 0))] * 2 + RING_SPECS,
        pl.BlockSpec((2, 128, 512), lambda i, c: (0, 0, 0)),
        jax.ShapeDtypeStruct((2, 128, 512), BF16),
    )(place, own, other, *blocks)


def own_product(rows, blocks):
    def body(rows_ref, *refs):
        refs[5][...] = ring_product(rows_ref, refs[:5]).reshape(2, 128, 512)

    return call(
        body,
        (),
        (1,),
        [pl.BlockSpec((4, 256, 512), lambda i: (0, 0, 0))] + RING_SPECS,
        pl.BlockSpec((2, 128, 512), lambda i: (0, 0, 0)),
        jax.ShapeDtypeStruct((2, 128, 512), F32),
    )(rows, *blocks)


def conv_project(core, near, far, history, conv_w, conv_b, weight):
    def body(core_ref, near_ref, far_ref, hist_ref, cw_ref, cb_ref, w_ref, conv_ref, low_ref, line):
        x_inner = (near_ref[0] + far_ref[0].astype(F32)).astype(BF16).astype(F32)
        line[0:8] = hist_ref[0]
        line[8:136] = x_inner
        total = cb_ref[...] + cw_ref[3:4] * x_inner
        for tap in range(3):
            total = total + cw_ref[tap : tap + 1] * line[5 + tap : 133 + tap]
        conv = silu(total).astype(BF16)
        conv_ref[0] = conv
        low_ref[0] = jnp.dot(conv, w_ref[...], preferred_element_type=F32).astype(BF16)

    return call(
        body,
        (core,),
        (2,),
        [
            pl.BlockSpec((1, 128, 512), lambda r, c: (r, 0, 0)),
            pl.BlockSpec((1, 128, 512), lambda r, c: (r, 0, 0)),
            pl.BlockSpec((1, 8, 512), lambda r, c: (r, 0, 0)),
            pl.BlockSpec((4, 512), lambda r, c: (0, 0)),
            pl.BlockSpec((1, 512), lambda r, c: (0, 0)),
            pl.BlockSpec((512, 640), lambda r, c: (0, 0)),
        ],
        [
            pl.BlockSpec((1, 128, 512), lambda r, c: (r, 0, 0)),
            pl.BlockSpec((1, 128, 640), lambda r, c: (r ^ c[0], 0, 0)),
        ],
        [
            jax.ShapeDtypeStruct((2, 128, 512), BF16),
            jax.ShapeDtypeStruct((2, 128, 640), BF16),
        ],
        (pltpu.VMEM((136, 512), F32),),
    )(core, near, far, history, conv_w, conv_b, weight)


def scan_block(
    core, lengths, low_own, low_other, conv, dt_proj, dt_bias, decay, skip, state
):
    def body(
        core_ref,
        len_ref,
        own_ref,
        other_ref,
        conv_ref,
        dtp_ref,
        dtb_ref,
        decay_ref,
        skip_ref,
        state_ref,
        mixed_ref,
        final_ref,
        step_s,
        drive_s,
        trail_s,
        dec_s,
    ):
        dec_s[...] = decay_ref[...] * (-LOG2E)
        lane = lax.broadcasted_iota(jnp.int32, (128, 128), 1)
        row = lax.broadcasted_iota(jnp.int32, (128, 128), 0)
        pick_entry = (row == lane % 16).astype(BF16)
        pick_read = (row == 16 + lane % 16).astype(BF16)
        diagonal = ((lane // 16) == (row % 8)).astype(F32)
        position = lax.broadcasted_iota(jnp.int32, (128, 512), 0)
        reads = []
        for slot, low_ref in enumerate((own_ref, other_ref)):
            request = core_ref[0] ^ slot
            mask = (position < len_ref[request]).astype(F32)
            raw = jnp.dot(low_ref[:, 0:512], dtp_ref[...], preferred_element_type=F32) + dtb_ref[...]
            step = (jnp.maximum(raw, 0.0) + jnp.log(1.0 + jnp.exp(-jnp.abs(raw)))) * mask
            step_s[slot] = step
            drive = (step * conv_ref[request].astype(F32)).astype(BF16)
            tail = low_ref[:, 512:640]
            entry = (jnp.dot(tail, pick_entry, preferred_element_type=F32) * diagonal).astype(BF16)
            reads.append(
                (jnp.dot(tail, pick_read, preferred_element_type=F32) * diagonal).astype(BF16)
            )
            for piece in range(8):
                for half in range(2):
                    at = piece * 16 + half * 8
                    keep = (
                        lax.broadcasted_iota(jnp.int32, (16, 128), 0) // 8 == half
                    ).astype(BF16)
                    drive_s[slot, at * 16 : at * 16 + 128] = lax.dot_general(
                        entry[piece * 16 : piece * 16 + 16] * keep,
                        drive[piece * 16 : piece * 16 + 16],
                        (((0,), (0,)), ((), ())),
                        preferred_element_type=F32,
                    )

        def advance(block, held):
            held = list(held)
            base = pl.multiple_of(block * 8, 8)
            for slot in range(2):
                steps = step_s[slot, pl.ds(base, 8)]
                now = held[slot]
                for offset in range(8):
                    rows = pl.ds(pl.multiple_of(block * 128 + offset * 16, 16), 16)
                    now = jnp.exp2(steps[offset : offset + 1] * dec_s[...]) * now + drive_s[slot, rows]
                    trail_s[slot, rows] = now.astype(BF16)
                held[slot] = now
            return tuple(held)

        first = tuple(state_ref[core_ref[0] ^ slot] for slot in range(2))
        last = lax.fori_loop(0, 16, advance, first)
        for slot in range(2):
            request = core_ref[0] ^ slot
            final_ref[request] = last[slot]
            outs = []
            for piece in range(16):
                outs.append(
                    jnp.dot(
                        reads[slot][piece * 8 : piece * 8 + 8],
                        trail_s[slot, piece * 128 : piece * 128 + 128],
                        preferred_element_type=F32,
                    )
                )
            mask = (position < len_ref[request]).astype(F32)
            mixed = jnp.concatenate(outs, axis=0) + skip_ref[...] * conv_ref[request].astype(F32)
            mixed_ref[request] = mixed * mask

    def whole(*shape):
        return pl.BlockSpec(shape, lambda i, c, n: (0,) * len(shape))

    return call(
        body,
        (core, lengths),
        (1,),
        [
            whole(128, 640),
            whole(128, 640),
            whole(2, 128, 512),
            whole(512, 512),
            whole(1, 512),
            whole(16, 512),
            whole(1, 512),
            whole(2, 16, 512),
        ],
        [whole(2, 128, 512), whole(2, 16, 512)],
        [
            jax.ShapeDtypeStruct((2, 128, 512), F32),
            jax.ShapeDtypeStruct((2, 16, 512), F32),
        ],
        (
            pltpu.VMEM((2, 128, 512), F32),
            pltpu.VMEM((2, 2048, 512), F32),
            pltpu.VMEM((2, 2048, 512), BF16),
            pltpu.VMEM((16, 512), F32),
        ),
    )(
        core,
        lengths,
        low_own,
        low_other,
        conv,
        dt_proj,
        dt_bias,
        decay,
        skip,
        state,
    )


def mixer_product(place, mixed, z_near, z_far, blocks):
    def body(place_ref, mixed_ref, near_ref, far_ref, *refs):
        own, below, above, pair, up_two, up_pair, down_two, down_pair, over, low, mid, high = refs[:12]
        own_ref, other_ref = refs[12:]
        z_gate = (near_ref[...] + far_ref[...].astype(F32)).astype(BF16).astype(F32)
        gated = (mixed_ref[...] * silu(z_gate)).astype(BF16).reshape(256, 512)

        def times(begin, end, value):
            return jnp.dot(gated[:, begin:end], value, preferred_element_type=F32)

        def split(top, bottom):
            return times(0, 256, top) + times(256, 512, bottom)

        sums = (
            lambda: times(0, 512, own[...]),
            lambda: times(0, 512, below[...]),
            lambda: times(0, 512, above[...]),
            lambda: split(up_two[...], down_two[...]),
            lambda: times(0, 512, pair[...]),
            lambda: split(up_pair[...], over[256:512]),
            lambda: split(over[0:256], down_pair[...]),
            lambda: times(0, 128, low[...]) + times(128, 256, mid[...]) + times(256, 512, high[...]),
        )
        for index, make in enumerate(sums):
            value = make().astype(BF16)
            part = ((place_ref[1] + RING[index % 4]) % 4) * 2 + (place_ref[2] ^ (index // 4))

            @pl.when(part // 4 == place_ref[0])
            def _():
                own_ref[part % 4, 0] = value[:, 0:256]
                own_ref[part % 4, 1] = value[:, 256:512]

            @pl.when(part // 4 != place_ref[0])
            def _():
                other_ref[part % 4, 0] = value[:, 0:256]
                other_ref[part % 4, 1] = value[:, 256:512]

    def whole(*shape):
        return pl.BlockSpec(shape, lambda i, c: (0,) * len(shape))

    def rows_at(count, index):
        return pl.BlockSpec((count, 512), lambda i, c: (index, 0))

    out_block, below, above, pair, up, down, over, low, mid, high = blocks
    return call(
        body,
        (place,),
        (1,),
        [whole(2, 128, 512)] * 3
        + [rows_at(512, 0), rows_at(512, 1), rows_at(512, 1), rows_at(512, 0)]
        + [rows_at(256, 1), rows_at(256, 2)] * 2
        + [rows_at(512, 0), rows_at(128, 0), rows_at(128, 0), rows_at(256, 0)],
        [whole(4, 2, 256, 256)] * 2,
        [jax.ShapeDtypeStruct((4, 2, 256, 256), BF16)] * 2,
    )(
        place,
        mixed,
        z_near,
        z_far,
        out_block,
        below,
        above,
        pair,
        up,
        up,
        down,
        down,
        over,
        low,
        mid,
        high,
    )


def tables_of(routes_t):
    expert = lax.broadcasted_iota(jnp.int32, (8, 256), 0)
    picks = [(expert == routes_t[k : k + 1]) for k in range(2)]
    counts = (picks[0] | picks[1]).astype(BF16)
    earlier = (
        lax.broadcasted_iota(jnp.int32, (256, 256), 0)
        < lax.broadcasted_iota(jnp.int32, (256, 256), 1)
    ).astype(BF16)
    before = jnp.dot(counts, earlier, preferred_element_type=F32)
    place = before + 96.0 * expert.astype(F32)
    slot_row = lax.broadcasted_iota(jnp.int32, (768, 256), 0)
    hit = None
    for pick in picks:
        slot = jnp.sum(jnp.where(pick, place, 0.0), axis=0, keepdims=True).astype(jnp.int32)
        mine = slot_row == slot
        hit = mine if hit is None else hit | mine
    return hit.astype(BF16)


def hidden_dispatch(block, parts, x_rows, gain, routes_t):
    def body(block_ref, parts_ref, x_ref, gain_ref, routes_ref, hidden_ref, out_ref):
        mixer = jnp.sum(parts_ref[...].astype(F32), axis=0)
        hidden = (x_ref[...].astype(F32) + mixer).astype(BF16)
        hidden_ref[...] = hidden
        scaled = (hidden.astype(F32) * gain_ref[...]).astype(BF16)
        out_ref[...] = jnp.dot(
            tables_of(routes_ref[...]), scaled, preferred_element_type=F32
        ).astype(BF16)

    return call(
        body,
        (block,),
        (1,),
        [
            pl.BlockSpec((8, 256, 256), lambda i, b: (0, 0, 0)),
            pl.BlockSpec((256, 256), lambda i, b: (0, b[0])),
            pl.BlockSpec((1, 256), lambda i, b: (0, b[0])),
            pl.BlockSpec((2, 256), lambda i, b: (0, 0)),
        ],
        [
            pl.BlockSpec((256, 256), lambda i, b: (0, 0)),
            pl.BlockSpec((768, 256), lambda i, b: (0, 0)),
        ],
        [
            jax.ShapeDtypeStruct((256, 256), BF16),
            jax.ShapeDtypeStruct((768, 256), BF16),
        ],
    )(block, parts, x_rows, gain, routes_t)


def block_places(core_at, x_at, far_at):
    near = [far_at * 4 + (x_at + step) % 4 for step in (0, 3, 1)]
    cross = [(1 - far_at) * 4 + (x_at + step) % 4 for step in (0, 3, 1, 2)]
    two = far_at * 4 + (x_at + 2) % 4
    order = near + cross[0:1] + [two] + cross[1:4]
    return jnp.stack([core_at * 8 + at for at in order] + [(1 - core_at) * 8 + at for at in order])


def gate_up(places, first, rows, inverse, router_row, w_gate, w_up, held=None):
    def body(places_ref, *refs):
        rows_refs, inverse_refs, router_refs = refs[0:8], refs[8:16], refs[16:24]
        gate_refs, up_refs = refs[24:32], refs[32:40]

        def stats():
            squares, logits = None, None
            for piece in range(8):
                value = rows_refs[piece][...].astype(F32)
                square = value * inverse_refs[piece][...]
                square = square * square
                square = square[:, 0:128] + square[:, 128:256]
                squares = square if squares is None else squares + square
                logit = value * router_refs[piece][...]
                logit = logit[:, 0:128] + logit[:, 128:256]
                logits = logit if logits is None else logits + logit
            return squares, logits

        gate_w = jnp.concatenate([ref[...] for ref in gate_refs], axis=0)
        up_w = jnp.concatenate([ref[...] for ref in up_refs], axis=0)
        if held is None:
            gate_out, up_out, squares_out, logits_out = refs[40:]

            @pl.when(pl.program_id(0) == 0)
            def _():
                squares_out[...], logits_out[...] = stats()

        else:
            gate_in, up_in, squares_in, logits_in, active_out, scale_s, weight_s = refs[40:]

            @pl.when(pl.program_id(0) == 0)
            def _():
                squares, logits = stats()
                squares = jnp.sum(squares_in[...] + squares, axis=1, keepdims=True)
                logits = jnp.sum(logits_in[...] + logits, axis=1, keepdims=True)
                scale = lax.rsqrt(squares * (1.0 / 4096.0) + EPS)
                scale_s[...] = jnp.broadcast_to(scale, (768, 128))
                weight_s[...] = jnp.broadcast_to(scale * sigmoid(logits * scale), (768, 128))

        for begin in range(0, 768, 256):
            at = slice(begin, begin + 256)
            units = jnp.concatenate([ref[at, :] for ref in rows_refs], axis=1)
            gate = jnp.dot(units, gate_w, preferred_element_type=F32)
            up = jnp.dot(units, up_w, preferred_element_type=F32)
            if held is None:
                gate_out[at, :] = gate
                up_out[at, :] = up
            else:
                gate = (gate + gate_in[at, :]) * scale_s[at, 0:1]
                up = (up + up_in[at, :]) * weight_s[at, 0:1]
                active_out[at, :] = (silu(gate) * up).astype(BF16)

    def at(piece):
        return first + piece % 4 + 8 * (piece // 4)

    def row_spec(piece):
        return pl.BlockSpec((1, 256), lambda n, p: (0, p[at(piece)]))

    def weight_spec(piece):
        return pl.BlockSpec((256, 256), lambda n, p: (p[at(piece)], n))

    def whole(*shape):
        return pl.BlockSpec(shape, lambda n, p: (0, 0))

    tile = pl.BlockSpec((768, 256), lambda n, p: (0, n))
    kept = [tile, tile, whole(768, 128), whole(768, 128)]
    if held is None:
        outs = kept
        shapes = [jax.ShapeDtypeStruct((768, 768), F32)] * 2 + [
            jax.ShapeDtypeStruct((768, 128), F32)
        ] * 2
    else:
        outs, shapes = tile, jax.ShapeDtypeStruct((768, 768), BF16)
    return call(
        body,
        (places,),
        (3,),
        [whole(768, 256)] * 8
        + [row_spec(piece) for piece in range(8)] * 2
        + [weight_spec(piece) for piece in range(8)] * 2
        + ([] if held is None else kept),
        outs,
        shapes,
        () if held is None else (pltpu.VMEM((768, 128), F32),) * 2,
        cost=pl.CostEstimate(flops=2 * 768 * 2048 * 1536, bytes_accessed=20 << 20, transcendentals=0),
    )(
        places,
        *rows,
        *([inverse] * 8),
        *([router_row] * 8),
        *([w_gate] * 8),
        *([w_up] * 8),
        *(() if held is None else held),
    )


def down_product(places, first, active, w_down, received=None):
    def body(places_ref, rows_ref, *refs):
        out_ref = refs[-1]
        for side in range(2):
            value = jnp.dot(rows_ref[...], refs[side][...], preferred_element_type=F32)
            if received is not None:
                value = value + refs[2][side].astype(F32)
            out_ref[side] = value.astype(BF16)

    def weight_spec(side):
        return pl.BlockSpec((768, 256), lambda i, p: (0, p[first + 2 * i + side]))

    blocks = pl.BlockSpec((2, 768, 256), lambda i, p: (i, 0, 0))
    return call(
        body,
        (places,),
        (2,),
        [pl.BlockSpec((768, 768), lambda i, p: (0, 0)), weight_spec(0), weight_spec(1)]
        + ([] if received is None else [blocks]),
        blocks,
        jax.ShapeDtypeStruct((4, 768, 256), BF16),
        cost=pl.CostEstimate(flops=2 * 768 * 768 * 1024, bytes_accessed=5 << 20, transcendentals=0),
    )(places, active, w_down, w_down, *(() if received is None else (received,)))


def whole_call(body, shapes, operands):
    def spec(shape):
        return pl.BlockSpec(shape, lambda i: (0,) * len(shape))

    outs = [jax.ShapeDtypeStruct(shape, BF16) for shape in shapes]
    return call(
        body,
        (),
        (1,),
        [spec(value.shape) for value in operands],
        [spec(shape) for shape in shapes],
        outs,
    )(*operands)


def fold_far(far, corner):
    def body(far_ref, low_ref, mid_ref, high_ref, up_ref, down_ref, cross_ref):
        def add(block, begin, end, ref, at):
            return (
                far_ref[block, begin:end].astype(F32) + ref[at : at + end - begin].astype(F32)
            ).astype(BF16)

        up_ref[0:384] = far_ref[0, 0:384]
        up_ref[384:640] = add(2, 0, 256, low_ref, 0)
        up_ref[640:768] = far_ref[2, 256:384]
        down_ref[0:128] = far_ref[0, 384:512]
        down_ref[128:384] = add(0, 512, 768, high_ref, 0)
        down_ref[384:512] = add(1, 384, 512, mid_ref, 128)
        down_ref[512:768] = far_ref[1, 512:768]
        cross_ref[0:384] = far_ref[2, 384:768]
        cross_ref[384:640] = far_ref[1, 0:256]
        cross_ref[640:768] = add(1, 256, 384, mid_ref, 0)

    return whole_call(body, [(768, 256)] * 3, (far,) + corner)


def fold_near(near, up, down, cross):
    def body(near_ref, up_ref, down_ref, cross_ref, left_ref, right_ref, row_ref):
        for out_ref, block, top, bottom in (
            (right_ref, 2, up_ref[0:384], cross_ref[0:384]),
            (left_ref, 1, cross_ref[384:768], down_ref[0:384]),
            (row_ref, 3, up_ref[384:768], down_ref[384:768]),
        ):
            out_ref[0:384] = (near_ref[block, 0:384].astype(F32) + top.astype(F32)).astype(BF16)
            out_ref[384:768] = (near_ref[block, 384:768].astype(F32) + bottom.astype(F32)).astype(
                BF16
            )

    return whole_call(body, [(768, 256)] * 3, (near, up, down, cross))


def fold_own(near, parts):
    def body(near_ref, a_ref, b_ref, c_ref, out_ref):
        total = near_ref[0].astype(F32) + a_ref[...].astype(F32)
        out_ref[...] = (total + b_ref[...].astype(F32) + c_ref[...].astype(F32)).astype(BF16)

    return whole_call(body, [(768, 256)], (near,) + parts)[0]


def combine(hidden, back, routes_t):
    def body(hidden_ref, back_ref, routes_ref, out_ref):
        mixed = lax.dot_general(
            tables_of(routes_ref[...]),
            back_ref[...],
            (((0,), (0,)), ((), ())),
            preferred_element_type=F32,
        )
        out_ref[...] = (hidden_ref[...].astype(F32) + mixed).astype(BF16)

    return call(
        body,
        (),
        (1,),
        [
            pl.BlockSpec((256, 256), lambda i: (0, 0)),
            pl.BlockSpec((768, 256), lambda i: (0, 0)),
            pl.BlockSpec((2, 256), lambda i: (0, 0)),
        ],
        pl.BlockSpec((256, 256), lambda i: (0, 0)),
        jax.ShapeDtypeStruct((256, 256), BF16),
    )(hidden, back, routes_t)


def assemble(core, own, other):
    def body(core_ref, own_ref, other_ref, out_ref):
        for side, ref in enumerate((own_ref, other_ref)):

            @pl.when(pl.program_id(0) == side)
            def _():
                for piece in range(4):
                    out_ref[:, piece * 256 : piece * 256 + 256] = ref[piece]

    return call(
        body,
        (core,),
        (2, 2),
        [
            pl.BlockSpec((4, 256, 256), lambda s, i, c: (jnp.where(s == 0, i, 1), 0, 0)),
            pl.BlockSpec((4, 256, 256), lambda s, i, c: (jnp.where(s == 0, 0, i), 0, 0)),
        ],
        pl.BlockSpec((256, 1024), lambda s, i, c: (0, (c[0] ^ s) * 2 + i)),
        jax.ShapeDtypeStruct((256, 4096), BF16),
    )(core, own, other)


def per_device(
    x_rows,
    lengths,
    routes,
    conv_state,
    ssm_state,
    norm1_gain,
    in_x,
    in_z,
    conv_w,
    conv_b,
    x_dt,
    x_bc,
    dt_proj,
    dt_bias,
    decay_rate,
    skip,
    out_w,
    norm2_gain,
    router,
    w_gate,
    w_up,
    w_down,
):
    core_at = lax.axis_index("core").astype(jnp.int32)
    core = core_at.reshape(1)
    chip_at = lax.axis_index(CHIPS).astype(jnp.int32)
    block = (core_at * 8 + chip_at).reshape(1)
    expert_at = lax.axis_index(DP).astype(jnp.int32)

    place = jnp.stack(
        [core_at, lax.axis_index("z").astype(jnp.int32), lax.axis_index("ylo").astype(jnp.int32)]
    )
    low_weight = jnp.concatenate([x_dt, x_bc, jnp.zeros((512, 96), BF16)], axis=1)
    history = jnp.pad(conv_state.astype(F32), ((0, 0), (5, 0), (0, 0)))
    routes_t = routes.T
    router_row = lax.dynamic_slice(router, (0, expert_at), (4096, 1)).astype(F32).reshape(1, 4096)

    rows_mine, rows_send = norm_split(place, x_rows, norm1_gain.reshape(1, 4096))
    pair_own = swap_pair(rows_send)
    x_below, x_above = from_below(in_x), from_above(in_x)
    x_halves = (x_below[:256], x_above[256:])
    x_blocks = gather_ring(in_x, x_below, x_above, x_halves)
    pair_other = swap_core(after(pair_own, *x_halves))
    both = after(jnp.concatenate([in_z, out_w]), pair_other, *x_halves)
    both_below, both_above = from_below(both), from_above(both)
    out_pair = swap_pair(after(out_w, pair_own))
    x_far = swap_pair(pair_product(place, pair_own, pair_other, x_blocks))
    sends = second_round(both_below, both_above, out_pair)
    x_near = after(own_product(rows_mine, x_blocks), *sends)
    conv, low = conv_project(
        core, x_near, x_far, history, conv_w, conv_b.reshape(1, 512), low_weight
    )
    low_pair = add_half(low[0], swap_core(low[1]))
    low_four = add_half(low_pair, lax.ppermute(low_pair, "x", [(i, i ^ 1) for i in range(4)]))
    low_line = add_half(low_four, lax.ppermute(low_four, "x", [(i, i ^ 2) for i in range(4)]))
    up, down, over = from_below(sends[0]), from_above(sends[1]), swap_pair(sends[2])
    low_own = add_half(low_line, swap_far(low_line))
    low_other = swap_core(low_own)
    mixed, final = scan_block(
        core,
        lengths,
        low_own,
        low_other,
        conv,
        dt_proj,
        dt_bias.reshape(1, 512),
        decay_rate,
        skip.reshape(1, 512),
        ssm_state,
    )
    z_blocks = (in_z, both_below, both_above, up, down)
    z_far = swap_pair(pair_product(place, pair_own, pair_other, z_blocks))
    corner = third_round(up, down, over)
    z_near = own_product(rows_mine, z_blocks)
    out_blocks = (out_w, both_below, both_above, out_pair, up, down, over) + corner
    mixer_own, mixer_other = mixer_product(place, mixed, z_near, z_far, out_blocks)
    mixer_pair = (mixer_own.astype(F32) + swap_core(mixer_other).astype(F32)).astype(BF16)
    mixer_parts = exchange(mixer_pair.reshape(8, 256, 256), CHIPS)
    places = block_places(
        core_at, lax.axis_index("x").astype(jnp.int32), lax.axis_index("yhi").astype(jnp.int32)
    )
    gain = norm2_gain.reshape(1, 4096)
    hidden, outgoing = hidden_dispatch(block, mixer_parts, x_rows, gain, routes_t)
    rows = exchange(outgoing.reshape(8, 96, 256), DP).reshape(768, 256)
    left, right, cross = from_left(rows), from_right(rows), swap_far(rows)
    near = (rows, left, right, cross)
    near_other = tuple(swap_core(value) for value in near)
    top, bottom = slice(0, 384), slice(384, 768)
    up = from_left(jnp.concatenate([left[top], cross[top]]))
    down = from_right(jnp.concatenate([right[bottom], cross[bottom]]))
    over = swap_far(jnp.concatenate([right[top], left[bottom]]))
    inverse = 1.0 / gain
    held = gate_up(places, 0, near + near_other, inverse, router_row, w_gate[0], w_up[0])
    up, down, over = (after(value, held[2]) for value in (up, down, over))
    two = jnp.concatenate([up[top], down[top]])
    cross_left = jnp.concatenate([up[bottom], over[bottom]])
    cross_right = jnp.concatenate([over[top], down[bottom]])
    cross_two = jnp.concatenate(
        [from_left(cross_left[0:256]), from_right(cross_right[256:512]), swap_far(two[512:768])]
    )
    far = (two, cross_left, cross_right, cross_two)
    far_other = tuple(swap_core(value) for value in far)
    active = gate_up(places, 4, far + far_other, inverse, router_row, w_gate[0], w_up[0], held)
    far_sent = swap_core(down_product(places, 12, active, w_down[0]))
    near_sent = swap_core(down_product(places, 8, active, w_down[0]))
    far_sum = down_product(places, 4, active, w_down[0], far_sent)
    corner = (
        from_left(far_sum[3, 0:256]),
        from_right(far_sum[3, 256:512]),
        swap_far(far_sum[3, 512:768]),
    )
    near_sum = down_product(places, 0, active, w_down[0], near_sent)
    up_send, down_send, cross_send = fold_far(far_sum, corner)
    to_left, to_right, to_row = fold_near(
        near_sum, from_left(up_send), from_right(down_send), swap_far(cross_send)
    )
    total = fold_own(near_sum, (from_left(to_right), from_right(to_left), swap_far(to_row)))
    back = exchange(total.reshape(8, 96, 256), DP).reshape(768, 256)
    out_own = spread(combine(hidden, back, routes_t))
    out_other = swap_core(out_own)
    return (assemble(core, out_own, out_other), final)


def solution(mesh):
    wide = Mesh(mesh.devices.reshape(4, 2, 2, 4, 2), ("z", "ylo", "yhi", "x", "core"))
    return jax.shard_map(
        per_device,
        mesh=wide,
        in_specs=(
            P(DP, None),
            P(DP),
            P(DP, None),
            P(DP, None, TENSOR),
            P(DP, None, TENSOR),
            P(),
            P(DP, TENSOR),
            P(DP, TENSOR),
            P(None, TENSOR),
            P(TENSOR),
            P(TENSOR, None),
            P(TENSOR, None),
            P(None, TENSOR),
            P(TENSOR),
            P(None, TENSOR),
            P(TENSOR),
            P(TENSOR, DP),
            P(),
            P(),
            P(DP, None, TENSOR),
            P(DP, None, TENSOR),
            P(DP, TENSOR, None),
        ),
        out_specs=(P(DP, None), P(DP, None, TENSOR)),
        check_vma=False,
    )
```

```python
import jax
import jax.numpy as jnp
from jax import lax
from jax.sharding import Mesh
from jax.sharding import PartitionSpec as P
from jax.experimental import pallas as pl
from jax.experimental.pallas import tpu as pltpu

F32 = jnp.float32
BF16 = jnp.bfloat16
DP = ("z", "ylo")
TENSOR = ("yhi", "x", "core")
CHIPS = ("yhi", "x")
EPS = 1e-05
LOG2E = 1.4426950408889634


def params(megabytes):
    return pltpu.CompilerParams(vmem_limit_bytes=megabytes << 20)


def call(
    body, scalars, grid, in_specs, out_specs, out_shape, scratch=(), cost=None, megabytes=24
):
    if cost is None:
        cost = pl.CostEstimate(flops=1 << 20, bytes_accessed=1 << 16, transcendentals=0)
    spec = pltpu.PrefetchScalarGridSpec(
        num_scalar_prefetch=len(scalars),
        grid=grid,
        in_specs=in_specs,
        out_specs=out_specs,
        scratch_shapes=scratch,
    )
    return pl.pallas_call(
        body, grid_spec=spec, out_shape=out_shape, compiler_params=params(megabytes), cost_estimate=cost
    )


def exchange(value, axes):
    return lax.all_to_all(value, axes, split_axis=0, concat_axis=0, tiled=True)


def spread(value):
    return exchange(jnp.broadcast_to(value[None], (8,) + value.shape), CHIPS)


def from_left(value):
    return lax.ppermute(value, "x", [(i, (i + 1) % 4) for i in range(4)])


def from_right(value):
    return lax.ppermute(value, "x", [(i, (i - 1) % 4) for i in range(4)])


def swap_far(value):
    return lax.ppermute(value, "yhi", [(0, 1), (1, 0)])


def add_half(value, received):
    return (value.astype(F32) + received.astype(F32)).astype(BF16)


def swap_core(value):
    return lax.ppermute(value, "core", [(0, 1), (1, 0)])


def sigmoid(value):
    return 1.0 / (1.0 + jnp.exp(-value))


def silu(value):
    return value * sigmoid(value)


RING = (0, 3, 1, 2)


def from_below(value):
    return lax.ppermute(value, "z", [(i, (i + 1) % 4) for i in range(4)])


def from_above(value):
    return lax.ppermute(value, "z", [(i, (i - 1) % 4) for i in range(4)])


def after(value, *earlier):
    return lax.optimization_barrier((value,) + earlier)[0]


def swap_pair(value):
    return lax.ppermute(value, "ylo", [(0, 1), (1, 0)])


def gather_ring(block, below, above, halves):
    return block, below, above, from_below(halves[0]), from_above(halves[1])


def second_round(below, above, pair):
    return (
        jnp.concatenate([below[:256], pair[:256]]),
        jnp.concatenate([above[256:], pair[256:]]),
        jnp.concatenate([above[:256], below[256:]]),
    )


def third_round(up, down, over):
    return from_below(up[256:384]), from_above(over[128:256]), swap_pair(down[:256])


def norm_split(place, x_rows, gain):
    def body(place_ref, x_ref, gain_ref, own_ref, send_ref):
        request = pl.ds(pl.multiple_of(place_ref[0] * 128, 128), 128)
        for rows, out_ref, member in (
            (slice(0, 256), own_ref, place_ref[2]),
            (request, send_ref, 1 - place_ref[2]),
        ):
            values = x_ref[rows, :].astype(F32)
            scale = lax.rsqrt(jnp.mean(values * values, axis=-1, keepdims=True) + EPS)
            for piece, shift in enumerate(RING):
                at = ((place_ref[1] + shift) % 4) * 2 + member
                columns = pl.ds(pl.multiple_of(at * 512, 512), 512)
                part = x_ref[rows, columns].astype(F32)
                out_ref[piece] = (part * scale * gain_ref[:, columns]).astype(BF16)

    return call(
        body,
        (place,),
        (1,),
        [
            pl.BlockSpec((256, 4096), lambda i, c: (0, 0)),
            pl.BlockSpec((1, 4096), lambda i, c: (0, 0)),
        ],
        [
            pl.BlockSpec((4, 256, 512), lambda i, c: (0, 0, 0)),
            pl.BlockSpec((4, 128, 512), lambda i, c: (0, 0, 0)),
        ],
        [
            jax.ShapeDtypeStruct((4, 256, 512), BF16),
            jax.ShapeDtypeStruct((4, 128, 512), BF16),
        ],
    )(place, x_rows, gain)


def ring_product(rows_ref, blocks):
    total = None
    for piece in range(3):
        term = jnp.dot(rows_ref[piece], blocks[piece][...], preferred_element_type=F32)
        total = term if total is None else total + term
    if len(blocks) == 4:
        return total + jnp.dot(rows_ref[3], blocks[3][...], preferred_element_type=F32)
    total = total + jnp.dot(rows_ref[3, :, 0:256], blocks[3][...], preferred_element_type=F32)
    return total + jnp.dot(rows_ref[3, :, 256:512], blocks[4][...], preferred_element_type=F32)


def ring_operands(blocks):
    if isinstance(blocks, tuple):
        return [pl.BlockSpec(block.shape, lambda i, c: (0, 0)) for block in blocks], blocks

    def at(shift):
        return pl.BlockSpec((512, 512), lambda i, c: ((c[1] + shift) % 4, 0))

    return [at(shift) for shift in RING], (blocks,) * 4


def pair_product(place, own, other, blocks):
    specs, arrays = ring_operands(blocks)

    def body(place_ref, own_ref, other_ref, *refs):
        for slot, rows_ref in enumerate((own_ref, other_ref)):
            refs[-1][place_ref[0] ^ slot] = ring_product(rows_ref, refs[:-1]).astype(BF16)

    return call(
        body,
        (place,),
        (1,),
        [pl.BlockSpec((4, 128, 512), lambda i, c: (0, 0, 0))] * 2 + specs,
        pl.BlockSpec((2, 128, 512), lambda i, c: (0, 0, 0)),
        jax.ShapeDtypeStruct((2, 128, 512), BF16),
    )(place, own, other, *arrays)


def own_product(place, rows, blocks):
    specs, arrays = ring_operands(blocks)

    def body(place_ref, rows_ref, *refs):
        refs[-1][...] = ring_product(rows_ref, refs[:-1]).reshape(2, 128, 512)

    return call(
        body,
        (place,),
        (1,),
        [pl.BlockSpec((4, 256, 512), lambda i, c: (0, 0, 0))] + specs,
        pl.BlockSpec((2, 128, 512), lambda i, c: (0, 0, 0)),
        jax.ShapeDtypeStruct((2, 128, 512), F32),
    )(place, rows, *arrays)


def conv_project(core, near, far, history, conv_w, conv_b, weight):
    def body(core_ref, near_ref, far_ref, hist_ref, cw_ref, cb_ref, w_ref, conv_ref, low_ref, line):
        x_inner = (near_ref[0] + far_ref[0].astype(F32)).astype(BF16).astype(F32)
        line[0:8] = hist_ref[0]
        line[8:136] = x_inner
        total = cb_ref[...] + cw_ref[3:4] * x_inner
        for tap in range(3):
            total = total + cw_ref[tap : tap + 1] * line[5 + tap : 133 + tap]
        conv = silu(total).astype(BF16)
        conv_ref[0] = conv
        low_ref[0] = jnp.dot(conv, w_ref[...], preferred_element_type=F32).astype(BF16)

    return call(
        body,
        (core,),
        (2,),
        [
            pl.BlockSpec((1, 128, 512), lambda r, c: (r, 0, 0)),
            pl.BlockSpec((1, 128, 512), lambda r, c: (r, 0, 0)),
            pl.BlockSpec((1, 8, 512), lambda r, c: (r, 0, 0)),
            pl.BlockSpec((4, 512), lambda r, c: (0, 0)),
            pl.BlockSpec((1, 512), lambda r, c: (0, 0)),
            pl.BlockSpec((512, 640), lambda r, c: (0, 0)),
        ],
        [
            pl.BlockSpec((1, 128, 512), lambda r, c: (r, 0, 0)),
            pl.BlockSpec((1, 128, 640), lambda r, c: (r ^ c[0], 0, 0)),
        ],
        [
            jax.ShapeDtypeStruct((2, 128, 512), BF16),
            jax.ShapeDtypeStruct((2, 128, 640), BF16),
        ],
        (pltpu.VMEM((136, 512), F32),),
    )(core, near, far, history, conv_w, conv_b, weight)


def scan_block(
    core, lengths, low_own, low_other, conv, dt_proj, dt_bias, decay, skip, state
):
    def body(
        core_ref,
        len_ref,
        own_ref,
        other_ref,
        conv_ref,
        dtp_ref,
        dtb_ref,
        decay_ref,
        skip_ref,
        state_ref,
        mixed_ref,
        final_ref,
        step_s,
        drive_s,
        trail_s,
        dec_s,
    ):
        dec_s[...] = decay_ref[...] * (-LOG2E)
        lane = lax.broadcasted_iota(jnp.int32, (128, 128), 1)
        row = lax.broadcasted_iota(jnp.int32, (128, 128), 0)
        pick_entry = (row == lane % 16).astype(BF16)
        pick_read = (row == 16 + lane % 16).astype(BF16)
        diagonal = ((lane // 16) == (row % 8)).astype(F32)
        position = lax.broadcasted_iota(jnp.int32, (128, 512), 0)
        reads = []
        for slot, low_ref in enumerate((own_ref, other_ref)):
            request = core_ref[0] ^ slot
            mask = (position < len_ref[request]).astype(F32)
            raw = jnp.dot(low_ref[:, 0:512], dtp_ref[...], preferred_element_type=F32) + dtb_ref[...]
            step = (jnp.maximum(raw, 0.0) + jnp.log(1.0 + jnp.exp(-jnp.abs(raw)))) * mask
            step_s[slot] = step
            drive = (step * conv_ref[request].astype(F32)).astype(BF16)
            tail = low_ref[:, 512:640]
            entry = (jnp.dot(tail, pick_entry, preferred_element_type=F32) * diagonal).astype(BF16)
            reads.append(
                (jnp.dot(tail, pick_read, preferred_element_type=F32) * diagonal).astype(BF16)
            )
            for piece in range(8):
                for half in range(2):
                    at = piece * 16 + half * 8
                    keep = (
                        lax.broadcasted_iota(jnp.int32, (16, 128), 0) // 8 == half
                    ).astype(BF16)
                    drive_s[slot, at * 16 : at * 16 + 128] = lax.dot_general(
                        entry[piece * 16 : piece * 16 + 16] * keep,
                        drive[piece * 16 : piece * 16 + 16],
                        (((0,), (0,)), ((), ())),
                        preferred_element_type=F32,
                    )

        def advance(block, held):
            held = list(held)
            base = pl.multiple_of(block * 8, 8)
            for slot in range(2):
                steps = step_s[slot, pl.ds(base, 8)]
                now = held[slot]
                for offset in range(8):
                    rows = pl.ds(pl.multiple_of(block * 128 + offset * 16, 16), 16)
                    now = jnp.exp2(steps[offset : offset + 1] * dec_s[...]) * now + drive_s[slot, rows]
                    trail_s[slot, rows] = now.astype(BF16)
                held[slot] = now
            return tuple(held)

        first = tuple(state_ref[core_ref[0] ^ slot] for slot in range(2))
        last = lax.fori_loop(0, 16, advance, first)
        for slot in range(2):
            request = core_ref[0] ^ slot
            final_ref[request] = last[slot]
            outs = []
            for piece in range(16):
                outs.append(
                    jnp.dot(
                        reads[slot][piece * 8 : piece * 8 + 8],
                        trail_s[slot, piece * 128 : piece * 128 + 128],
                        preferred_element_type=F32,
                    )
                )
            mask = (position < len_ref[request]).astype(F32)
            mixed = jnp.concatenate(outs, axis=0) + skip_ref[...] * conv_ref[request].astype(F32)
            mixed_ref[request] = mixed * mask

    def whole(*shape):
        return pl.BlockSpec(shape, lambda i, c, n: (0,) * len(shape))

    return call(
        body,
        (core, lengths),
        (1,),
        [
            whole(128, 640),
            whole(128, 640),
            whole(2, 128, 512),
            whole(512, 512),
            whole(1, 512),
            whole(16, 512),
            whole(1, 512),
            whole(2, 16, 512),
        ],
        [whole(2, 128, 512), whole(2, 16, 512)],
        [
            jax.ShapeDtypeStruct((2, 128, 512), F32),
            jax.ShapeDtypeStruct((2, 16, 512), F32),
        ],
        (
            pltpu.VMEM((2, 128, 512), F32),
            pltpu.VMEM((2, 2048, 512), F32),
            pltpu.VMEM((2, 2048, 512), BF16),
            pltpu.VMEM((16, 512), F32),
        ),
    )(
        core,
        lengths,
        low_own,
        low_other,
        conv,
        dt_proj,
        dt_bias,
        decay,
        skip,
        state,
    )


def mixer_product(place, mixed, z_near, z_far, blocks):
    def body(place_ref, mixed_ref, near_ref, far_ref, *refs):
        own, below, above, pair, up, down, over, low, mid, high = refs[:10]
        own_ref, other_ref = refs[10:]
        z_gate = (near_ref[...] + far_ref[...].astype(F32)).astype(BF16).astype(F32)
        gated = (mixed_ref[...] * silu(z_gate)).astype(BF16).reshape(256, 512)

        def times(begin, end, value):
            return jnp.dot(gated[:, begin:end], value, preferred_element_type=F32)

        def split(top, bottom):
            return times(0, 256, top) + times(256, 512, bottom)

        sums = (
            lambda: times(0, 512, own[...]),
            lambda: times(0, 512, below[...]),
            lambda: times(0, 512, above[...]),
            lambda: split(up[0:256], down[0:256]),
            lambda: times(0, 512, pair[...]),
            lambda: split(up[256:512], over[256:512]),
            lambda: split(over[0:256], down[256:512]),
            lambda: times(0, 128, low[...]) + times(128, 256, mid[...]) + times(256, 512, high[...]),
        )
        for index, make in enumerate(sums):
            value = make().astype(BF16)
            part = ((place_ref[1] + RING[index % 4]) % 4) * 2 + (place_ref[2] ^ (index // 4))

            @pl.when(part // 4 == place_ref[0])
            def _():
                own_ref[part % 4, 0] = value[:, 0:256]
                own_ref[part % 4, 1] = value[:, 256:512]

            @pl.when(part // 4 != place_ref[0])
            def _():
                other_ref[part % 4, 0] = value[:, 0:256]
                other_ref[part % 4, 1] = value[:, 256:512]

    def whole(*shape):
        return pl.BlockSpec(shape, lambda i, c: (0,) * len(shape))

    return call(
        body,
        (place,),
        (1,),
        [whole(2, 128, 512)] * 3 + [whole(*block.shape) for block in blocks],
        [whole(4, 2, 256, 256)] * 2,
        [jax.ShapeDtypeStruct((4, 2, 256, 256), BF16)] * 2,
    )(place, mixed, z_near, z_far, *blocks)


def tables_of(routes_t):
    expert = lax.broadcasted_iota(jnp.int32, (8, 256), 0)
    picks = [(expert == routes_t[k : k + 1]) for k in range(2)]
    counts = (picks[0] | picks[1]).astype(BF16)
    earlier = (
        lax.broadcasted_iota(jnp.int32, (256, 256), 0)
        < lax.broadcasted_iota(jnp.int32, (256, 256), 1)
    ).astype(BF16)
    before = jnp.dot(counts, earlier, preferred_element_type=F32)
    place = before + 96.0 * expert.astype(F32)
    slot_row = lax.broadcasted_iota(jnp.int32, (768, 256), 0)
    hit = None
    for pick in picks:
        slot = jnp.sum(jnp.where(pick, place, 0.0), axis=0, keepdims=True).astype(jnp.int32)
        mine = slot_row == slot
        hit = mine if hit is None else hit | mine
    return hit.astype(BF16)


def hidden_dispatch(block, parts, x_rows, gain, routes_t):
    def body(block_ref, parts_ref, x_ref, gain_ref, routes_ref, hidden_ref, out_ref):
        mixer = jnp.sum(parts_ref[...].astype(F32), axis=0)
        hidden = (x_ref[...].astype(F32) + mixer).astype(BF16)
        hidden_ref[...] = hidden
        scaled = (hidden.astype(F32) * gain_ref[...]).astype(BF16)
        out_ref[...] = jnp.dot(
            tables_of(routes_ref[...]), scaled, preferred_element_type=F32
        ).astype(BF16)

    return call(
        body,
        (block,),
        (1,),
        [
            pl.BlockSpec((8, 256, 256), lambda i, b: (0, 0, 0)),
            pl.BlockSpec((256, 256), lambda i, b: (0, b[0])),
            pl.BlockSpec((1, 256), lambda i, b: (0, b[0])),
            pl.BlockSpec((2, 256), lambda i, b: (0, 0)),
        ],
        [
            pl.BlockSpec((256, 256), lambda i, b: (0, 0)),
            pl.BlockSpec((768, 256), lambda i, b: (0, 0)),
        ],
        [
            jax.ShapeDtypeStruct((256, 256), BF16),
            jax.ShapeDtypeStruct((768, 256), BF16),
        ],
    )(block, parts, x_rows, gain, routes_t)


def block_places(core_at, x_at, far_at):
    near = [far_at * 4 + (x_at + step) % 4 for step in (0, 3, 1)]
    cross = [(1 - far_at) * 4 + (x_at + step) % 4 for step in (0, 3, 1, 2)]
    two = far_at * 4 + (x_at + 2) % 4
    order = near + cross[0:1] + [two] + cross[1:4]
    return jnp.stack([core_at * 8 + at for at in order] + [(1 - core_at) * 8 + at for at in order])


def gate_up(places, first, rows, inverse, router_row, w_gate, w_up, held=None):
    def body(places_ref, *refs):
        rows_refs, inverse_refs, router_refs = refs[0:8], refs[8:16], refs[16:24]
        gate_refs, up_refs = refs[24:32], refs[32:40]

        def stats():
            squares, logits = None, None
            for piece in range(8):
                value = rows_refs[piece][...].astype(F32)
                square = value * inverse_refs[piece][...]
                square = square * square
                square = square[:, 0:128] + square[:, 128:256]
                squares = square if squares is None else squares + square
                logit = value * router_refs[piece][...]
                logit = logit[:, 0:128] + logit[:, 128:256]
                logits = logit if logits is None else logits + logit
            return squares, logits

        gate_w = jnp.concatenate([ref[...] for ref in gate_refs], axis=0)
        up_w = jnp.concatenate([ref[...] for ref in up_refs], axis=0)
        if held is None:
            gate_out, up_out, squares_out, logits_out = refs[40:]

            @pl.when(pl.program_id(0) == 0)
            def _():
                squares_out[...], logits_out[...] = stats()

        else:
            gate_in, up_in, squares_in, logits_in, active_out, scale_s, weight_s = refs[40:]

            @pl.when(pl.program_id(0) == 0)
            def _():
                squares, logits = stats()
                squares = jnp.sum(squares_in[...] + squares, axis=1, keepdims=True)
                logits = jnp.sum(logits_in[...] + logits, axis=1, keepdims=True)
                scale = lax.rsqrt(squares * (1.0 / 4096.0) + EPS)
                scale_s[...] = jnp.broadcast_to(scale, (768, 128))
                weight_s[...] = jnp.broadcast_to(scale * sigmoid(logits * scale), (768, 128))

        for begin in range(0, 768, 256):
            at = slice(begin, begin + 256)
            units = jnp.concatenate([ref[at, :] for ref in rows_refs], axis=1)
            gate = jnp.dot(units, gate_w, preferred_element_type=F32)
            up = jnp.dot(units, up_w, preferred_element_type=F32)
            if held is None:
                gate_out[at, :] = gate
                up_out[at, :] = up
            else:
                gate = (gate + gate_in[at, :]) * scale_s[at, 0:1]
                up = (up + up_in[at, :]) * weight_s[at, 0:1]
                active_out[at, :] = (silu(gate) * up).astype(BF16)

    def at(piece):
        return first + piece % 4 + 8 * (piece // 4)

    def row_spec(piece):
        return pl.BlockSpec((1, 256), lambda n, p: (0, p[at(piece)]))

    def weight_spec(piece):
        return pl.BlockSpec((256, 256), lambda n, p: (p[at(piece)], n))

    def whole(*shape):
        return pl.BlockSpec(shape, lambda n, p: (0, 0))

    tile = pl.BlockSpec((768, 256), lambda n, p: (0, n))
    kept = [tile, tile, whole(768, 128), whole(768, 128)]
    if held is None:
        outs = kept
        shapes = [jax.ShapeDtypeStruct((768, 768), F32)] * 2 + [
            jax.ShapeDtypeStruct((768, 128), F32)
        ] * 2
    else:
        outs, shapes = tile, jax.ShapeDtypeStruct((768, 768), BF16)
    return call(
        body,
        (places,),
        (3,),
        [whole(768, 256)] * 8
        + [row_spec(piece) for piece in range(8)] * 2
        + [weight_spec(piece) for piece in range(8)] * 2
        + ([] if held is None else kept),
        outs,
        shapes,
        () if held is None else (pltpu.VMEM((768, 128), F32),) * 2,
        cost=pl.CostEstimate(flops=2 * 768 * 2048 * 1536, bytes_accessed=20 << 20, transcendentals=0),
        megabytes=48,
    )(
        places,
        *rows,
        *([inverse] * 8),
        *([router_row] * 8),
        *([w_gate] * 8),
        *([w_up] * 8),
        *(() if held is None else held),
    )


def down_product(places, first, active, w_down, received=None):
    def body(places_ref, rows_ref, *refs):
        out_ref = refs[-1]
        for side in range(2):
            value = jnp.dot(rows_ref[...], refs[side][...], preferred_element_type=F32)
            if received is not None:
                value = value + refs[2][side].astype(F32)
            out_ref[side] = value.astype(BF16)

    def weight_spec(side):
        return pl.BlockSpec((768, 256), lambda i, p: (0, p[first + 2 * i + side]))

    blocks = pl.BlockSpec((2, 768, 256), lambda i, p: (i, 0, 0))
    return call(
        body,
        (places,),
        (2,),
        [pl.BlockSpec((768, 768), lambda i, p: (0, 0)), weight_spec(0), weight_spec(1)]
        + ([] if received is None else [blocks]),
        blocks,
        jax.ShapeDtypeStruct((4, 768, 256), BF16),
        cost=pl.CostEstimate(flops=2 * 768 * 768 * 1024, bytes_accessed=5 << 20, transcendentals=0),
        megabytes=48,
    )(places, active, w_down, w_down, *(() if received is None else (received,)))


def whole_call(body, shapes, operands):
    def spec(shape):
        return pl.BlockSpec(shape, lambda i: (0,) * len(shape))

    outs = [jax.ShapeDtypeStruct(shape, BF16) for shape in shapes]
    return call(
        body,
        (),
        (1,),
        [spec(value.shape) for value in operands],
        [spec(shape) for shape in shapes],
        outs,
    )(*operands)


def fold_far(far, corner):
    def body(far_ref, low_ref, mid_ref, high_ref, up_ref, down_ref, cross_ref):
        def add(block, begin, end, ref, at):
            return (
                far_ref[block, begin:end].astype(F32) + ref[at : at + end - begin].astype(F32)
            ).astype(BF16)

        up_ref[0:384] = far_ref[0, 0:384]
        up_ref[384:640] = add(2, 0, 256, low_ref, 0)
        up_ref[640:768] = far_ref[2, 256:384]
        down_ref[0:128] = far_ref[0, 384:512]
        down_ref[128:384] = add(0, 512, 768, high_ref, 0)
        down_ref[384:512] = add(1, 384, 512, mid_ref, 128)
        down_ref[512:768] = far_ref[1, 512:768]
        cross_ref[0:384] = far_ref[2, 384:768]
        cross_ref[384:640] = far_ref[1, 0:256]
        cross_ref[640:768] = add(1, 256, 384, mid_ref, 0)

    return whole_call(body, [(768, 256)] * 3, (far,) + corner)


def fold_near(near, up, down, cross):
    def body(near_ref, up_ref, down_ref, cross_ref, left_ref, right_ref, row_ref):
        for out_ref, block, top, bottom in (
            (right_ref, 2, up_ref[0:384], cross_ref[0:384]),
            (left_ref, 1, cross_ref[384:768], down_ref[0:384]),
            (row_ref, 3, up_ref[384:768], down_ref[384:768]),
        ):
            out_ref[0:384] = (near_ref[block, 0:384].astype(F32) + top.astype(F32)).astype(BF16)
            out_ref[384:768] = (near_ref[block, 384:768].astype(F32) + bottom.astype(F32)).astype(
                BF16
            )

    return whole_call(body, [(768, 256)] * 3, (near, up, down, cross))


def fold_own(near, parts):
    def body(near_ref, a_ref, b_ref, c_ref, out_ref):
        total = near_ref[0].astype(F32) + a_ref[...].astype(F32)
        out_ref[...] = (total + b_ref[...].astype(F32) + c_ref[...].astype(F32)).astype(BF16)

    return whole_call(body, [(768, 256)], (near,) + parts)[0]


def combine(hidden, back, routes_t):
    def body(hidden_ref, back_ref, routes_ref, out_ref):
        mixed = lax.dot_general(
            tables_of(routes_ref[...]),
            back_ref[...],
            (((0,), (0,)), ((), ())),
            preferred_element_type=F32,
        )
        out_ref[...] = (hidden_ref[...].astype(F32) + mixed).astype(BF16)

    return call(
        body,
        (),
        (1,),
        [
            pl.BlockSpec((256, 256), lambda i: (0, 0)),
            pl.BlockSpec((768, 256), lambda i: (0, 0)),
            pl.BlockSpec((2, 256), lambda i: (0, 0)),
        ],
        pl.BlockSpec((256, 256), lambda i: (0, 0)),
        jax.ShapeDtypeStruct((256, 256), BF16),
    )(hidden, back, routes_t)


def assemble(core, own, other):
    def body(core_ref, own_ref, other_ref, out_ref):
        for side, ref in enumerate((own_ref, other_ref)):

            @pl.when(pl.program_id(0) == side)
            def _():
                for piece in range(4):
                    out_ref[:, piece * 256 : piece * 256 + 256] = ref[piece]

    return call(
        body,
        (core,),
        (2, 2),
        [
            pl.BlockSpec((4, 256, 256), lambda s, i, c: (jnp.where(s == 0, i, 1), 0, 0)),
            pl.BlockSpec((4, 256, 256), lambda s, i, c: (jnp.where(s == 0, 0, i), 0, 0)),
        ],
        pl.BlockSpec((256, 1024), lambda s, i, c: (0, (c[0] ^ s) * 2 + i)),
        jax.ShapeDtypeStruct((256, 4096), BF16),
    )(core, own, other)


def per_device(
    x_rows,
    lengths,
    routes,
    conv_state,
    ssm_state,
    norm1_gain,
    in_x,
    in_z,
    conv_w,
    conv_b,
    x_dt,
    x_bc,
    dt_proj,
    dt_bias,
    decay_rate,
    skip,
    out_w,
    norm2_gain,
    router,
    w_gate,
    w_up,
    w_down,
):
    core_at = lax.axis_index("core").astype(jnp.int32)
    core = core_at.reshape(1)
    chip_at = lax.axis_index(CHIPS).astype(jnp.int32)
    block = (core_at * 8 + chip_at).reshape(1)
    expert_at = lax.axis_index(DP).astype(jnp.int32)

    place = jnp.stack(
        [core_at, lax.axis_index("z").astype(jnp.int32), lax.axis_index("ylo").astype(jnp.int32)]
    )
    low_weight = jnp.concatenate([x_dt, x_bc, jnp.zeros((512, 96), BF16)], axis=1)
    history = jnp.pad(conv_state.astype(F32), ((0, 0), (5, 0), (0, 0)))
    routes_t = routes.T
    router_row = lax.dynamic_slice(router, (0, expert_at), (4096, 1)).astype(F32).reshape(1, 4096)

    rows_mine, rows_send = norm_split(place, x_rows, norm1_gain.reshape(1, 4096))
    pair_own = swap_pair(rows_send)
    x_below, x_above = from_below(in_x), from_above(in_x)
    x_halves = (x_below[:256], x_above[256:])
    x_blocks = gather_ring(in_x, x_below, x_above, x_halves)
    pair_other = swap_core(after(pair_own, *x_halves))
    z_block = lax.all_gather(after(in_z, *x_halves), "z", axis=0, tiled=True)
    out_block = after(out_w, pair_other, *x_halves)
    out_below, out_above = from_below(out_block), from_above(out_block)
    out_pair = swap_pair(after(out_w, pair_own))
    x_far = swap_pair(pair_product(place, pair_own, pair_other, x_blocks))
    sends = second_round(out_below, out_above, out_pair)
    x_near = after(own_product(place, rows_mine, x_blocks), *sends)
    conv, low = conv_project(
        core, x_near, x_far, history, conv_w, conv_b.reshape(1, 512), low_weight
    )
    low_pair = add_half(low[0], swap_core(low[1]))
    low_four = add_half(low_pair, lax.ppermute(low_pair, "x", [(i, i ^ 1) for i in range(4)]))
    low_line = add_half(low_four, lax.ppermute(low_four, "x", [(i, i ^ 2) for i in range(4)]))
    up, down, over = from_below(sends[0]), from_above(sends[1]), swap_pair(sends[2])
    low_own = add_half(low_line, swap_far(low_line))
    low_other = swap_core(low_own)
    mixed, final = scan_block(
        core,
        lengths,
        low_own,
        low_other,
        conv,
        dt_proj,
        dt_bias.reshape(1, 512),
        decay_rate,
        skip.reshape(1, 512),
        ssm_state,
    )
    z_far = swap_pair(pair_product(place, pair_own, pair_other, z_block))
    corner = third_round(up, down, over)
    z_near = own_product(place, rows_mine, z_block)
    out_blocks = (out_w, out_below, out_above, out_pair, up, down, over) + corner
    mixer_own, mixer_other = mixer_product(place, mixed, z_near, z_far, out_blocks)
    mixer_pair = (mixer_own.astype(F32) + swap_core(mixer_other).astype(F32)).astype(BF16)
    mixer_parts = exchange(mixer_pair.reshape(8, 256, 256), CHIPS)
    places = block_places(
        core_at, lax.axis_index("x").astype(jnp.int32), lax.axis_index("yhi").astype(jnp.int32)
    )
    gain = norm2_gain.reshape(1, 4096)
    hidden, outgoing = hidden_dispatch(block, mixer_parts, x_rows, gain, routes_t)
    rows = exchange(outgoing.reshape(8, 96, 256), DP).reshape(768, 256)
    left, right, cross = from_left(rows), from_right(rows), swap_far(rows)
    near = (rows, left, right, cross)
    near_other = tuple(swap_core(value) for value in near)
    top, bottom = slice(0, 384), slice(384, 768)
    up = from_left(jnp.concatenate([left[top], cross[top]]))
    down = from_right(jnp.concatenate([right[bottom], cross[bottom]]))
    over = swap_far(jnp.concatenate([right[top], left[bottom]]))
    inverse = 1.0 / gain
    held = gate_up(places, 0, near + near_other, inverse, router_row, w_gate[0], w_up[0])
    up, down, over = (after(value, held[2]) for value in (up, down, over))
    two = jnp.concatenate([up[top], down[top]])
    cross_left = jnp.concatenate([up[bottom], over[bottom]])
    cross_right = jnp.concatenate([over[top], down[bottom]])
    cross_two = jnp.concatenate(
        [from_left(cross_left[0:256]), from_right(cross_right[256:512]), swap_far(two[512:768])]
    )
    far = (two, cross_left, cross_right, cross_two)
    far_other = tuple(swap_core(value) for value in far)
    active = gate_up(places, 4, far + far_other, inverse, router_row, w_gate[0], w_up[0], held)
    far_sent = swap_core(down_product(places, 12, active, w_down[0]))
    near_sent = swap_core(down_product(places, 8, active, w_down[0]))
    far_sum = down_product(places, 4, active, w_down[0], far_sent)
    corner = (
        from_left(far_sum[3, 0:256]),
        from_right(far_sum[3, 256:512]),
        swap_far(far_sum[3, 512:768]),
    )
    near_sum = down_product(places, 0, active, w_down[0], near_sent)
    up_send, down_send, cross_send = fold_far(far_sum, corner)
    to_left, to_right, to_row = fold_near(
        near_sum, from_left(up_send), from_right(down_send), swap_far(cross_send)
    )
    total = fold_own(near_sum, (from_left(to_right), from_right(to_left), swap_far(to_row)))
    back = exchange(total.reshape(8, 96, 256), DP).reshape(768, 256)
    out_own = spread(combine(hidden, back, routes_t))
    out_other = swap_core(out_own)
    return (assemble(core, out_own, out_other), final)


def solution(mesh):
    wide = Mesh(mesh.devices.reshape(4, 2, 2, 4, 2), ("z", "ylo", "yhi", "x", "core"))
    return jax.shard_map(
        per_device,
        mesh=wide,
        in_specs=(
            P(DP, None),
            P(DP),
            P(DP, None),
            P(DP, None, TENSOR),
            P(DP, None, TENSOR),
            P(),
            P(DP, TENSOR),
            P(DP, TENSOR),
            P(None, TENSOR),
            P(TENSOR),
            P(TENSOR, None),
            P(TENSOR, None),
            P(None, TENSOR),
            P(TENSOR),
            P(None, TENSOR),
            P(TENSOR),
            P(TENSOR, DP),
            P(),
            P(),
            P(DP, None, TENSOR),
            P(DP, None, TENSOR),
            P(DP, TENSOR, None),
        ),
        out_specs=(P(DP, None), P(DP, None, TENSOR)),
        check_vma=False,
    )
```

```python
import jax
import jax.numpy as jnp
from jax import lax
from jax.sharding import Mesh
from jax.sharding import PartitionSpec as P
from jax.experimental import pallas as pl
from jax.experimental.pallas import tpu as pltpu

F32 = jnp.float32
BF16 = jnp.bfloat16
DP = ("z", "ylo")
TENSOR = ("yhi", "x", "core")
CHIPS = ("yhi", "x")
EPS = 1e-05
LOG2E = 1.4426950408889634


def params(megabytes):
    return pltpu.CompilerParams(vmem_limit_bytes=megabytes << 20)


def call(
    body, scalars, grid, in_specs, out_specs, out_shape, scratch=(), cost=None, megabytes=24
):
    if cost is None:
        cost = pl.CostEstimate(flops=1 << 20, bytes_accessed=1 << 16, transcendentals=0)
    spec = pltpu.PrefetchScalarGridSpec(
        num_scalar_prefetch=len(scalars),
        grid=grid,
        in_specs=in_specs,
        out_specs=out_specs,
        scratch_shapes=scratch,
    )
    return pl.pallas_call(
        body, grid_spec=spec, out_shape=out_shape, compiler_params=params(megabytes), cost_estimate=cost
    )


def exchange(value, axes):
    return lax.all_to_all(value, axes, split_axis=0, concat_axis=0, tiled=True)


def spread(value):
    return exchange(jnp.broadcast_to(value[None], (8,) + value.shape), CHIPS)


def from_left(value):
    return lax.ppermute(value, "x", [(i, (i + 1) % 4) for i in range(4)])


def from_right(value):
    return lax.ppermute(value, "x", [(i, (i - 1) % 4) for i in range(4)])


def swap_far(value):
    return lax.ppermute(value, "yhi", [(0, 1), (1, 0)])


def add_half(value, received):
    return (value.astype(F32) + received.astype(F32)).astype(BF16)


def swap_core(value):
    return lax.ppermute(value, "core", [(0, 1), (1, 0)])


def sigmoid(value):
    return 1.0 / (1.0 + jnp.exp(-value))


def silu(value):
    return value * sigmoid(value)


RING = (0, 3, 1, 2)


def from_below(value):
    return lax.ppermute(value, "z", [(i, (i + 1) % 4) for i in range(4)])


def from_above(value):
    return lax.ppermute(value, "z", [(i, (i - 1) % 4) for i in range(4)])


def after(value, *earlier):
    return lax.optimization_barrier((value,) + earlier)[0]


def swap_pair(value):
    return lax.ppermute(value, "ylo", [(0, 1), (1, 0)])


def gather_ring(block, below, above, halves):
    return block, below, above, from_below(halves[0]), from_above(halves[1])


def second_round(below, above, pair):
    return (
        jnp.concatenate([below[0:256], below[512:768], pair[0:256]]),
        jnp.concatenate([above[256:512], above[768:1024], pair[256:512]]),
        jnp.concatenate([above[512:768], below[768:1024]]),
    )


def third_round(up, down, over):
    return from_below(up[512:640]), from_above(over[128:256]), swap_pair(down[256:512])


def norm_split(place, x_rows, gain):
    def body(place_ref, x_ref, gain_ref, own_ref, send_ref):
        request = pl.ds(pl.multiple_of(place_ref[0] * 128, 128), 128)
        for rows, out_ref, member in (
            (slice(0, 256), own_ref, place_ref[2]),
            (request, send_ref, 1 - place_ref[2]),
        ):
            values = x_ref[rows, :].astype(F32)
            scale = lax.rsqrt(jnp.mean(values * values, axis=-1, keepdims=True) + EPS)
            for piece, shift in enumerate(RING):
                at = ((place_ref[1] + shift) % 4) * 2 + member
                columns = pl.ds(pl.multiple_of(at * 512, 512), 512)
                part = x_ref[rows, columns].astype(F32)
                out_ref[piece] = (part * scale * gain_ref[:, columns]).astype(BF16)

    return call(
        body,
        (place,),
        (1,),
        [
            pl.BlockSpec((256, 4096), lambda i, c: (0, 0)),
            pl.BlockSpec((1, 4096), lambda i, c: (0, 0)),
        ],
        [
            pl.BlockSpec((4, 256, 512), lambda i, c: (0, 0, 0)),
            pl.BlockSpec((4, 128, 512), lambda i, c: (0, 0, 0)),
        ],
        [
            jax.ShapeDtypeStruct((4, 256, 512), BF16),
            jax.ShapeDtypeStruct((4, 128, 512), BF16),
        ],
    )(place, x_rows, gain)


def ring_product(rows_ref, blocks):
    total = None
    for piece in range(3):
        term = jnp.dot(rows_ref[piece], blocks[piece][...], preferred_element_type=F32)
        total = term if total is None else total + term
    total = total + jnp.dot(rows_ref[3, :, 0:256], blocks[3][...], preferred_element_type=F32)
    return total + jnp.dot(rows_ref[3, :, 256:512], blocks[4][...], preferred_element_type=F32)


RING_SPECS = [pl.BlockSpec((512, 512), lambda *_: (0, 0))] * 3 + [
    pl.BlockSpec((256, 512), lambda *_: (0, 0))
] * 2


def pair_product(place, own, other, blocks):
    def body(place_ref, own_ref, other_ref, *refs):
        for slot, rows_ref in enumerate((own_ref, other_ref)):
            refs[5][place_ref[0] ^ slot] = ring_product(rows_ref, refs[:5]).astype(BF16)

    return call(
        body,
        (place,),
        (1,),
        [pl.BlockSpec((4, 128, 512), lambda i, c: (0, 0, 0))] * 2 + RING_SPECS,
        pl.BlockSpec((2, 128, 512), lambda i, c: (0, 0, 0)),
        jax.ShapeDtypeStruct((2, 128, 512), BF16),
    )(place, own, other, *blocks)


def own_product(rows, blocks):
    def body(rows_ref, *refs):
        refs[5][...] = ring_product(rows_ref, refs[:5]).reshape(2, 128, 512)

    return call(
        body,
        (),
        (1,),
        [pl.BlockSpec((4, 256, 512), lambda i: (0, 0, 0))] + RING_SPECS,
        pl.BlockSpec((2, 128, 512), lambda i: (0, 0, 0)),
        jax.ShapeDtypeStruct((2, 128, 512), F32),
    )(rows, *blocks)


def conv_project(core, near, far, history, conv_w, conv_b, weight):
    def body(core_ref, near_ref, far_ref, hist_ref, cw_ref, cb_ref, w_ref, conv_ref, low_ref, line):
        x_inner = (near_ref[0] + far_ref[0].astype(F32)).astype(BF16).astype(F32)
        line[0:8] = hist_ref[0]
        line[8:136] = x_inner
        total = cb_ref[...] + cw_ref[3:4] * x_inner
        for tap in range(3):
            total = total + cw_ref[tap : tap + 1] * line[5 + tap : 133 + tap]
        conv = silu(total).astype(BF16)
        conv_ref[0] = conv
        low_ref[0] = jnp.dot(conv, w_ref[...], preferred_element_type=F32).astype(BF16)

    return call(
        body,
        (core,),
        (2,),
        [
            pl.BlockSpec((1, 128, 512), lambda r, c: (r, 0, 0)),
            pl.BlockSpec((1, 128, 512), lambda r, c: (r, 0, 0)),
            pl.BlockSpec((1, 8, 512), lambda r, c: (r, 0, 0)),
            pl.BlockSpec((4, 512), lambda r, c: (0, 0)),
            pl.BlockSpec((1, 512), lambda r, c: (0, 0)),
            pl.BlockSpec((512, 640), lambda r, c: (0, 0)),
        ],
        [
            pl.BlockSpec((1, 128, 512), lambda r, c: (r, 0, 0)),
            pl.BlockSpec((1, 128, 640), lambda r, c: (r ^ c[0], 0, 0)),
        ],
        [
            jax.ShapeDtypeStruct((2, 128, 512), BF16),
            jax.ShapeDtypeStruct((2, 128, 640), BF16),
        ],
        (pltpu.VMEM((136, 512), F32),),
    )(core, near, far, history, conv_w, conv_b, weight)


def scan_block(
    core, lengths, low_own, low_other, conv, dt_proj, dt_bias, decay, skip, state
):
    def body(
        core_ref,
        len_ref,
        own_ref,
        other_ref,
        conv_ref,
        dtp_ref,
        dtb_ref,
        decay_ref,
        skip_ref,
        state_ref,
        mixed_ref,
        final_ref,
        step_s,
        drive_s,
        trail_s,
        dec_s,
    ):
        dec_s[...] = decay_ref[...] * (-LOG2E)
        lane = lax.broadcasted_iota(jnp.int32, (128, 128), 1)
        row = lax.broadcasted_iota(jnp.int32, (128, 128), 0)
        pick_entry = (row == lane % 16).astype(BF16)
        pick_read = (row == 16 + lane % 16).astype(BF16)
        diagonal = ((lane // 16) == (row % 8)).astype(F32)
        position = lax.broadcasted_iota(jnp.int32, (128, 512), 0)
        reads = []
        for slot, low_ref in enumerate((own_ref, other_ref)):
            request = core_ref[0] ^ slot
            mask = (position < len_ref[request]).astype(F32)
            raw = jnp.dot(low_ref[:, 0:512], dtp_ref[...], preferred_element_type=F32) + dtb_ref[...]
            step = (jnp.maximum(raw, 0.0) + jnp.log(1.0 + jnp.exp(-jnp.abs(raw)))) * mask
            step_s[slot] = step
            drive = (step * conv_ref[request].astype(F32)).astype(BF16)
            tail = low_ref[:, 512:640]
            entry = (jnp.dot(tail, pick_entry, preferred_element_type=F32) * diagonal).astype(BF16)
            reads.append(
                (jnp.dot(tail, pick_read, preferred_element_type=F32) * diagonal).astype(BF16)
            )
            for piece in range(8):
                for half in range(2):
                    at = piece * 16 + half * 8
                    keep = (
                        lax.broadcasted_iota(jnp.int32, (16, 128), 0) // 8 == half
                    ).astype(BF16)
                    drive_s[slot, at * 16 : at * 16 + 128] = lax.dot_general(
                        entry[piece * 16 : piece * 16 + 16] * keep,
                        drive[piece * 16 : piece * 16 + 16],
                        (((0,), (0,)), ((), ())),
                        preferred_element_type=F32,
                    )

        def advance(block, held):
            held = list(held)
            base = pl.multiple_of(block * 8, 8)
            for slot in range(2):
                steps = step_s[slot, pl.ds(base, 8)]
                now = held[slot]
                for offset in range(8):
                    rows = pl.ds(pl.multiple_of(block * 128 + offset * 16, 16), 16)
                    now = jnp.exp2(steps[offset : offset + 1] * dec_s[...]) * now + drive_s[slot, rows]
                    trail_s[slot, rows] = now.astype(BF16)
                held[slot] = now
            return tuple(held)

        first = tuple(state_ref[core_ref[0] ^ slot] for slot in range(2))
        last = lax.fori_loop(0, 16, advance, first)
        for slot in range(2):
            request = core_ref[0] ^ slot
            final_ref[request] = last[slot]
            outs = []
            for piece in range(16):
                outs.append(
                    jnp.dot(
                        reads[slot][piece * 8 : piece * 8 + 8],
                        trail_s[slot, piece * 128 : piece * 128 + 128],
                        preferred_element_type=F32,
                    )
                )
            mask = (position < len_ref[request]).astype(F32)
            mixed = jnp.concatenate(outs, axis=0) + skip_ref[...] * conv_ref[request].astype(F32)
            mixed_ref[request] = mixed * mask

    def whole(*shape):
        return pl.BlockSpec(shape, lambda i, c, n: (0,) * len(shape))

    return call(
        body,
        (core, lengths),
        (1,),
        [
            whole(128, 640),
            whole(128, 640),
            whole(2, 128, 512),
            whole(512, 512),
            whole(1, 512),
            whole(16, 512),
            whole(1, 512),
            whole(2, 16, 512),
        ],
        [whole(2, 128, 512), whole(2, 16, 512)],
        [
            jax.ShapeDtypeStruct((2, 128, 512), F32),
            jax.ShapeDtypeStruct((2, 16, 512), F32),
        ],
        (
            pltpu.VMEM((2, 128, 512), F32),
            pltpu.VMEM((2, 2048, 512), F32),
            pltpu.VMEM((2, 2048, 512), BF16),
            pltpu.VMEM((16, 512), F32),
        ),
    )(
        core,
        lengths,
        low_own,
        low_other,
        conv,
        dt_proj,
        dt_bias,
        decay,
        skip,
        state,
    )


def mixer_product(place, mixed, z_near, z_far, blocks):
    def body(place_ref, mixed_ref, near_ref, far_ref, *refs):
        own, below, above, pair, up_two, up_pair, down_two, down_pair, over, low, mid, high = refs[:12]
        own_ref, other_ref = refs[12:]
        z_gate = (near_ref[...] + far_ref[...].astype(F32)).astype(BF16).astype(F32)
        gated = (mixed_ref[...] * silu(z_gate)).astype(BF16).reshape(256, 512)

        def times(begin, end, value):
            return jnp.dot(gated[:, begin:end], value, preferred_element_type=F32)

        def split(top, bottom):
            return times(0, 256, top) + times(256, 512, bottom)

        sums = (
            lambda: times(0, 512, own[...]),
            lambda: times(0, 512, below[...]),
            lambda: times(0, 512, above[...]),
            lambda: split(up_two[...], down_two[...]),
            lambda: times(0, 512, pair[...]),
            lambda: split(up_pair[...], over[256:512]),
            lambda: split(over[0:256], down_pair[...]),
            lambda: times(0, 128, low[...]) + times(128, 256, mid[...]) + times(256, 512, high[...]),
        )
        for index, make in enumerate(sums):
            value = make().astype(BF16)
            part = ((place_ref[1] + RING[index % 4]) % 4) * 2 + (place_ref[2] ^ (index // 4))

            @pl.when(part // 4 == place_ref[0])
            def _():
                own_ref[part % 4, 0] = value[:, 0:256]
                own_ref[part % 4, 1] = value[:, 256:512]

            @pl.when(part // 4 != place_ref[0])
            def _():
                other_ref[part % 4, 0] = value[:, 0:256]
                other_ref[part % 4, 1] = value[:, 256:512]

    def whole(*shape):
        return pl.BlockSpec(shape, lambda i, c: (0,) * len(shape))

    def rows_at(count, index):
        return pl.BlockSpec((count, 512), lambda i, c: (index, 0))

    out_block, below, above, pair, up, down, over, low, mid, high = blocks
    return call(
        body,
        (place,),
        (1,),
        [whole(2, 128, 512)] * 3
        + [rows_at(512, 0), rows_at(512, 1), rows_at(512, 1), rows_at(512, 0)]
        + [rows_at(256, 1), rows_at(256, 2)] * 2
        + [rows_at(512, 0), rows_at(128, 0), rows_at(128, 0), rows_at(256, 0)],
        [whole(4, 2, 256, 256)] * 2,
        [jax.ShapeDtypeStruct((4, 2, 256, 256), BF16)] * 2,
    )(
        place,
        mixed,
        z_near,
        z_far,
        out_block,
        below,
        above,
        pair,
        up,
        up,
        down,
        down,
        over,
        low,
        mid,
        high,
    )


def tables_of(routes_t):
    expert = lax.broadcasted_iota(jnp.int32, (8, 256), 0)
    picks = [(expert == routes_t[k : k + 1]) for k in range(2)]
    counts = (picks[0] | picks[1]).astype(BF16)
    earlier = (
        lax.broadcasted_iota(jnp.int32, (256, 256), 0)
        < lax.broadcasted_iota(jnp.int32, (256, 256), 1)
    ).astype(BF16)
    before = jnp.dot(counts, earlier, preferred_element_type=F32)
    place = before + 96.0 * expert.astype(F32)
    slot_row = lax.broadcasted_iota(jnp.int32, (768, 256), 0)
    hit = None
    for pick in picks:
        slot = jnp.sum(jnp.where(pick, place, 0.0), axis=0, keepdims=True).astype(jnp.int32)
        mine = slot_row == slot
        hit = mine if hit is None else hit | mine
    return hit.astype(BF16)


def hidden_dispatch(block, parts, x_rows, gain, routes_t):
    def body(block_ref, parts_ref, x_ref, gain_ref, routes_ref, hidden_ref, out_ref):
        mixer = jnp.sum(parts_ref[...].astype(F32), axis=0)
        hidden = (x_ref[...].astype(F32) + mixer).astype(BF16)
        hidden_ref[...] = hidden
        scaled = (hidden.astype(F32) * gain_ref[...]).astype(BF16)
        out_ref[...] = jnp.dot(
            tables_of(routes_ref[...]), scaled, preferred_element_type=F32
        ).astype(BF16)

    return call(
        body,
        (block,),
        (1,),
        [
            pl.BlockSpec((8, 256, 256), lambda i, b: (0, 0, 0)),
            pl.BlockSpec((256, 256), lambda i, b: (0, b[0])),
            pl.BlockSpec((1, 256), lambda i, b: (0, b[0])),
            pl.BlockSpec((2, 256), lambda i, b: (0, 0)),
        ],
        [
            pl.BlockSpec((256, 256), lambda i, b: (0, 0)),
            pl.BlockSpec((768, 256), lambda i, b: (0, 0)),
        ],
        [
            jax.ShapeDtypeStruct((256, 256), BF16),
            jax.ShapeDtypeStruct((768, 256), BF16),
        ],
    )(block, parts, x_rows, gain, routes_t)


def block_places(core_at, x_at, far_at):
    near = [far_at * 4 + (x_at + step) % 4 for step in (0, 3, 1)]
    cross = [(1 - far_at) * 4 + (x_at + step) % 4 for step in (0, 3, 1, 2)]
    two = far_at * 4 + (x_at + 2) % 4
    order = near + cross[0:1] + [two] + cross[1:4]
    return jnp.stack([core_at * 8 + at for at in order] + [(1 - core_at) * 8 + at for at in order])


def gate_up(places, first, rows, inverse, router_row, w_gate, w_up, held=None):
    def body(places_ref, *refs):
        rows_refs, inverse_refs, router_refs = refs[0:8], refs[8:16], refs[16:24]
        gate_refs, up_refs = refs[24:32], refs[32:40]

        def stats():
            squares, logits = None, None
            for piece in range(8):
                value = rows_refs[piece][...].astype(F32)
                square = value * inverse_refs[piece][...]
                square = square * square
                square = square[:, 0:128] + square[:, 128:256]
                squares = square if squares is None else squares + square
                logit = value * router_refs[piece][...]
                logit = logit[:, 0:128] + logit[:, 128:256]
                logits = logit if logits is None else logits + logit
            return squares, logits

        gate_w = jnp.concatenate([ref[...] for ref in gate_refs], axis=0)
        up_w = jnp.concatenate([ref[...] for ref in up_refs], axis=0)
        if held is None:
            gate_out, up_out, squares_out, logits_out = refs[40:]

            @pl.when(pl.program_id(0) == 0)
            def _():
                squares_out[...], logits_out[...] = stats()

        else:
            gate_in, up_in, squares_in, logits_in, active_out, scale_s, weight_s = refs[40:]

            @pl.when(pl.program_id(0) == 0)
            def _():
                squares, logits = stats()
                squares = jnp.sum(squares_in[...] + squares, axis=1, keepdims=True)
                logits = jnp.sum(logits_in[...] + logits, axis=1, keepdims=True)
                scale = lax.rsqrt(squares * (1.0 / 4096.0) + EPS)
                scale_s[...] = jnp.broadcast_to(scale, (768, 128))
                weight_s[...] = jnp.broadcast_to(scale * sigmoid(logits * scale), (768, 128))

        for begin in range(0, 768, 256):
            at = slice(begin, begin + 256)
            units = jnp.concatenate([ref[at, :] for ref in rows_refs], axis=1)
            gate = jnp.dot(units, gate_w, preferred_element_type=F32)
            up = jnp.dot(units, up_w, preferred_element_type=F32)
            if held is None:
                gate_out[at, :] = gate
                up_out[at, :] = up
            else:
                gate = (gate + gate_in[at, :]) * scale_s[at, 0:1]
                up = (up + up_in[at, :]) * weight_s[at, 0:1]
                active_out[at, :] = (silu(gate) * up).astype(BF16)

    def at(piece):
        return first + piece % 4 + 8 * (piece // 4)

    def row_spec(piece):
        return pl.BlockSpec((1, 256), lambda n, p: (0, p[at(piece)]))

    def weight_spec(piece):
        return pl.BlockSpec((256, 256), lambda n, p: (p[at(piece)], n))

    def whole(*shape):
        return pl.BlockSpec(shape, lambda n, p: (0, 0))

    tile = pl.BlockSpec((768, 256), lambda n, p: (0, n))
    kept = [tile, tile, whole(768, 128), whole(768, 128)]
    if held is None:
        outs = kept
        shapes = [jax.ShapeDtypeStruct((768, 768), F32)] * 2 + [
            jax.ShapeDtypeStruct((768, 128), F32)
        ] * 2
    else:
        outs, shapes = tile, jax.ShapeDtypeStruct((768, 768), BF16)
    return call(
        body,
        (places,),
        (3,),
        [whole(768, 256)] * 8
        + [row_spec(piece) for piece in range(8)] * 2
        + [weight_spec(piece) for piece in range(8)] * 2
        + ([] if held is None else kept),
        outs,
        shapes,
        () if held is None else (pltpu.VMEM((768, 128), F32),) * 2,
        cost=pl.CostEstimate(flops=2 * 768 * 2048 * 1536, bytes_accessed=20 << 20, transcendentals=0),
        megabytes=48,
    )(
        places,
        *rows,
        *([inverse] * 8),
        *([router_row] * 8),
        *([w_gate] * 8),
        *([w_up] * 8),
        *(() if held is None else held),
    )


def down_product(places, first, active, w_down, received=None):
    def body(places_ref, rows_ref, *refs):
        out_ref = refs[-1]
        for side in range(2):
            value = jnp.dot(rows_ref[...], refs[side][...], preferred_element_type=F32)
            if received is not None:
                value = value + refs[2][side].astype(F32)
            out_ref[side] = value.astype(BF16)

    def weight_spec(side):
        return pl.BlockSpec((768, 256), lambda i, p: (0, p[first + 2 * i + side]))

    blocks = pl.BlockSpec((2, 768, 256), lambda i, p: (i, 0, 0))
    return call(
        body,
        (places,),
        (2,),
        [pl.BlockSpec((768, 768), lambda i, p: (0, 0)), weight_spec(0), weight_spec(1)]
        + ([] if received is None else [blocks]),
        blocks,
        jax.ShapeDtypeStruct((4, 768, 256), BF16),
        cost=pl.CostEstimate(flops=2 * 768 * 768 * 1024, bytes_accessed=5 << 20, transcendentals=0),
        megabytes=48,
    )(places, active, w_down, w_down, *(() if received is None else (received,)))


def whole_call(body, shapes, operands):
    def spec(shape):
        return pl.BlockSpec(shape, lambda i: (0,) * len(shape))

    outs = [jax.ShapeDtypeStruct(shape, BF16) for shape in shapes]
    return call(
        body,
        (),
        (1,),
        [spec(value.shape) for value in operands],
        [spec(shape) for shape in shapes],
        outs,
    )(*operands)


def fold_far(far, corner):
    def body(far_ref, low_ref, mid_ref, high_ref, up_ref, down_ref, cross_ref):
        def add(block, begin, end, ref, at):
            return (
                far_ref[block, begin:end].astype(F32) + ref[at : at + end - begin].astype(F32)
            ).astype(BF16)

        up_ref[0:384] = far_ref[0, 0:384]
        up_ref[384:640] = add(2, 0, 256, low_ref, 0)
        up_ref[640:768] = far_ref[2, 256:384]
        down_ref[0:128] = far_ref[0, 384:512]
        down_ref[128:384] = add(0, 512, 768, high_ref, 0)
        down_ref[384:512] = add(1, 384, 512, mid_ref, 128)
        down_ref[512:768] = far_ref[1, 512:768]
        cross_ref[0:384] = far_ref[2, 384:768]
        cross_ref[384:640] = far_ref[1, 0:256]
        cross_ref[640:768] = add(1, 256, 384, mid_ref, 0)

    return whole_call(body, [(768, 256)] * 3, (far,) + corner)


def fold_near(near, up, down, cross):
    def body(near_ref, up_ref, down_ref, cross_ref, left_ref, right_ref, row_ref):
        for out_ref, block, top, bottom in (
            (right_ref, 2, up_ref[0:384], cross_ref[0:384]),
            (left_ref, 1, cross_ref[384:768], down_ref[0:384]),
            (row_ref, 3, up_ref[384:768], down_ref[384:768]),
        ):
            out_ref[0:384] = (near_ref[block, 0:384].astype(F32) + top.astype(F32)).astype(BF16)
            out_ref[384:768] = (near_ref[block, 384:768].astype(F32) + bottom.astype(F32)).astype(
                BF16
            )

    return whole_call(body, [(768, 256)] * 3, (near, up, down, cross))


def fold_own(near, parts):
    def body(near_ref, a_ref, b_ref, c_ref, out_ref):
        total = near_ref[0].astype(F32) + a_ref[...].astype(F32)
        out_ref[...] = (total + b_ref[...].astype(F32) + c_ref[...].astype(F32)).astype(BF16)

    return whole_call(body, [(768, 256)], (near,) + parts)[0]


def combine(hidden, back, routes_t):
    def body(hidden_ref, back_ref, routes_ref, out_ref):
        mixed = lax.dot_general(
            tables_of(routes_ref[...]),
            back_ref[...],
            (((0,), (0,)), ((), ())),
            preferred_element_type=F32,
        )
        out_ref[...] = (hidden_ref[...].astype(F32) + mixed).astype(BF16)

    return call(
        body,
        (),
        (1,),
        [
            pl.BlockSpec((256, 256), lambda i: (0, 0)),
            pl.BlockSpec((768, 256), lambda i: (0, 0)),
            pl.BlockSpec((2, 256), lambda i: (0, 0)),
        ],
        pl.BlockSpec((256, 256), lambda i: (0, 0)),
        jax.ShapeDtypeStruct((256, 256), BF16),
    )(hidden, back, routes_t)


def assemble(core, own, other):
    def body(core_ref, own_ref, other_ref, out_ref):
        for side, ref in enumerate((own_ref, other_ref)):

            @pl.when(pl.program_id(0) == side)
            def _():
                for piece in range(4):
                    out_ref[:, piece * 256 : piece * 256 + 256] = ref[piece]

    return call(
        body,
        (core,),
        (2, 2),
        [
            pl.BlockSpec((4, 256, 256), lambda s, i, c: (jnp.where(s == 0, i, 1), 0, 0)),
            pl.BlockSpec((4, 256, 256), lambda s, i, c: (jnp.where(s == 0, 0, i), 0, 0)),
        ],
        pl.BlockSpec((256, 1024), lambda s, i, c: (0, (c[0] ^ s) * 2 + i)),
        jax.ShapeDtypeStruct((256, 4096), BF16),
    )(core, own, other)


def per_device(
    x_rows,
    lengths,
    routes,
    conv_state,
    ssm_state,
    norm1_gain,
    in_x,
    in_z,
    conv_w,
    conv_b,
    x_dt,
    x_bc,
    dt_proj,
    dt_bias,
    decay_rate,
    skip,
    out_w,
    norm2_gain,
    router,
    w_gate,
    w_up,
    w_down,
):
    core_at = lax.axis_index("core").astype(jnp.int32)
    core = core_at.reshape(1)
    chip_at = lax.axis_index(CHIPS).astype(jnp.int32)
    block = (core_at * 8 + chip_at).reshape(1)
    expert_at = lax.axis_index(DP).astype(jnp.int32)

    place = jnp.stack(
        [core_at, lax.axis_index("z").astype(jnp.int32), lax.axis_index("ylo").astype(jnp.int32)]
    )
    low_weight = jnp.concatenate([x_dt, x_bc, jnp.zeros((512, 96), BF16)], axis=1)
    history = jnp.pad(conv_state.astype(F32), ((0, 0), (5, 0), (0, 0)))
    routes_t = routes.T
    router_row = lax.dynamic_slice(router, (0, expert_at), (4096, 1)).astype(F32).reshape(1, 4096)

    rows_mine, rows_send = norm_split(place, x_rows, norm1_gain.reshape(1, 4096))
    pair_own = swap_pair(rows_send)
    x_below, x_above = from_below(in_x), from_above(in_x)
    x_halves = (x_below[:256], x_above[256:])
    x_blocks = gather_ring(in_x, x_below, x_above, x_halves)
    pair_other = swap_core(after(pair_own, *x_halves))
    both = after(jnp.concatenate([in_z, out_w]), pair_other, *x_blocks[3:5])
    both_below, both_above = from_below(both), from_above(both)
    out_pair = swap_pair(after(out_w, pair_own))
    x_far = swap_pair(pair_product(place, pair_own, pair_other, x_blocks))
    sends = second_round(both_below, both_above, out_pair)
    x_near = own_product(rows_mine, x_blocks)
    conv, low = conv_project(
        core, x_near, x_far, history, conv_w, conv_b.reshape(1, 512), low_weight
    )
    low_pair = add_half(low[0], swap_core(low[1]))
    low_pair = after(low_pair, *sends)
    low_four = add_half(low_pair, lax.ppermute(low_pair, "x", [(i, i ^ 1) for i in range(4)]))
    low_line = add_half(low_four, lax.ppermute(low_four, "x", [(i, i ^ 2) for i in range(4)]))
    up, down, over = from_below(sends[0]), from_above(sends[1]), swap_pair(sends[2])
    low_own = add_half(low_line, swap_far(low_line))
    low_other = swap_core(low_own)
    mixed, final = scan_block(
        core,
        lengths,
        low_own,
        low_other,
        conv,
        dt_proj,
        dt_bias.reshape(1, 512),
        decay_rate,
        skip.reshape(1, 512),
        ssm_state,
    )
    z_blocks = (in_z, both_below, both_above, up, down)
    z_far = swap_pair(pair_product(place, pair_own, pair_other, z_blocks))
    corner = third_round(up, down, over)
    z_near = own_product(rows_mine, z_blocks)
    out_blocks = (out_w, both_below, both_above, out_pair, up, down, over) + corner
    mixer_own, mixer_other = mixer_product(place, mixed, z_near, z_far, out_blocks)
    mixer_pair = (mixer_own.astype(F32) + swap_core(mixer_other).astype(F32)).astype(BF16)
    mixer_parts = exchange(mixer_pair.reshape(8, 256, 256), CHIPS)
    places = block_places(
        core_at, lax.axis_index("x").astype(jnp.int32), lax.axis_index("yhi").astype(jnp.int32)
    )
    gain = norm2_gain.reshape(1, 4096)
    hidden, outgoing = hidden_dispatch(block, mixer_parts, x_rows, gain, routes_t)
    rows = exchange(outgoing.reshape(8, 96, 256), DP).reshape(768, 256)
    left, right, cross = from_left(rows), from_right(rows), swap_far(rows)
    near = (rows, left, right, cross)
    near_other = tuple(swap_core(value) for value in near)
    top, bottom = slice(0, 384), slice(384, 768)
    up = from_left(jnp.concatenate([left[top], cross[top]]))
    down = from_right(jnp.concatenate([right[bottom], cross[bottom]]))
    over = swap_far(jnp.concatenate([right[top], left[bottom]]))
    inverse = 1.0 / gain
    held = gate_up(places, 0, near + near_other, inverse, router_row, w_gate[0], w_up[0])
    up, down, over = (after(value, held[2]) for value in (up, down, over))
    two = jnp.concatenate([up[top], down[top]])
    cross_left = jnp.concatenate([up[bottom], over[bottom]])
    cross_right = jnp.concatenate([over[top], down[bottom]])
    cross_two = jnp.concatenate(
        [from_left(cross_left[0:256]), from_right(cross_right[256:512]), swap_far(two[512:768])]
    )
    far = (two, cross_left, cross_right, cross_two)
    far_other = tuple(swap_core(value) for value in far)
    active = gate_up(places, 4, far + far_other, inverse, router_row, w_gate[0], w_up[0], held)
    far_sent = swap_core(down_product(places, 12, active, w_down[0]))
    near_sent = swap_core(down_product(places, 8, active, w_down[0]))
    far_sum = down_product(places, 4, active, w_down[0], far_sent)
    corner = (
        from_left(far_sum[3, 0:256]),
        from_right(far_sum[3, 256:512]),
        swap_far(far_sum[3, 512:768]),
    )
    near_sum = down_product(places, 0, active, w_down[0], near_sent)
    up_send, down_send, cross_send = fold_far(far_sum, corner)
    to_left, to_right, to_row = fold_near(
        near_sum, from_left(up_send), from_right(down_send), swap_far(cross_send)
    )
    total = fold_own(near_sum, (from_left(to_right), from_right(to_left), swap_far(to_row)))
    back = exchange(total.reshape(8, 96, 256), DP).reshape(768, 256)
    out_own = spread(combine(hidden, back, routes_t))
    out_other = swap_core(out_own)
    return (assemble(core, out_own, out_other), final)


def solution(mesh):
    wide = Mesh(mesh.devices.reshape(4, 2, 2, 4, 2), ("z", "ylo", "yhi", "x", "core"))
    return jax.shard_map(
        per_device,
        mesh=wide,
        in_specs=(
            P(DP, None),
            P(DP),
            P(DP, None),
            P(DP, None, TENSOR),
            P(DP, None, TENSOR),
            P(),
            P(DP, TENSOR),
            P(DP, TENSOR),
            P(None, TENSOR),
            P(TENSOR),
            P(TENSOR, None),
            P(TENSOR, None),
            P(None, TENSOR),
            P(TENSOR),
            P(None, TENSOR),
            P(TENSOR),
            P(TENSOR, DP),
            P(),
            P(),
            P(DP, None, TENSOR),
            P(DP, None, TENSOR),
            P(DP, TENSOR, None),
        ),
        out_specs=(P(DP, None), P(DP, None, TENSOR)),
        check_vma=False,
    )
```

```python
import jax
import jax.numpy as jnp
from jax import lax
from jax.sharding import Mesh
from jax.sharding import PartitionSpec as P
from jax.experimental import pallas as pl
from jax.experimental.pallas import tpu as pltpu

F32 = jnp.float32
BF16 = jnp.bfloat16
DP = ("z", "ylo")
TENSOR = ("yhi", "x", "core")
CHIPS = ("yhi", "x")
EPS = 1e-05
LOG2E = 1.4426950408889634


def params(megabytes):
    return pltpu.CompilerParams(vmem_limit_bytes=megabytes << 20)


def call(
    body, scalars, grid, in_specs, out_specs, out_shape, scratch=(), cost=None, megabytes=24
):
    if cost is None:
        cost = pl.CostEstimate(flops=1 << 20, bytes_accessed=1 << 16, transcendentals=0)
    spec = pltpu.PrefetchScalarGridSpec(
        num_scalar_prefetch=len(scalars),
        grid=grid,
        in_specs=in_specs,
        out_specs=out_specs,
        scratch_shapes=scratch,
    )
    return pl.pallas_call(
        body, grid_spec=spec, out_shape=out_shape, compiler_params=params(megabytes), cost_estimate=cost
    )


def exchange(value, axes):
    return lax.all_to_all(value, axes, split_axis=0, concat_axis=0, tiled=True)


def spread(value):
    return exchange(jnp.broadcast_to(value[None], (8,) + value.shape), CHIPS)


def from_left(value):
    return lax.ppermute(value, "x", [(i, (i + 1) % 4) for i in range(4)])


def from_right(value):
    return lax.ppermute(value, "x", [(i, (i - 1) % 4) for i in range(4)])


def swap_far(value):
    return lax.ppermute(value, "yhi", [(0, 1), (1, 0)])


def add_half(value, received):
    return (value.astype(F32) + received.astype(F32)).astype(BF16)


def swap_core(value):
    return lax.ppermute(value, "core", [(0, 1), (1, 0)])


def sigmoid(value):
    return 1.0 / (1.0 + jnp.exp(-value))


def silu(value):
    return value * sigmoid(value)


RING = (0, 3, 1, 2)


def from_below(value):
    return lax.ppermute(value, "z", [(i, (i + 1) % 4) for i in range(4)])


def from_above(value):
    return lax.ppermute(value, "z", [(i, (i - 1) % 4) for i in range(4)])


def after(value, *earlier):
    return lax.optimization_barrier((value,) + earlier)[0]


def swap_pair(value):
    return lax.ppermute(value, "ylo", [(0, 1), (1, 0)])


def gather_ring(block, below, above, halves):
    return block, below, above, from_below(halves[0]), from_above(halves[1])


def second_round(below, above, pair):
    return (
        jnp.concatenate([below[0:256], below[512:768], pair[0:256]]),
        jnp.concatenate([above[256:512], above[768:1024], pair[256:512]]),
        jnp.concatenate([above[512:768], below[768:1024]]),
    )


def third_round(up, down, over):
    return from_below(up[512:640]), from_above(over[128:256]), swap_pair(down[256:512])


def norm_split(place, x_rows, gain):
    def body(place_ref, x_ref, gain_ref, own_ref, send_ref):
        request = pl.ds(pl.multiple_of(place_ref[0] * 128, 128), 128)
        for rows, out_ref, member in (
            (slice(0, 256), own_ref, place_ref[2]),
            (request, send_ref, 1 - place_ref[2]),
        ):
            values = x_ref[rows, :].astype(F32)
            scale = lax.rsqrt(jnp.mean(values * values, axis=-1, keepdims=True) + EPS)
            for piece, shift in enumerate(RING):
                at = ((place_ref[1] + shift) % 4) * 2 + member
                columns = pl.ds(pl.multiple_of(at * 512, 512), 512)
                part = x_ref[rows, columns].astype(F32)
                out_ref[piece] = (part * scale * gain_ref[:, columns]).astype(BF16)

    return call(
        body,
        (place,),
        (1,),
        [
            pl.BlockSpec((256, 4096), lambda i, c: (0, 0)),
            pl.BlockSpec((1, 4096), lambda i, c: (0, 0)),
        ],
        [
            pl.BlockSpec((4, 256, 512), lambda i, c: (0, 0, 0)),
            pl.BlockSpec((4, 128, 512), lambda i, c: (0, 0, 0)),
        ],
        [
            jax.ShapeDtypeStruct((4, 256, 512), BF16),
            jax.ShapeDtypeStruct((4, 128, 512), BF16),
        ],
    )(place, x_rows, gain)


def ring_product(rows_ref, blocks):
    total = None
    for piece in range(3):
        term = jnp.dot(rows_ref[piece], blocks[piece][...], preferred_element_type=F32)
        total = term if total is None else total + term
    total = total + jnp.dot(rows_ref[3, :, 0:256], blocks[3][...], preferred_element_type=F32)
    return total + jnp.dot(rows_ref[3, :, 256:512], blocks[4][...], preferred_element_type=F32)


RING_SPECS = [pl.BlockSpec((512, 512), lambda *_: (0, 0))] * 3 + [
    pl.BlockSpec((256, 512), lambda *_: (0, 0))
] * 2


def pair_product(place, own, other, blocks):
    def body(place_ref, own_ref, other_ref, *refs):
        for slot, rows_ref in enumerate((own_ref, other_ref)):
            refs[5][place_ref[0] ^ slot] = ring_product(rows_ref, refs[:5]).astype(BF16)

    return call(
        body,
        (place,),
        (1,),
        [pl.BlockSpec((4, 128, 512), lambda i, c: (0, 0, 0))] * 2 + RING_SPECS,
        pl.BlockSpec((2, 128, 512), lambda i, c: (0, 0, 0)),
        jax.ShapeDtypeStruct((2, 128, 512), BF16),
    )(place, own, other, *blocks)


def own_product(rows, blocks):
    def body(rows_ref, *refs):
        refs[5][...] = ring_product(rows_ref, refs[:5]).reshape(2, 128, 512)

    return call(
        body,
        (),
        (1,),
        [pl.BlockSpec((4, 256, 512), lambda i: (0, 0, 0))] + RING_SPECS,
        pl.BlockSpec((2, 128, 512), lambda i: (0, 0, 0)),
        jax.ShapeDtypeStruct((2, 128, 512), F32),
    )(rows, *blocks)


def conv_project(core, near, far, history, conv_w, conv_b, weight):
    def body(core_ref, near_ref, far_ref, hist_ref, cw_ref, cb_ref, w_ref, conv_ref, low_ref, line):
        x_inner = (near_ref[0] + far_ref[0].astype(F32)).astype(BF16).astype(F32)
        line[0:8] = hist_ref[0]
        line[8:136] = x_inner
        total = cb_ref[...] + cw_ref[3:4] * x_inner
        for tap in range(3):
            total = total + cw_ref[tap : tap + 1] * line[5 + tap : 133 + tap]
        conv = silu(total).astype(BF16)
        conv_ref[0] = conv
        low_ref[0] = jnp.dot(conv, w_ref[...], preferred_element_type=F32).astype(BF16)

    return call(
        body,
        (core,),
        (2,),
        [
            pl.BlockSpec((1, 128, 512), lambda r, c: (r, 0, 0)),
            pl.BlockSpec((1, 128, 512), lambda r, c: (r, 0, 0)),
            pl.BlockSpec((1, 8, 512), lambda r, c: (r, 0, 0)),
            pl.BlockSpec((4, 512), lambda r, c: (0, 0)),
            pl.BlockSpec((1, 512), lambda r, c: (0, 0)),
            pl.BlockSpec((512, 640), lambda r, c: (0, 0)),
        ],
        [
            pl.BlockSpec((1, 128, 512), lambda r, c: (r, 0, 0)),
            pl.BlockSpec((1, 128, 640), lambda r, c: (r ^ c[0], 0, 0)),
        ],
        [
            jax.ShapeDtypeStruct((2, 128, 512), BF16),
            jax.ShapeDtypeStruct((2, 128, 640), BF16),
        ],
        (pltpu.VMEM((136, 512), F32),),
    )(core, near, far, history, conv_w, conv_b, weight)


def scan_block(
    core, lengths, low_own, low_other, conv, dt_proj, dt_bias, decay, skip, state
):
    def body(
        core_ref,
        len_ref,
        own_ref,
        other_ref,
        conv_ref,
        dtp_ref,
        dtb_ref,
        decay_ref,
        skip_ref,
        state_ref,
        mixed_ref,
        final_ref,
        step_s,
        drive_s,
        trail_s,
        dec_s,
    ):
        dec_s[...] = decay_ref[...] * (-LOG2E)
        lane = lax.broadcasted_iota(jnp.int32, (128, 128), 1)
        row = lax.broadcasted_iota(jnp.int32, (128, 128), 0)
        pick_entry = (row == lane % 16).astype(BF16)
        pick_read = (row == 16 + lane % 16).astype(BF16)
        diagonal = ((lane // 16) == (row % 8)).astype(F32)
        position = lax.broadcasted_iota(jnp.int32, (128, 512), 0)
        reads = []
        for slot, low_ref in enumerate((own_ref, other_ref)):
            request = core_ref[0] ^ slot
            mask = (position < len_ref[request]).astype(F32)
            raw = jnp.dot(low_ref[:, 0:512], dtp_ref[...], preferred_element_type=F32) + dtb_ref[...]
            step = (jnp.maximum(raw, 0.0) + jnp.log(1.0 + jnp.exp(-jnp.abs(raw)))) * mask
            step_s[slot] = step
            drive = (step * conv_ref[request].astype(F32)).astype(BF16)
            tail = low_ref[:, 512:640]
            entry = (jnp.dot(tail, pick_entry, preferred_element_type=F32) * diagonal).astype(BF16)
            reads.append(
                (jnp.dot(tail, pick_read, preferred_element_type=F32) * diagonal).astype(BF16)
            )
            for piece in range(8):
                for half in range(2):
                    at = piece * 16 + half * 8
                    keep = (
                        lax.broadcasted_iota(jnp.int32, (16, 128), 0) // 8 == half
                    ).astype(BF16)
                    drive_s[slot, at * 16 : at * 16 + 128] = lax.dot_general(
                        entry[piece * 16 : piece * 16 + 16] * keep,
                        drive[piece * 16 : piece * 16 + 16],
                        (((0,), (0,)), ((), ())),
                        preferred_element_type=F32,
                    )

        def advance(block, held):
            held = list(held)
            base = pl.multiple_of(block * 8, 8)
            for slot in range(2):
                steps = step_s[slot, pl.ds(base, 8)]
                now = held[slot]
                for offset in range(8):
                    rows = pl.ds(pl.multiple_of(block * 128 + offset * 16, 16), 16)
                    now = jnp.exp2(steps[offset : offset + 1] * dec_s[...]) * now + drive_s[slot, rows]
                    trail_s[slot, rows] = now.astype(BF16)
                held[slot] = now
            return tuple(held)

        first = tuple(state_ref[core_ref[0] ^ slot] for slot in range(2))
        last = lax.fori_loop(0, 16, advance, first)
        for slot in range(2):
            request = core_ref[0] ^ slot
            final_ref[request] = last[slot]
            outs = []
            for piece in range(16):
                outs.append(
                    jnp.dot(
                        reads[slot][piece * 8 : piece * 8 + 8],
                        trail_s[slot, piece * 128 : piece * 128 + 128],
                        preferred_element_type=F32,
                    )
                )
            mask = (position < len_ref[request]).astype(F32)
            mixed = jnp.concatenate(outs, axis=0) + skip_ref[...] * conv_ref[request].astype(F32)
            mixed_ref[request] = mixed * mask

    def whole(*shape):
        return pl.BlockSpec(shape, lambda i, c, n: (0,) * len(shape))

    return call(
        body,
        (core, lengths),
        (1,),
        [
            whole(128, 640),
            whole(128, 640),
            whole(2, 128, 512),
            whole(512, 512),
            whole(1, 512),
            whole(16, 512),
            whole(1, 512),
            whole(2, 16, 512),
        ],
        [whole(2, 128, 512), whole(2, 16, 512)],
        [
            jax.ShapeDtypeStruct((2, 128, 512), F32),
            jax.ShapeDtypeStruct((2, 16, 512), F32),
        ],
        (
            pltpu.VMEM((2, 128, 512), F32),
            pltpu.VMEM((2, 2048, 512), F32),
            pltpu.VMEM((2, 2048, 512), BF16),
            pltpu.VMEM((16, 512), F32),
        ),
    )(
        core,
        lengths,
        low_own,
        low_other,
        conv,
        dt_proj,
        dt_bias,
        decay,
        skip,
        state,
    )


def mixer_product(place, mixed, z_near, z_far, blocks):
    def body(place_ref, mixed_ref, near_ref, far_ref, *refs):
        own, below, above, pair, up_two, up_pair, down_two, down_pair, over, low, mid, high = refs[:12]
        own_ref, other_ref = refs[12:]
        z_gate = (near_ref[...] + far_ref[...].astype(F32)).astype(BF16).astype(F32)
        gated = (mixed_ref[...] * silu(z_gate)).astype(BF16).reshape(256, 512)

        def times(begin, end, value):
            return jnp.dot(gated[:, begin:end], value, preferred_element_type=F32)

        def split(top, bottom):
            return times(0, 256, top) + times(256, 512, bottom)

        sums = (
            lambda: times(0, 512, own[...]),
            lambda: times(0, 512, below[...]),
            lambda: times(0, 512, above[...]),
            lambda: split(up_two[...], down_two[...]),
            lambda: times(0, 512, pair[...]),
            lambda: split(up_pair[...], over[256:512]),
            lambda: split(over[0:256], down_pair[...]),
            lambda: times(0, 128, low[...]) + times(128, 256, mid[...]) + times(256, 512, high[...]),
        )
        for index, make in enumerate(sums):
            value = make().astype(BF16)
            part = ((place_ref[1] + RING[index % 4]) % 4) * 2 + (place_ref[2] ^ (index // 4))

            @pl.when(part // 4 == place_ref[0])
            def _():
                own_ref[part % 4, 0] = value[:, 0:256]
                own_ref[part % 4, 1] = value[:, 256:512]

            @pl.when(part // 4 != place_ref[0])
            def _():
                other_ref[part % 4, 0] = value[:, 0:256]
                other_ref[part % 4, 1] = value[:, 256:512]

    def whole(*shape):
        return pl.BlockSpec(shape, lambda i, c: (0,) * len(shape))

    def rows_at(count, index):
        return pl.BlockSpec((count, 512), lambda i, c: (index, 0))

    out_block, below, above, pair, up, down, over, low, mid, high = blocks
    return call(
        body,
        (place,),
        (1,),
        [whole(2, 128, 512)] * 3
        + [rows_at(512, 0), rows_at(512, 1), rows_at(512, 1), rows_at(512, 0)]
        + [rows_at(256, 1), rows_at(256, 2)] * 2
        + [rows_at(512, 0), rows_at(128, 0), rows_at(128, 0), rows_at(256, 0)],
        [whole(4, 2, 256, 256)] * 2,
        [jax.ShapeDtypeStruct((4, 2, 256, 256), BF16)] * 2,
    )(
        place,
        mixed,
        z_near,
        z_far,
        out_block,
        below,
        above,
        pair,
        up,
        up,
        down,
        down,
        over,
        low,
        mid,
        high,
    )


def tables_of(routes_t):
    expert = lax.broadcasted_iota(jnp.int32, (8, 256), 0)
    picks = [(expert == routes_t[k : k + 1]) for k in range(2)]
    counts = (picks[0] | picks[1]).astype(BF16)
    earlier = (
        lax.broadcasted_iota(jnp.int32, (256, 256), 0)
        < lax.broadcasted_iota(jnp.int32, (256, 256), 1)
    ).astype(BF16)
    before = jnp.dot(counts, earlier, preferred_element_type=F32)
    place = before + 96.0 * expert.astype(F32)
    slot_row = lax.broadcasted_iota(jnp.int32, (768, 256), 0)
    hit = None
    for pick in picks:
        slot = jnp.sum(jnp.where(pick, place, 0.0), axis=0, keepdims=True).astype(jnp.int32)
        mine = slot_row == slot
        hit = mine if hit is None else hit | mine
    return hit.astype(BF16)


def hidden_dispatch(block, parts, x_rows, gain, routes_t):
    def body(block_ref, parts_ref, x_ref, gain_ref, routes_ref, hidden_ref, out_ref):
        mixer = jnp.sum(parts_ref[...].astype(F32), axis=0)
        hidden = (x_ref[...].astype(F32) + mixer).astype(BF16)
        hidden_ref[...] = hidden
        scaled = (hidden.astype(F32) * gain_ref[...]).astype(BF16)
        out_ref[...] = jnp.dot(
            tables_of(routes_ref[...]), scaled, preferred_element_type=F32
        ).astype(BF16)

    return call(
        body,
        (block,),
        (1,),
        [
            pl.BlockSpec((8, 256, 256), lambda i, b: (0, 0, 0)),
            pl.BlockSpec((256, 256), lambda i, b: (0, b[0])),
            pl.BlockSpec((1, 256), lambda i, b: (0, b[0])),
            pl.BlockSpec((2, 256), lambda i, b: (0, 0)),
        ],
        [
            pl.BlockSpec((256, 256), lambda i, b: (0, 0)),
            pl.BlockSpec((768, 256), lambda i, b: (0, 0)),
        ],
        [
            jax.ShapeDtypeStruct((256, 256), BF16),
            jax.ShapeDtypeStruct((768, 256), BF16),
        ],
    )(block, parts, x_rows, gain, routes_t)


def block_places(core_at, x_at, far_at):
    near = [far_at * 4 + (x_at + step) % 4 for step in (0, 3, 1)]
    cross = [(1 - far_at) * 4 + (x_at + step) % 4 for step in (0, 3, 1, 2)]
    two = far_at * 4 + (x_at + 2) % 4
    order = near + cross[0:1] + [two] + cross[1:4]
    return jnp.stack([core_at * 8 + at for at in order] + [(1 - core_at) * 8 + at for at in order])


def gate_up(places, first, rows, inverse, router_row, w_gate, w_up, held=None):
    def body(places_ref, *refs):
        rows_refs, inverse_refs, router_refs = refs[0:8], refs[8:16], refs[16:24]
        gate_refs, up_refs = refs[24:32], refs[32:40]

        def stats():
            squares, logits = None, None
            for piece in range(8):
                value = rows_refs[piece][...].astype(F32)
                square = value * inverse_refs[piece][...]
                square = square * square
                square = square[:, 0:128] + square[:, 128:256]
                squares = square if squares is None else squares + square
                logit = value * router_refs[piece][...]
                logit = logit[:, 0:128] + logit[:, 128:256]
                logits = logit if logits is None else logits + logit
            return squares, logits

        gate_w = jnp.concatenate([ref[...] for ref in gate_refs], axis=0)
        up_w = jnp.concatenate([ref[...] for ref in up_refs], axis=0)
        if held is None:
            gate_out, up_out, squares_out, logits_out = refs[40:]

            @pl.when(pl.program_id(0) == 0)
            def _():
                squares_out[...], logits_out[...] = stats()

        else:
            gate_in, up_in, squares_in, logits_in, active_out, scale_s, weight_s = refs[40:]

            @pl.when(pl.program_id(0) == 0)
            def _():
                squares, logits = stats()
                squares = jnp.sum(squares_in[...] + squares, axis=1, keepdims=True)
                logits = jnp.sum(logits_in[...] + logits, axis=1, keepdims=True)
                scale = lax.rsqrt(squares * (1.0 / 4096.0) + EPS)
                scale_s[...] = jnp.broadcast_to(scale, (768, 128))
                weight_s[...] = jnp.broadcast_to(scale * sigmoid(logits * scale), (768, 128))

        for begin in range(0, 768, 256):
            at = slice(begin, begin + 256)
            units = jnp.concatenate([ref[at, :] for ref in rows_refs], axis=1)
            gate = jnp.dot(units, gate_w, preferred_element_type=F32)
            up = jnp.dot(units, up_w, preferred_element_type=F32)
            if held is None:
                gate_out[at, :] = gate
                up_out[at, :] = up
            else:
                gate = (gate + gate_in[at, :]) * scale_s[at, 0:1]
                up = (up + up_in[at, :]) * weight_s[at, 0:1]
                active_out[at, :] = (silu(gate) * up).astype(BF16)

    def at(piece):
        return first + piece % 4 + 8 * (piece // 4)

    def row_spec(piece):
        return pl.BlockSpec((1, 256), lambda n, p: (0, p[at(piece)]))

    def weight_spec(piece):
        return pl.BlockSpec((256, 256), lambda n, p: (p[at(piece)], n))

    def whole(*shape):
        return pl.BlockSpec(shape, lambda n, p: (0, 0))

    tile = pl.BlockSpec((768, 256), lambda n, p: (0, n))
    kept = [tile, tile, whole(768, 128), whole(768, 128)]
    if held is None:
        outs = kept
        shapes = [jax.ShapeDtypeStruct((768, 768), F32)] * 2 + [
            jax.ShapeDtypeStruct((768, 128), F32)
        ] * 2
    else:
        outs, shapes = tile, jax.ShapeDtypeStruct((768, 768), BF16)
    return call(
        body,
        (places,),
        (3,),
        [whole(768, 256)] * 8
        + [row_spec(piece) for piece in range(8)] * 2
        + [weight_spec(piece) for piece in range(8)] * 2
        + ([] if held is None else kept),
        outs,
        shapes,
        () if held is None else (pltpu.VMEM((768, 128), F32),) * 2,
        cost=pl.CostEstimate(flops=2 * 768 * 2048 * 1536, bytes_accessed=20 << 20, transcendentals=0),
        megabytes=40,
    )(
        places,
        *rows,
        *([inverse] * 8),
        *([router_row] * 8),
        *([w_gate] * 8),
        *([w_up] * 8),
        *(() if held is None else held),
    )


def down_product(places, first, active, w_down, received=None):
    def body(places_ref, rows_ref, *refs):
        out_ref = refs[-1]
        for side in range(2):
            value = jnp.dot(rows_ref[...], refs[side][...], preferred_element_type=F32)
            if received is not None:
                value = value + refs[2][side].astype(F32)
            out_ref[side] = value.astype(BF16)

    def weight_spec(side):
        return pl.BlockSpec((768, 256), lambda i, p: (0, p[first + 2 * i + side]))

    blocks = pl.BlockSpec((2, 768, 256), lambda i, p: (i, 0, 0))
    return call(
        body,
        (places,),
        (2,),
        [pl.BlockSpec((768, 768), lambda i, p: (0, 0)), weight_spec(0), weight_spec(1)]
        + ([] if received is None else [blocks]),
        blocks,
        jax.ShapeDtypeStruct((4, 768, 256), BF16),
        cost=pl.CostEstimate(flops=2 * 768 * 768 * 1024, bytes_accessed=5 << 20, transcendentals=0),
        megabytes=24,
    )(places, active, w_down, w_down, *(() if received is None else (received,)))


def whole_call(body, shapes, operands):
    def spec(shape):
        return pl.BlockSpec(shape, lambda i: (0,) * len(shape))

    outs = [jax.ShapeDtypeStruct(shape, BF16) for shape in shapes]
    return call(
        body,
        (),
        (1,),
        [spec(value.shape) for value in operands],
        [spec(shape) for shape in shapes],
        outs,
    )(*operands)


def fold_far(far, corner):
    def body(far_ref, low_ref, mid_ref, high_ref, up_ref, down_ref, cross_ref):
        def add(block, begin, end, ref, at):
            return (
                far_ref[block, begin:end].astype(F32) + ref[at : at + end - begin].astype(F32)
            ).astype(BF16)

        up_ref[0:384] = far_ref[0, 0:384]
        up_ref[384:640] = add(2, 0, 256, low_ref, 0)
        up_ref[640:768] = far_ref[2, 256:384]
        down_ref[0:128] = far_ref[0, 384:512]
        down_ref[128:384] = add(0, 512, 768, high_ref, 0)
        down_ref[384:512] = add(1, 384, 512, mid_ref, 128)
        down_ref[512:768] = far_ref[1, 512:768]
        cross_ref[0:384] = far_ref[2, 384:768]
        cross_ref[384:640] = far_ref[1, 0:256]
        cross_ref[640:768] = add(1, 256, 384, mid_ref, 0)

    return whole_call(body, [(768, 256)] * 3, (far,) + corner)


def fold_near(near, up, down, cross):
    def body(near_ref, up_ref, down_ref, cross_ref, left_ref, right_ref, row_ref):
        for out_ref, block, top, bottom in (
            (right_ref, 2, up_ref[0:384], cross_ref[0:384]),
            (left_ref, 1, cross_ref[384:768], down_ref[0:384]),
            (row_ref, 3, up_ref[384:768], down_ref[384:768]),
        ):
            out_ref[0:384] = (near_ref[block, 0:384].astype(F32) + top.astype(F32)).astype(BF16)
            out_ref[384:768] = (near_ref[block, 384:768].astype(F32) + bottom.astype(F32)).astype(
                BF16
            )

    return whole_call(body, [(768, 256)] * 3, (near, up, down, cross))


def fold_own(near, parts):
    def body(near_ref, a_ref, b_ref, c_ref, out_ref):
        total = near_ref[0].astype(F32) + a_ref[...].astype(F32)
        out_ref[...] = (total + b_ref[...].astype(F32) + c_ref[...].astype(F32)).astype(BF16)

    return whole_call(body, [(768, 256)], (near,) + parts)[0]


def combine(hidden, back, routes_t):
    def body(hidden_ref, back_ref, routes_ref, out_ref):
        mixed = lax.dot_general(
            tables_of(routes_ref[...]),
            back_ref[...],
            (((0,), (0,)), ((), ())),
            preferred_element_type=F32,
        )
        out_ref[...] = (hidden_ref[...].astype(F32) + mixed).astype(BF16)

    return call(
        body,
        (),
        (1,),
        [
            pl.BlockSpec((256, 256), lambda i: (0, 0)),
            pl.BlockSpec((768, 256), lambda i: (0, 0)),
            pl.BlockSpec((2, 256), lambda i: (0, 0)),
        ],
        pl.BlockSpec((256, 256), lambda i: (0, 0)),
        jax.ShapeDtypeStruct((256, 256), BF16),
    )(hidden, back, routes_t)


def assemble(core, own, other):
    def body(core_ref, own_ref, other_ref, out_ref):
        for side, ref in enumerate((own_ref, other_ref)):

            @pl.when(pl.program_id(0) == side)
            def _():
                for piece in range(4):
                    out_ref[:, piece * 256 : piece * 256 + 256] = ref[piece]

    return call(
        body,
        (core,),
        (2, 2),
        [
            pl.BlockSpec((4, 256, 256), lambda s, i, c: (jnp.where(s == 0, i, 1), 0, 0)),
            pl.BlockSpec((4, 256, 256), lambda s, i, c: (jnp.where(s == 0, 0, i), 0, 0)),
        ],
        pl.BlockSpec((256, 1024), lambda s, i, c: (0, (c[0] ^ s) * 2 + i)),
        jax.ShapeDtypeStruct((256, 4096), BF16),
    )(core, own, other)


def per_device(
    x_rows,
    lengths,
    routes,
    conv_state,
    ssm_state,
    norm1_gain,
    in_x,
    in_z,
    conv_w,
    conv_b,
    x_dt,
    x_bc,
    dt_proj,
    dt_bias,
    decay_rate,
    skip,
    out_w,
    norm2_gain,
    router,
    w_gate,
    w_up,
    w_down,
):
    core_at = lax.axis_index("core").astype(jnp.int32)
    core = core_at.reshape(1)
    chip_at = lax.axis_index(CHIPS).astype(jnp.int32)
    block = (core_at * 8 + chip_at).reshape(1)
    expert_at = lax.axis_index(DP).astype(jnp.int32)

    place = jnp.stack(
        [core_at, lax.axis_index("z").astype(jnp.int32), lax.axis_index("ylo").astype(jnp.int32)]
    )
    low_weight = jnp.concatenate([x_dt, x_bc, jnp.zeros((512, 96), BF16)], axis=1)
    history = jnp.pad(conv_state.astype(F32), ((0, 0), (5, 0), (0, 0)))
    routes_t = routes.T
    router_row = lax.dynamic_slice(router, (0, expert_at), (4096, 1)).astype(F32).reshape(1, 4096)

    rows_mine, rows_send = norm_split(place, x_rows, norm1_gain.reshape(1, 4096))
    pair_own = swap_pair(rows_send)
    x_below, x_above = from_below(in_x), from_above(in_x)
    x_halves = (x_below[:256], x_above[256:])
    x_blocks = gather_ring(in_x, x_below, x_above, x_halves)
    pair_other = swap_core(after(pair_own, *x_halves))
    both = after(jnp.concatenate([in_z, out_w]), pair_other, *x_blocks[3:5])
    both_below, both_above = from_below(both), from_above(both)
    out_pair = swap_pair(after(out_w, pair_own))
    x_far = swap_pair(pair_product(place, pair_own, pair_other, x_blocks))
    sends = second_round(both_below, both_above, out_pair)
    x_near = own_product(rows_mine, x_blocks)
    conv, low = conv_project(
        core, x_near, x_far, history, conv_w, conv_b.reshape(1, 512), low_weight
    )
    low_pair = add_half(low[0], swap_core(low[1]))
    inverse = 1.0 / norm2_gain.reshape(1, 4096)
    low_pair = after(low_pair, router_row, inverse, *sends)
    low_two = add_half(low_pair, swap_far(low_pair))
    low_four = add_half(low_two, lax.ppermute(low_two, "x", [(i, i ^ 1) for i in range(4)]))
    up, down, over = from_below(sends[0]), from_above(sends[1]), swap_pair(sends[2])
    low_own = add_half(low_four, lax.ppermute(low_four, "x", [(i, i ^ 2) for i in range(4)]))
    low_other = swap_core(low_own)
    mixed, final = scan_block(
        core,
        lengths,
        low_own,
        low_other,
        conv,
        dt_proj,
        dt_bias.reshape(1, 512),
        decay_rate,
        skip.reshape(1, 512),
        ssm_state,
    )
    z_blocks = (in_z, both_below, both_above, up, down)
    z_far = swap_pair(pair_product(place, pair_own, pair_other, z_blocks))
    corner = third_round(up, down, over)
    z_near = own_product(rows_mine, z_blocks)
    out_blocks = (out_w, both_below, both_above, out_pair, up, down, over) + corner
    mixer_own, mixer_other = mixer_product(place, mixed, z_near, z_far, out_blocks)
    mixer_pair = (mixer_own.astype(F32) + swap_core(mixer_other).astype(F32)).astype(BF16)
    mixer_parts = exchange(mixer_pair.reshape(8, 256, 256), CHIPS)
    places = block_places(
        core_at, lax.axis_index("x").astype(jnp.int32), lax.axis_index("yhi").astype(jnp.int32)
    )
    gain = norm2_gain.reshape(1, 4096)
    hidden, outgoing = hidden_dispatch(block, mixer_parts, x_rows, gain, routes_t)
    rows = exchange(outgoing.reshape(8, 96, 256), DP).reshape(768, 256)
    left, right, cross = from_left(rows), from_right(rows), swap_far(rows)
    near = (rows, left, right, cross)
    near_other = tuple(swap_core(value) for value in near)
    top, bottom = slice(0, 384), slice(384, 768)
    up = from_left(jnp.concatenate([left[top], cross[top]]))
    down = from_right(jnp.concatenate([right[bottom], cross[bottom]]))
    over = swap_far(jnp.concatenate([right[top], left[bottom]]))
    held = gate_up(places, 0, near + near_other, inverse, router_row, w_gate[0], w_up[0])
    up, down, over = (after(value, held[2]) for value in (up, down, over))
    two = jnp.concatenate([up[top], down[top]])
    cross_left = jnp.concatenate([up[bottom], over[bottom]])
    cross_right = jnp.concatenate([over[top], down[bottom]])
    cross_two = jnp.concatenate(
        [from_left(cross_left[0:256]), from_right(cross_right[256:512]), swap_far(two[512:768])]
    )
    far = (two, cross_left, cross_right, cross_two)
    far_other = tuple(swap_core(value) for value in far)
    active = gate_up(places, 4, far + far_other, inverse, router_row, w_gate[0], w_up[0], held)
    far_sent = swap_core(down_product(places, 12, active, w_down[0]))
    far_sum = add_half(down_product(places, 4, active, w_down[0]), far_sent)
    near_sent = swap_core(down_product(places, 8, after(active, far_sum), w_down[0]))
    corner = (
        from_left(far_sum[3, 0:256]),
        from_right(far_sum[3, 256:512]),
        swap_far(far_sum[3, 512:768]),
    )
    near_sum = down_product(places, 0, active, w_down[0], near_sent)
    up_send, down_send, cross_send = fold_far(far_sum, corner)
    to_left, to_right, to_row = fold_near(
        near_sum, from_left(up_send), from_right(down_send), swap_far(cross_send)
    )
    total = fold_own(near_sum, (from_left(to_right), from_right(to_left), swap_far(to_row)))
    back = exchange(total.reshape(8, 96, 256), DP).reshape(768, 256)
    out_own = spread(combine(hidden, back, routes_t))
    out_other = swap_core(out_own)
    return (assemble(core, out_own, out_other), final)


def solution(mesh):
    wide = Mesh(mesh.devices.reshape(4, 2, 2, 4, 2), ("z", "ylo", "yhi", "x", "core"))
    return jax.shard_map(
        per_device,
        mesh=wide,
        in_specs=(
            P(DP, None),
            P(DP),
            P(DP, None),
            P(DP, None, TENSOR),
            P(DP, None, TENSOR),
            P(),
            P(DP, TENSOR),
            P(DP, TENSOR),
            P(None, TENSOR),
            P(TENSOR),
            P(TENSOR, None),
            P(TENSOR, None),
            P(None, TENSOR),
            P(TENSOR),
            P(None, TENSOR),
            P(TENSOR),
            P(TENSOR, DP),
            P(),
            P(),
            P(DP, None, TENSOR),
            P(DP, None, TENSOR),
            P(DP, TENSOR, None),
        ),
        out_specs=(P(DP, None), P(DP, None, TENSOR)),
        check_vma=False,
    )
```

```python
import jax
import jax.numpy as jnp
from jax import lax
from jax.sharding import Mesh
from jax.sharding import PartitionSpec as P
from jax.experimental import pallas as pl
from jax.experimental.pallas import tpu as pltpu

F32 = jnp.float32
BF16 = jnp.bfloat16
DP = ("z", "ylo")
TENSOR = ("yhi", "x", "core")
CHIPS = ("yhi", "x")
EPS = 1e-05
LOG2E = 1.4426950408889634


def params(megabytes):
    return pltpu.CompilerParams(vmem_limit_bytes=megabytes << 20)


def call(
    body, scalars, grid, in_specs, out_specs, out_shape, scratch=(), cost=None, megabytes=24
):
    if cost is None:
        cost = pl.CostEstimate(flops=1 << 20, bytes_accessed=1 << 16, transcendentals=0)
    spec = pltpu.PrefetchScalarGridSpec(
        num_scalar_prefetch=len(scalars),
        grid=grid,
        in_specs=in_specs,
        out_specs=out_specs,
        scratch_shapes=scratch,
    )
    return pl.pallas_call(
        body, grid_spec=spec, out_shape=out_shape, compiler_params=params(megabytes), cost_estimate=cost
    )


def exchange(value, axes):
    return lax.all_to_all(value, axes, split_axis=0, concat_axis=0, tiled=True)


def spread(value):
    return exchange(jnp.broadcast_to(value[None], (8,) + value.shape), CHIPS)


def from_left(value):
    return lax.ppermute(value, "x", [(i, (i + 1) % 4) for i in range(4)])


def from_right(value):
    return lax.ppermute(value, "x", [(i, (i - 1) % 4) for i in range(4)])


def swap_far(value):
    return lax.ppermute(value, "yhi", [(0, 1), (1, 0)])


def add_half(value, received):
    return (value.astype(F32) + received.astype(F32)).astype(BF16)


def swap_core(value):
    return lax.ppermute(value, "core", [(0, 1), (1, 0)])


def sigmoid(value):
    return 1.0 / (1.0 + jnp.exp(-value))


def silu(value):
    return value * sigmoid(value)


RING = (0, 3, 1, 2)


def from_below(value):
    return lax.ppermute(value, "z", [(i, (i + 1) % 4) for i in range(4)])


def from_above(value):
    return lax.ppermute(value, "z", [(i, (i - 1) % 4) for i in range(4)])


def after(value, *earlier):
    return lax.optimization_barrier((value,) + earlier)[0]


def swap_pair(value):
    return lax.ppermute(value, "ylo", [(0, 1), (1, 0)])


def gather_ring(block, below, above, halves):
    return block, below, above, from_below(halves[0]), from_above(halves[1])


def second_round(below, above, pair):
    return (
        jnp.concatenate([below[0:256], below[512:768], pair[0:256]]),
        jnp.concatenate([above[256:512], above[768:1024], pair[256:512]]),
        jnp.concatenate([above[512:768], below[768:1024]]),
    )


def third_round(up, down, over):
    return from_below(up[512:640]), from_above(over[128:256]), swap_pair(down[256:512])


def norm_split(place, x_rows, gain):
    def body(place_ref, x_ref, gain_ref, own_ref, send_ref):
        request = pl.ds(pl.multiple_of(place_ref[0] * 128, 128), 128)
        for rows, out_ref, member in (
            (slice(0, 256), own_ref, place_ref[2]),
            (request, send_ref, 1 - place_ref[2]),
        ):
            values = x_ref[rows, :].astype(F32)
            scale = lax.rsqrt(jnp.mean(values * values, axis=-1, keepdims=True) + EPS)
            for piece, shift in enumerate(RING):
                at = ((place_ref[1] + shift) % 4) * 2 + member
                columns = pl.ds(pl.multiple_of(at * 512, 512), 512)
                part = x_ref[rows, columns].astype(F32)
                out_ref[piece] = (part * scale * gain_ref[:, columns]).astype(BF16)

    return call(
        body,
        (place,),
        (1,),
        [
            pl.BlockSpec((256, 4096), lambda i, c: (0, 0)),
            pl.BlockSpec((1, 4096), lambda i, c: (0, 0)),
        ],
        [
            pl.BlockSpec((4, 256, 512), lambda i, c: (0, 0, 0)),
            pl.BlockSpec((4, 128, 512), lambda i, c: (0, 0, 0)),
        ],
        [
            jax.ShapeDtypeStruct((4, 256, 512), BF16),
            jax.ShapeDtypeStruct((4, 128, 512), BF16),
        ],
    )(place, x_rows, gain)


def ring_product(rows_ref, blocks):
    total = None
    for piece in range(3):
        term = jnp.dot(rows_ref[piece], blocks[piece][...], preferred_element_type=F32)
        total = term if total is None else total + term
    total = total + jnp.dot(rows_ref[3, :, 0:256], blocks[3][...], preferred_element_type=F32)
    return total + jnp.dot(rows_ref[3, :, 256:512], blocks[4][...], preferred_element_type=F32)


RING_SPECS = [pl.BlockSpec((512, 512), lambda *_: (0, 0))] * 3 + [
    pl.BlockSpec((256, 512), lambda *_: (0, 0))
] * 2


def pair_product(place, own, other, blocks):
    def body(place_ref, own_ref, other_ref, *refs):
        for slot, rows_ref in enumerate((own_ref, other_ref)):
            refs[5][place_ref[0] ^ slot] = ring_product(rows_ref, refs[:5]).astype(BF16)

    return call(
        body,
        (place,),
        (1,),
        [pl.BlockSpec((4, 128, 512), lambda i, c: (0, 0, 0))] * 2 + RING_SPECS,
        pl.BlockSpec((2, 128, 512), lambda i, c: (0, 0, 0)),
        jax.ShapeDtypeStruct((2, 128, 512), BF16),
    )(place, own, other, *blocks)


def own_product(rows, blocks):
    def body(rows_ref, *refs):
        refs[5][...] = ring_product(rows_ref, refs[:5]).reshape(2, 128, 512)

    return call(
        body,
        (),
        (1,),
        [pl.BlockSpec((4, 256, 512), lambda i: (0, 0, 0))] + RING_SPECS,
        pl.BlockSpec((2, 128, 512), lambda i: (0, 0, 0)),
        jax.ShapeDtypeStruct((2, 128, 512), F32),
    )(rows, *blocks)


def conv_project(core, near, far, history, conv_w, conv_b, weight):
    def body(core_ref, near_ref, far_ref, hist_ref, cw_ref, cb_ref, w_ref, conv_ref, low_ref, line):
        x_inner = (near_ref[0] + far_ref[0].astype(F32)).astype(BF16).astype(F32)
        line[0:8] = hist_ref[0]
        line[8:136] = x_inner
        total = cb_ref[...] + cw_ref[3:4] * x_inner
        for tap in range(3):
            total = total + cw_ref[tap : tap + 1] * line[5 + tap : 133 + tap]
        conv = silu(total).astype(BF16)
        conv_ref[0] = conv
        low_ref[0] = jnp.dot(conv, w_ref[...], preferred_element_type=F32).astype(BF16)

    return call(
        body,
        (core,),
        (2,),
        [
            pl.BlockSpec((1, 128, 512), lambda r, c: (r, 0, 0)),
            pl.BlockSpec((1, 128, 512), lambda r, c: (r, 0, 0)),
            pl.BlockSpec((1, 8, 512), lambda r, c: (r, 0, 0)),
            pl.BlockSpec((4, 512), lambda r, c: (0, 0)),
            pl.BlockSpec((1, 512), lambda r, c: (0, 0)),
            pl.BlockSpec((512, 640), lambda r, c: (0, 0)),
        ],
        [
            pl.BlockSpec((1, 128, 512), lambda r, c: (r, 0, 0)),
            pl.BlockSpec((1, 128, 640), lambda r, c: (r ^ c[0], 0, 0)),
        ],
        [
            jax.ShapeDtypeStruct((2, 128, 512), BF16),
            jax.ShapeDtypeStruct((2, 128, 640), BF16),
        ],
        (pltpu.VMEM((136, 512), F32),),
    )(core, near, far, history, conv_w, conv_b, weight)


def scan_block(
    core, lengths, low_own, low_other, conv, dt_proj, dt_bias, decay, skip, state
):
    def body(
        core_ref,
        len_ref,
        own_ref,
        other_ref,
        conv_ref,
        dtp_ref,
        dtb_ref,
        decay_ref,
        skip_ref,
        state_ref,
        mixed_ref,
        final_ref,
        step_s,
        drive_s,
        trail_s,
        dec_s,
    ):
        dec_s[...] = decay_ref[...] * (-LOG2E)
        lane = lax.broadcasted_iota(jnp.int32, (128, 128), 1)
        row = lax.broadcasted_iota(jnp.int32, (128, 128), 0)
        pick_entry = (row == lane % 16).astype(BF16)
        pick_read = (row == 16 + lane % 16).astype(BF16)
        diagonal = ((lane // 16) == (row % 8)).astype(F32)
        position = lax.broadcasted_iota(jnp.int32, (128, 512), 0)
        reads = []
        for slot, low_ref in enumerate((own_ref, other_ref)):
            request = core_ref[0] ^ slot
            mask = (position < len_ref[request]).astype(F32)
            raw = jnp.dot(low_ref[:, 0:512], dtp_ref[...], preferred_element_type=F32) + dtb_ref[...]
            step = (jnp.maximum(raw, 0.0) + jnp.log(1.0 + jnp.exp(-jnp.abs(raw)))) * mask
            step_s[slot] = step
            drive = (step * conv_ref[request].astype(F32)).astype(BF16)
            tail = low_ref[:, 512:640]
            entry = (jnp.dot(tail, pick_entry, preferred_element_type=F32) * diagonal).astype(BF16)
            reads.append(
                (jnp.dot(tail, pick_read, preferred_element_type=F32) * diagonal).astype(BF16)
            )
            for piece in range(8):
                for half in range(2):
                    at = piece * 16 + half * 8
                    keep = (
                        lax.broadcasted_iota(jnp.int32, (16, 128), 0) // 8 == half
                    ).astype(BF16)
                    drive_s[slot, at * 16 : at * 16 + 128] = lax.dot_general(
                        entry[piece * 16 : piece * 16 + 16] * keep,
                        drive[piece * 16 : piece * 16 + 16],
                        (((0,), (0,)), ((), ())),
                        preferred_element_type=F32,
                    )

        def advance(block, held):
            held = list(held)
            base = pl.multiple_of(block * 8, 8)
            for slot in range(2):
                steps = step_s[slot, pl.ds(base, 8)]
                now = held[slot]
                for offset in range(8):
                    rows = pl.ds(pl.multiple_of(block * 128 + offset * 16, 16), 16)
                    now = jnp.exp2(steps[offset : offset + 1] * dec_s[...]) * now + drive_s[slot, rows]
                    trail_s[slot, rows] = now.astype(BF16)
                held[slot] = now
            return tuple(held)

        first = tuple(state_ref[core_ref[0] ^ slot] for slot in range(2))
        last = lax.fori_loop(0, 16, advance, first)
        for slot in range(2):
            request = core_ref[0] ^ slot
            final_ref[request] = last[slot]
            outs = []
            for piece in range(16):
                outs.append(
                    jnp.dot(
                        reads[slot][piece * 8 : piece * 8 + 8],
                        trail_s[slot, piece * 128 : piece * 128 + 128],
                        preferred_element_type=F32,
                    )
                )
            mask = (position < len_ref[request]).astype(F32)
            mixed = jnp.concatenate(outs, axis=0) + skip_ref[...] * conv_ref[request].astype(F32)
            mixed_ref[request] = mixed * mask

    def whole(*shape):
        return pl.BlockSpec(shape, lambda i, c, n: (0,) * len(shape))

    return call(
        body,
        (core, lengths),
        (1,),
        [
            whole(128, 640),
            whole(128, 640),
            whole(2, 128, 512),
            whole(512, 512),
            whole(1, 512),
            whole(16, 512),
            whole(1, 512),
            whole(2, 16, 512),
        ],
        [whole(2, 128, 512), whole(2, 16, 512)],
        [
            jax.ShapeDtypeStruct((2, 128, 512), F32),
            jax.ShapeDtypeStruct((2, 16, 512), F32),
        ],
        (
            pltpu.VMEM((2, 128, 512), F32),
            pltpu.VMEM((2, 2048, 512), F32),
            pltpu.VMEM((2, 2048, 512), BF16),
            pltpu.VMEM((16, 512), F32),
        ),
    )(
        core,
        lengths,
        low_own,
        low_other,
        conv,
        dt_proj,
        dt_bias,
        decay,
        skip,
        state,
    )


def mixer_product(place, mixed, z_near, z_far, blocks):
    def body(place_ref, mixed_ref, near_ref, far_ref, *refs):
        own, below, above, pair, up_two, up_pair, down_two, down_pair, over, low, mid, high = refs[:12]
        own_ref, other_ref = refs[12:]
        z_gate = (near_ref[...] + far_ref[...].astype(F32)).astype(BF16).astype(F32)
        gated = (mixed_ref[...] * silu(z_gate)).astype(BF16).reshape(256, 512)

        def times(begin, end, value):
            return jnp.dot(gated[:, begin:end], value, preferred_element_type=F32)

        def split(top, bottom):
            return times(0, 256, top) + times(256, 512, bottom)

        sums = (
            lambda: times(0, 512, own[...]),
            lambda: times(0, 512, below[...]),
            lambda: times(0, 512, above[...]),
            lambda: split(up_two[...], down_two[...]),
            lambda: times(0, 512, pair[...]),
            lambda: split(up_pair[...], over[256:512]),
            lambda: split(over[0:256], down_pair[...]),
            lambda: times(0, 128, low[...]) + times(128, 256, mid[...]) + times(256, 512, high[...]),
        )
        for index, make in enumerate(sums):
            value = make().astype(BF16)
            part = ((place_ref[1] + RING[index % 4]) % 4) * 2 + (place_ref[2] ^ (index // 4))

            @pl.when(part // 4 == place_ref[0])
            def _():
                own_ref[part % 4, 0] = value[:, 0:256]
                own_ref[part % 4, 1] = value[:, 256:512]

            @pl.when(part // 4 != place_ref[0])
            def _():
                other_ref[part % 4, 0] = value[:, 0:256]
                other_ref[part % 4, 1] = value[:, 256:512]

    def whole(*shape):
        return pl.BlockSpec(shape, lambda i, c: (0,) * len(shape))

    def rows_at(count, index):
        return pl.BlockSpec((count, 512), lambda i, c: (index, 0))

    out_block, below, above, pair, up, down, over, low, mid, high = blocks
    return call(
        body,
        (place,),
        (1,),
        [whole(2, 128, 512)] * 3
        + [rows_at(512, 0), rows_at(512, 1), rows_at(512, 1), rows_at(512, 0)]
        + [rows_at(256, 1), rows_at(256, 2)] * 2
        + [rows_at(512, 0), rows_at(128, 0), rows_at(128, 0), rows_at(256, 0)],
        [whole(4, 2, 256, 256)] * 2,
        [jax.ShapeDtypeStruct((4, 2, 256, 256), BF16)] * 2,
    )(
        place,
        mixed,
        z_near,
        z_far,
        out_block,
        below,
        above,
        pair,
        up,
        up,
        down,
        down,
        over,
        low,
        mid,
        high,
    )


def tables_of(routes_t):
    expert = lax.broadcasted_iota(jnp.int32, (8, 256), 0)
    picks = [(expert == routes_t[k : k + 1]) for k in range(2)]
    counts = (picks[0] | picks[1]).astype(BF16)
    earlier = (
        lax.broadcasted_iota(jnp.int32, (256, 256), 0)
        < lax.broadcasted_iota(jnp.int32, (256, 256), 1)
    ).astype(BF16)
    before = jnp.dot(counts, earlier, preferred_element_type=F32)
    place = before + 96.0 * expert.astype(F32)
    slot_row = lax.broadcasted_iota(jnp.int32, (768, 256), 0)
    hit = None
    for pick in picks:
        slot = jnp.sum(jnp.where(pick, place, 0.0), axis=0, keepdims=True).astype(jnp.int32)
        mine = slot_row == slot
        hit = mine if hit is None else hit | mine
    return hit.astype(BF16)


def hidden_dispatch(block, parts, x_rows, gain, routes_t):
    def body(block_ref, parts_ref, x_ref, gain_ref, routes_ref, hidden_ref, out_ref):
        mixer = jnp.sum(parts_ref[...].astype(F32), axis=0)
        hidden = (x_ref[...].astype(F32) + mixer).astype(BF16)
        hidden_ref[...] = hidden
        scaled = (hidden.astype(F32) * gain_ref[...]).astype(BF16)
        out_ref[...] = jnp.dot(
            tables_of(routes_ref[...]), scaled, preferred_element_type=F32
        ).astype(BF16)

    return call(
        body,
        (block,),
        (1,),
        [
            pl.BlockSpec((8, 256, 256), lambda i, b: (0, 0, 0)),
            pl.BlockSpec((256, 256), lambda i, b: (0, b[0])),
            pl.BlockSpec((1, 256), lambda i, b: (0, b[0])),
            pl.BlockSpec((2, 256), lambda i, b: (0, 0)),
        ],
        [
            pl.BlockSpec((256, 256), lambda i, b: (0, 0)),
            pl.BlockSpec((768, 256), lambda i, b: (0, 0)),
        ],
        [
            jax.ShapeDtypeStruct((256, 256), BF16),
            jax.ShapeDtypeStruct((768, 256), BF16),
        ],
    )(block, parts, x_rows, gain, routes_t)


def block_places(core_at, x_at, far_at):
    near = [far_at * 4 + (x_at + step) % 4 for step in (0, 3, 1)]
    cross = [(1 - far_at) * 4 + (x_at + step) % 4 for step in (0, 3, 1, 2)]
    two = far_at * 4 + (x_at + 2) % 4
    order = near + cross[0:1] + [two] + cross[1:4]
    return jnp.stack([core_at * 8 + at for at in order] + [(1 - core_at) * 8 + at for at in order])


def gate_up(places, first, rows, inverse, router_row, w_gate, w_up, held=None):
    def body(places_ref, *refs):
        rows_refs, inverse_refs, router_refs = refs[0:8], refs[8:16], refs[16:24]
        gate_refs, up_refs = refs[24:32], refs[32:40]

        def stats():
            squares, logits = None, None
            for piece in range(8):
                value = rows_refs[piece][...].astype(F32)
                square = value * inverse_refs[piece][...]
                square = square * square
                square = square[:, 0:128] + square[:, 128:256]
                squares = square if squares is None else squares + square
                logit = value * router_refs[piece][...]
                logit = logit[:, 0:128] + logit[:, 128:256]
                logits = logit if logits is None else logits + logit
            return squares, logits

        gate_w = jnp.concatenate([ref[...] for ref in gate_refs], axis=0)
        up_w = jnp.concatenate([ref[...] for ref in up_refs], axis=0)
        if held is None:
            gate_out, up_out, squares_out, logits_out = refs[40:]

            @pl.when(pl.program_id(0) == 0)
            def _():
                squares_out[...], logits_out[...] = stats()

        else:
            gate_in, up_in, squares_in, logits_in, active_out, scale_s, weight_s = refs[40:]

            @pl.when(pl.program_id(0) == 0)
            def _():
                squares, logits = stats()
                squares = jnp.sum(squares_in[...] + squares, axis=1, keepdims=True)
                logits = jnp.sum(logits_in[...] + logits, axis=1, keepdims=True)
                scale = lax.rsqrt(squares * (1.0 / 4096.0) + EPS)
                scale_s[...] = jnp.broadcast_to(scale, (768, 128))
                weight_s[...] = jnp.broadcast_to(scale * sigmoid(logits * scale), (768, 128))

        for begin in range(0, 768, 256):
            at = slice(begin, begin + 256)
            units = jnp.concatenate([ref[at, :] for ref in rows_refs], axis=1)
            gate = jnp.dot(units, gate_w, preferred_element_type=F32)
            up = jnp.dot(units, up_w, preferred_element_type=F32)
            if held is None:
                gate_out[at, :] = gate
                up_out[at, :] = up
            else:
                gate = (gate + gate_in[at, :]) * scale_s[at, 0:1]
                up = (up + up_in[at, :]) * weight_s[at, 0:1]
                active_out[at, :] = (silu(gate) * up).astype(BF16)

    def at(piece):
        return first + piece % 4 + 8 * (piece // 4)

    def row_spec(piece):
        return pl.BlockSpec((1, 256), lambda n, p: (0, p[at(piece)]))

    def weight_spec(piece):
        return pl.BlockSpec((256, 256), lambda n, p: (p[at(piece)], n))

    def whole(*shape):
        return pl.BlockSpec(shape, lambda n, p: (0, 0))

    tile = pl.BlockSpec((768, 256), lambda n, p: (0, n))
    kept = [tile, tile, whole(768, 128), whole(768, 128)]
    if held is None:
        outs = kept
        shapes = [jax.ShapeDtypeStruct((768, 768), F32)] * 2 + [
            jax.ShapeDtypeStruct((768, 128), F32)
        ] * 2
    else:
        outs, shapes = tile, jax.ShapeDtypeStruct((768, 768), BF16)
    return call(
        body,
        (places,),
        (3,),
        [whole(768, 256)] * 8
        + [row_spec(piece) for piece in range(8)] * 2
        + [weight_spec(piece) for piece in range(8)] * 2
        + ([] if held is None else kept),
        outs,
        shapes,
        () if held is None else (pltpu.VMEM((768, 128), F32),) * 2,
        cost=pl.CostEstimate(flops=2 * 768 * 2048 * 1536, bytes_accessed=20 << 20, transcendentals=0),
        megabytes=40,
    )(
        places,
        *rows,
        *([inverse] * 8),
        *([router_row] * 8),
        *([w_gate] * 8),
        *([w_up] * 8),
        *(() if held is None else held),
    )


def down_product(places, first, active, w_down, received=None):
    def body(places_ref, rows_ref, *refs):
        out_ref = refs[-1]
        for side in range(2):
            value = jnp.dot(rows_ref[...], refs[side][...], preferred_element_type=F32)
            if received is not None:
                value = value + refs[2][side].astype(F32)
            out_ref[side] = value.astype(BF16)

    def weight_spec(side):
        return pl.BlockSpec((768, 256), lambda i, p: (0, p[first + 2 * i + side]))

    blocks = pl.BlockSpec((2, 768, 256), lambda i, p: (i, 0, 0))
    return call(
        body,
        (places,),
        (2,),
        [pl.BlockSpec((768, 768), lambda i, p: (0, 0)), weight_spec(0), weight_spec(1)]
        + ([] if received is None else [blocks]),
        blocks,
        jax.ShapeDtypeStruct((4, 768, 256), BF16),
        cost=pl.CostEstimate(flops=2 * 768 * 768 * 1024, bytes_accessed=5 << 20, transcendentals=0),
        megabytes=24,
    )(places, active, w_down, w_down, *(() if received is None else (received,)))


def whole_call(body, shapes, operands):
    def spec(shape):
        return pl.BlockSpec(shape, lambda i: (0,) * len(shape))

    outs = [jax.ShapeDtypeStruct(shape, BF16) for shape in shapes]
    return call(
        body,
        (),
        (1,),
        [spec(value.shape) for value in operands],
        [spec(shape) for shape in shapes],
        outs,
    )(*operands)


def fold_far(far, corner):
    def body(far_ref, low_ref, mid_ref, high_ref, up_ref, down_ref, cross_ref):
        def add(block, begin, end, ref, at):
            return (
                far_ref[block, begin:end].astype(F32) + ref[at : at + end - begin].astype(F32)
            ).astype(BF16)

        up_ref[0:384] = far_ref[0, 0:384]
        up_ref[384:640] = add(2, 0, 256, low_ref, 0)
        up_ref[640:768] = far_ref[2, 256:384]
        down_ref[0:128] = far_ref[0, 384:512]
        down_ref[128:384] = add(0, 512, 768, high_ref, 0)
        down_ref[384:512] = add(1, 384, 512, mid_ref, 128)
        down_ref[512:768] = far_ref[1, 512:768]
        cross_ref[0:384] = far_ref[2, 384:768]
        cross_ref[384:640] = far_ref[1, 0:256]
        cross_ref[640:768] = add(1, 256, 384, mid_ref, 0)

    return whole_call(body, [(768, 256)] * 3, (far,) + corner)


def fold_near(near, up, down, cross):
    def body(near_ref, up_ref, down_ref, cross_ref, left_ref, right_ref, row_ref):
        for out_ref, block, top, bottom in (
            (right_ref, 2, up_ref[0:384], cross_ref[0:384]),
            (left_ref, 1, cross_ref[384:768], down_ref[0:384]),
            (row_ref, 3, up_ref[384:768], down_ref[384:768]),
        ):
            out_ref[0:384] = (near_ref[block, 0:384].astype(F32) + top.astype(F32)).astype(BF16)
            out_ref[384:768] = (near_ref[block, 384:768].astype(F32) + bottom.astype(F32)).astype(
                BF16
            )

    return whole_call(body, [(768, 256)] * 3, (near, up, down, cross))


def fold_own(near, parts):
    def body(near_ref, a_ref, b_ref, c_ref, out_ref):
        total = near_ref[0].astype(F32) + a_ref[...].astype(F32)
        out_ref[...] = (total + b_ref[...].astype(F32) + c_ref[...].astype(F32)).astype(BF16)

    return whole_call(body, [(768, 256)], (near,) + parts)[0]


def combine(hidden, back, routes_t):
    def body(hidden_ref, back_ref, routes_ref, out_ref):
        mixed = lax.dot_general(
            tables_of(routes_ref[...]),
            back_ref[...],
            (((0,), (0,)), ((), ())),
            preferred_element_type=F32,
        )
        out_ref[...] = (hidden_ref[...].astype(F32) + mixed).astype(BF16)

    return call(
        body,
        (),
        (1,),
        [
            pl.BlockSpec((256, 256), lambda i: (0, 0)),
            pl.BlockSpec((768, 256), lambda i: (0, 0)),
            pl.BlockSpec((2, 256), lambda i: (0, 0)),
        ],
        pl.BlockSpec((256, 256), lambda i: (0, 0)),
        jax.ShapeDtypeStruct((256, 256), BF16),
    )(hidden, back, routes_t)


def assemble(core, own, other):
    def body(core_ref, own_ref, other_ref, out_ref):
        for side, ref in enumerate((own_ref, other_ref)):

            @pl.when(pl.program_id(0) == side)
            def _():
                for piece in range(4):
                    out_ref[:, piece * 256 : piece * 256 + 256] = ref[piece]

    return call(
        body,
        (core,),
        (2, 2),
        [
            pl.BlockSpec((4, 256, 256), lambda s, i, c: (jnp.where(s == 0, i, 1), 0, 0)),
            pl.BlockSpec((4, 256, 256), lambda s, i, c: (jnp.where(s == 0, 0, i), 0, 0)),
        ],
        pl.BlockSpec((256, 1024), lambda s, i, c: (0, (c[0] ^ s) * 2 + i)),
        jax.ShapeDtypeStruct((256, 4096), BF16),
    )(core, own, other)


def per_device(
    x_rows,
    lengths,
    routes,
    conv_state,
    ssm_state,
    norm1_gain,
    in_x,
    in_z,
    conv_w,
    conv_b,
    x_dt,
    x_bc,
    dt_proj,
    dt_bias,
    decay_rate,
    skip,
    out_w,
    norm2_gain,
    router,
    w_gate,
    w_up,
    w_down,
):
    core_at = lax.axis_index("core").astype(jnp.int32)
    core = core_at.reshape(1)
    chip_at = lax.axis_index(CHIPS).astype(jnp.int32)
    block = (core_at * 8 + chip_at).reshape(1)
    expert_at = lax.axis_index(DP).astype(jnp.int32)

    place = jnp.stack(
        [core_at, lax.axis_index("z").astype(jnp.int32), lax.axis_index("ylo").astype(jnp.int32)]
    )
    low_weight = jnp.concatenate([x_dt, x_bc, jnp.zeros((512, 96), BF16)], axis=1)
    history = jnp.pad(conv_state.astype(F32), ((0, 0), (5, 0), (0, 0)))
    routes_t = routes.T
    router_row = lax.dynamic_slice(router, (0, expert_at), (4096, 1)).astype(F32).reshape(1, 4096)

    rows_mine, rows_send = norm_split(place, x_rows, norm1_gain.reshape(1, 4096))
    pair_own = swap_pair(rows_send)
    x_below, x_above = from_below(in_x), from_above(in_x)
    x_halves = (x_below[:256], x_above[256:])
    x_blocks = gather_ring(in_x, x_below, x_above, x_halves)
    pair_other = swap_core(after(pair_own, *x_halves))
    both = after(jnp.concatenate([in_z, out_w]), pair_other, *x_blocks[3:5])
    both_below, both_above = from_below(both), from_above(both)
    out_pair = swap_pair(after(out_w, pair_own))
    x_far = swap_pair(pair_product(place, pair_own, pair_other, x_blocks))
    sends = second_round(both_below, both_above, out_pair)
    x_near = own_product(rows_mine, x_blocks)
    conv, low = conv_project(
        core, x_near, x_far, history, conv_w, conv_b.reshape(1, 512), low_weight
    )
    low_pair = add_half(low[0], swap_core(low[1]))
    inverse = 1.0 / norm2_gain.reshape(1, 4096)
    low_pair = after(low_pair, router_row, inverse, *sends)
    low_two = add_half(low_pair, swap_far(low_pair))
    low_four = add_half(low_two, lax.ppermute(low_two, "x", [(i, i ^ 1) for i in range(4)]))
    up, down, over = from_below(sends[0]), from_above(sends[1]), swap_pair(sends[2])
    low_own = add_half(low_four, lax.ppermute(low_four, "x", [(i, i ^ 2) for i in range(4)]))
    low_other = swap_core(low_own)
    mixed, final = scan_block(
        core,
        lengths,
        low_own,
        low_other,
        conv,
        dt_proj,
        dt_bias.reshape(1, 512),
        decay_rate,
        skip.reshape(1, 512),
        ssm_state,
    )
    z_blocks = (in_z, both_below, both_above, up, down)
    z_far = swap_pair(pair_product(place, pair_own, pair_other, z_blocks))
    corner = third_round(up, down, over)
    z_near = own_product(rows_mine, z_blocks)
    out_blocks = (out_w, both_below, both_above, out_pair, up, down, over) + corner
    mixer_own, mixer_other = mixer_product(place, mixed, z_near, z_far, out_blocks)
    mixer_pair = (mixer_own.astype(F32) + swap_core(mixer_other).astype(F32)).astype(BF16)
    mixer_parts = exchange(mixer_pair.reshape(8, 256, 256), CHIPS)
    places = block_places(
        core_at, lax.axis_index("x").astype(jnp.int32), lax.axis_index("yhi").astype(jnp.int32)
    )
    gain = norm2_gain.reshape(1, 4096)
    hidden, outgoing = hidden_dispatch(block, mixer_parts, x_rows, gain, routes_t)
    rows = exchange(outgoing.reshape(8, 96, 256), DP).reshape(768, 256)
    left, right, cross = from_left(rows), from_right(rows), swap_far(rows)
    near = (rows, left, right, cross)
    near_other = tuple(swap_core(value) for value in near)
    top, bottom = slice(0, 384), slice(384, 768)
    up = from_left(jnp.concatenate([left[top], cross[top]]))
    down = from_right(jnp.concatenate([right[bottom], cross[bottom]]))
    over = swap_far(jnp.concatenate([right[top], left[bottom]]))
    held = gate_up(places, 0, near + near_other, inverse, router_row, w_gate[0], w_up[0])
    up, down, over = (after(value, held[2]) for value in (up, down, over))
    two = jnp.concatenate([up[top], down[top]])
    cross_left = jnp.concatenate([up[bottom], over[bottom]])
    cross_right = jnp.concatenate([over[top], down[bottom]])
    cross_two = jnp.concatenate(
        [from_left(cross_left[0:256]), from_right(cross_right[256:512]), swap_far(two[512:768])]
    )
    far = (two, cross_left, cross_right, cross_two)
    far_other = tuple(swap_core(value) for value in far)
    active = gate_up(places, 4, far + far_other, inverse, router_row, w_gate[0], w_up[0], held)
    far_sent = swap_core(down_product(places, 12, active, w_down[0]))
    near_sent = swap_core(down_product(places, 8, active, w_down[0]))
    far_sum = down_product(places, 4, active, w_down[0], far_sent)
    corner = (
        from_left(far_sum[3, 0:256]),
        from_right(far_sum[3, 256:512]),
        swap_far(far_sum[3, 512:768]),
    )
    near_sum = down_product(places, 0, active, w_down[0], near_sent)
    up_send, down_send, cross_send = fold_far(far_sum, corner)
    to_left, to_right, to_row = fold_near(
        near_sum, from_left(up_send), from_right(down_send), swap_far(cross_send)
    )
    total = fold_own(near_sum, (from_left(to_right), from_right(to_left), swap_far(to_row)))
    back = exchange(total.reshape(8, 96, 256), DP).reshape(768, 256)
    out_own = spread(combine(hidden, back, routes_t))
    out_other = swap_core(out_own)
    return (assemble(core, out_own, out_other), final)


def solution(mesh):
    wide = Mesh(mesh.devices.reshape(4, 2, 2, 4, 2), ("z", "ylo", "yhi", "x", "core"))
    return jax.shard_map(
        per_device,
        mesh=wide,
        in_specs=(
            P(DP, None),
            P(DP),
            P(DP, None),
            P(DP, None, TENSOR),
            P(DP, None, TENSOR),
            P(),
            P(DP, TENSOR),
            P(DP, TENSOR),
            P(None, TENSOR),
            P(TENSOR),
            P(TENSOR, None),
            P(TENSOR, None),
            P(None, TENSOR),
            P(TENSOR),
            P(None, TENSOR),
            P(TENSOR),
            P(TENSOR, DP),
            P(),
            P(),
            P(DP, None, TENSOR),
            P(DP, None, TENSOR),
            P(DP, TENSOR, None),
        ),
        out_specs=(P(DP, None), P(DP, None, TENSOR)),
        check_vma=False,
    )
```

```python
import jax
import jax.numpy as jnp
from jax import lax
from jax.sharding import Mesh
from jax.sharding import PartitionSpec as P
from jax.experimental import pallas as pl
from jax.experimental.pallas import tpu as pltpu

F32 = jnp.float32
BF16 = jnp.bfloat16
DP = ("z", "ylo")
TENSOR = ("yhi", "x", "core")
CHIPS = ("yhi", "x")
EPS = 1e-05
LOG2E = 1.4426950408889634


def params(megabytes):
    return pltpu.CompilerParams(vmem_limit_bytes=megabytes << 20)


def call(
    body, scalars, grid, in_specs, out_specs, out_shape, scratch=(), cost=None, megabytes=24, alias=None
):
    if cost is None:
        cost = pl.CostEstimate(flops=1 << 20, bytes_accessed=1 << 16, transcendentals=0)
    spec = pltpu.PrefetchScalarGridSpec(
        num_scalar_prefetch=len(scalars),
        grid=grid,
        in_specs=in_specs,
        out_specs=out_specs,
        scratch_shapes=scratch,
    )
    return pl.pallas_call(
        body, grid_spec=spec, out_shape=out_shape, compiler_params=params(megabytes), cost_estimate=cost, input_output_aliases=alias or {}
    )


def exchange(value, axes):
    return lax.all_to_all(value, axes, split_axis=0, concat_axis=0, tiled=True)


def spread(value):
    return exchange(jnp.broadcast_to(value[None], (8,) + value.shape), CHIPS)


def from_left(value):
    return lax.ppermute(value, "x", [(i, (i + 1) % 4) for i in range(4)])


def from_right(value):
    return lax.ppermute(value, "x", [(i, (i - 1) % 4) for i in range(4)])


def swap_far(value):
    return lax.ppermute(value, "yhi", [(0, 1), (1, 0)])


def add_half(value, received):
    return (value.astype(F32) + received.astype(F32)).astype(BF16)


def swap_core(value):
    return lax.ppermute(value, "core", [(0, 1), (1, 0)])


def sigmoid(value):
    return 1.0 / (1.0 + jnp.exp(-value))


def silu(value):
    return value * sigmoid(value)


RING = (0, 3, 1, 2)


def from_below(value):
    return lax.ppermute(value, "z", [(i, (i + 1) % 4) for i in range(4)])


def from_above(value):
    return lax.ppermute(value, "z", [(i, (i - 1) % 4) for i in range(4)])


def after(value, *earlier):
    return lax.optimization_barrier((value,) + earlier)[0]


def swap_pair(value):
    return lax.ppermute(value, "ylo", [(0, 1), (1, 0)])


def gather_ring(block, below, above, halves):
    return block, below, above, from_below(halves[0]), from_above(halves[1])


def second_round(below, above, pair):
    return (
        jnp.concatenate([below[0:256], below[512:768], pair[0:256]]),
        jnp.concatenate([above[256:512], above[768:1024], pair[256:512]]),
        jnp.concatenate([above[512:768], below[768:1024]]),
    )


def third_round(up, down, over):
    return from_below(up[512:640]), from_above(over[128:256]), swap_pair(down[256:512])


def norm_split(place, x_rows, gain):
    def body(place_ref, x_ref, gain_ref, own_ref, send_ref):
        request = pl.ds(pl.multiple_of(place_ref[0] * 128, 128), 128)
        for rows, out_ref, member in (
            (slice(0, 256), own_ref, place_ref[2]),
            (request, send_ref, 1 - place_ref[2]),
        ):
            values = x_ref[rows, :].astype(F32)
            scale = lax.rsqrt(jnp.mean(values * values, axis=-1, keepdims=True) + EPS)
            for piece, shift in enumerate(RING):
                at = ((place_ref[1] + shift) % 4) * 2 + member
                columns = pl.ds(pl.multiple_of(at * 512, 512), 512)
                part = x_ref[rows, columns].astype(F32)
                out_ref[piece] = (part * scale * gain_ref[:, columns]).astype(BF16)

    return call(
        body,
        (place,),
        (1,),
        [
            pl.BlockSpec((256, 4096), lambda i, c: (0, 0)),
            pl.BlockSpec((1, 4096), lambda i, c: (0, 0)),
        ],
        [
            pl.BlockSpec((4, 256, 512), lambda i, c: (0, 0, 0)),
            pl.BlockSpec((4, 128, 512), lambda i, c: (0, 0, 0)),
        ],
        [
            jax.ShapeDtypeStruct((4, 256, 512), BF16),
            jax.ShapeDtypeStruct((4, 128, 512), BF16),
        ],
    )(place, x_rows, gain)


def ring_product(rows_ref, blocks):
    total = None
    for piece in range(3):
        term = jnp.dot(rows_ref[piece], blocks[piece][...], preferred_element_type=F32)
        total = term if total is None else total + term
    total = total + jnp.dot(rows_ref[3, :, 0:256], blocks[3][...], preferred_element_type=F32)
    return total + jnp.dot(rows_ref[3, :, 256:512], blocks[4][...], preferred_element_type=F32)


RING_SPECS = [pl.BlockSpec((512, 512), lambda *_: (0, 0))] * 3 + [
    pl.BlockSpec((256, 512), lambda *_: (0, 0))
] * 2


def pair_product(place, own, other, blocks):
    def body(place_ref, own_ref, other_ref, *refs):
        for slot, rows_ref in enumerate((own_ref, other_ref)):
            refs[5][place_ref[0] ^ slot] = ring_product(rows_ref, refs[:5]).astype(BF16)

    return call(
        body,
        (place,),
        (1,),
        [pl.BlockSpec((4, 128, 512), lambda i, c: (0, 0, 0))] * 2 + RING_SPECS,
        pl.BlockSpec((2, 128, 512), lambda i, c: (0, 0, 0)),
        jax.ShapeDtypeStruct((2, 128, 512), BF16),
    )(place, own, other, *blocks)


def own_product(rows, blocks):
    def body(rows_ref, *refs):
        refs[5][...] = ring_product(rows_ref, refs[:5]).reshape(2, 128, 512)

    return call(
        body,
        (),
        (1,),
        [pl.BlockSpec((4, 256, 512), lambda i: (0, 0, 0))] + RING_SPECS,
        pl.BlockSpec((2, 128, 512), lambda i: (0, 0, 0)),
        jax.ShapeDtypeStruct((2, 128, 512), F32),
    )(rows, *blocks)


def conv_project(core, near, far, history, conv_w, conv_b, weight):
    def body(core_ref, near_ref, far_ref, hist_ref, cw_ref, cb_ref, w_ref, conv_ref, low_ref, line):
        x_inner = (near_ref[0] + far_ref[0].astype(F32)).astype(BF16).astype(F32)
        line[0:8] = hist_ref[0]
        line[8:136] = x_inner
        total = cb_ref[...] + cw_ref[3:4] * x_inner
        for tap in range(3):
            total = total + cw_ref[tap : tap + 1] * line[5 + tap : 133 + tap]
        conv = silu(total).astype(BF16)
        conv_ref[0] = conv
        low_ref[0] = jnp.dot(conv, w_ref[...], preferred_element_type=F32).astype(BF16)

    return call(
        body,
        (core,),
        (2,),
        [
            pl.BlockSpec((1, 128, 512), lambda r, c: (r, 0, 0)),
            pl.BlockSpec((1, 128, 512), lambda r, c: (r, 0, 0)),
            pl.BlockSpec((1, 8, 512), lambda r, c: (r, 0, 0)),
            pl.BlockSpec((4, 512), lambda r, c: (0, 0)),
            pl.BlockSpec((1, 512), lambda r, c: (0, 0)),
            pl.BlockSpec((512, 640), lambda r, c: (0, 0)),
        ],
        [
            pl.BlockSpec((1, 128, 512), lambda r, c: (r, 0, 0)),
            pl.BlockSpec((1, 128, 640), lambda r, c: (r ^ c[0], 0, 0)),
        ],
        [
            jax.ShapeDtypeStruct((2, 128, 512), BF16),
            jax.ShapeDtypeStruct((2, 128, 640), BF16),
        ],
        (pltpu.VMEM((136, 512), F32),),
    )(core, near, far, history, conv_w, conv_b, weight)


def scan_block(
    core, lengths, low_own, low_other, conv, dt_proj, dt_bias, decay, skip, state
):
    def body(
        core_ref,
        len_ref,
        own_ref,
        other_ref,
        conv_ref,
        dtp_ref,
        dtb_ref,
        decay_ref,
        skip_ref,
        state_ref,
        mixed_ref,
        final_ref,
        step_s,
        drive_s,
        trail_s,
        dec_s,
    ):
        dec_s[...] = decay_ref[...] * (-LOG2E)
        lane = lax.broadcasted_iota(jnp.int32, (128, 128), 1)
        row = lax.broadcasted_iota(jnp.int32, (128, 128), 0)
        pick_entry = (row == lane % 16).astype(BF16)
        pick_read = (row == 16 + lane % 16).astype(BF16)
        diagonal = ((lane // 16) == (row % 8)).astype(F32)
        position = lax.broadcasted_iota(jnp.int32, (128, 512), 0)
        reads = []
        for slot, low_ref in enumerate((own_ref, other_ref)):
            request = core_ref[0] ^ slot
            mask = (position < len_ref[request]).astype(F32)
            raw = jnp.dot(low_ref[:, 0:512], dtp_ref[...], preferred_element_type=F32) + dtb_ref[...]
            step = (jnp.maximum(raw, 0.0) + jnp.log(1.0 + jnp.exp(-jnp.abs(raw)))) * mask
            step_s[slot] = step
            drive = (step * conv_ref[request].astype(F32)).astype(BF16)
            tail = low_ref[:, 512:640]
            entry = (jnp.dot(tail, pick_entry, preferred_element_type=F32) * diagonal).astype(BF16)
            reads.append(
                (jnp.dot(tail, pick_read, preferred_element_type=F32) * diagonal).astype(BF16)
            )
            for piece in range(8):
                for half in range(2):
                    at = piece * 16 + half * 8
                    keep = (
                        lax.broadcasted_iota(jnp.int32, (16, 128), 0) // 8 == half
                    ).astype(BF16)
                    drive_s[slot, at * 16 : at * 16 + 128] = lax.dot_general(
                        entry[piece * 16 : piece * 16 + 16] * keep,
                        drive[piece * 16 : piece * 16 + 16],
                        (((0,), (0,)), ((), ())),
                        preferred_element_type=F32,
                    )

        def advance(block, held):
            held = list(held)
            base = pl.multiple_of(block * 8, 8)
            for slot in range(2):
                steps = step_s[slot, pl.ds(base, 8)]
                now = held[slot]
                for offset in range(8):
                    rows = pl.ds(pl.multiple_of(block * 128 + offset * 16, 16), 16)
                    now = jnp.exp2(steps[offset : offset + 1] * dec_s[...]) * now + drive_s[slot, rows]
                    trail_s[slot, rows] = now.astype(BF16)
                held[slot] = now
            return tuple(held)

        first = tuple(state_ref[core_ref[0] ^ slot] for slot in range(2))
        last = lax.fori_loop(0, 16, advance, first)
        for slot in range(2):
            request = core_ref[0] ^ slot
            final_ref[request] = last[slot]
            outs = []
            for piece in range(16):
                outs.append(
                    jnp.dot(
                        reads[slot][piece * 8 : piece * 8 + 8],
                        trail_s[slot, piece * 128 : piece * 128 + 128],
                        preferred_element_type=F32,
                    )
                )
            mask = (position < len_ref[request]).astype(F32)
            mixed = jnp.concatenate(outs, axis=0) + skip_ref[...] * conv_ref[request].astype(F32)
            mixed_ref[request] = mixed * mask

    def whole(*shape):
        return pl.BlockSpec(shape, lambda i, c, n: (0,) * len(shape))

    return call(
        body,
        (core, lengths),
        (1,),
        [
            whole(128, 640),
            whole(128, 640),
            whole(2, 128, 512),
            whole(512, 512),
            whole(1, 512),
            whole(16, 512),
            whole(1, 512),
            whole(2, 16, 512),
        ],
        [whole(2, 128, 512), whole(2, 16, 512)],
        [
            jax.ShapeDtypeStruct((2, 128, 512), F32),
            jax.ShapeDtypeStruct((2, 16, 512), F32),
        ],
        (
            pltpu.VMEM((2, 128, 512), F32),
            pltpu.VMEM((2, 2048, 512), F32),
            pltpu.VMEM((2, 2048, 512), BF16),
            pltpu.VMEM((16, 512), F32),
        ),
    )(
        core,
        lengths,
        low_own,
        low_other,
        conv,
        dt_proj,
        dt_bias,
        decay,
        skip,
        state,
    )


def mixer_product(place, mixed, z_near, z_far, blocks):
    def body(place_ref, mixed_ref, near_ref, far_ref, *refs):
        own, below, above, pair, up_two, up_pair, down_two, down_pair, over, low, mid, high = refs[:12]
        own_ref, other_ref = refs[12:]
        z_gate = (near_ref[...] + far_ref[...].astype(F32)).astype(BF16).astype(F32)
        gated = (mixed_ref[...] * silu(z_gate)).astype(BF16).reshape(256, 512)

        def times(begin, end, value):
            return jnp.dot(gated[:, begin:end], value, preferred_element_type=F32)

        def split(top, bottom):
            return times(0, 256, top) + times(256, 512, bottom)

        sums = (
            lambda: times(0, 512, own[...]),
            lambda: times(0, 512, below[...]),
            lambda: times(0, 512, above[...]),
            lambda: split(up_two[...], down_two[...]),
            lambda: times(0, 512, pair[...]),
            lambda: split(up_pair[...], over[256:512]),
            lambda: split(over[0:256], down_pair[...]),
            lambda: times(0, 128, low[...]) + times(128, 256, mid[...]) + times(256, 512, high[...]),
        )
        for index, make in enumerate(sums):
            value = make().astype(BF16)
            part = ((place_ref[1] + RING[index % 4]) % 4) * 2 + (place_ref[2] ^ (index // 4))

            @pl.when(part // 4 == place_ref[0])
            def _():
                own_ref[part % 4, 0] = value[:, 0:256]
                own_ref[part % 4, 1] = value[:, 256:512]

            @pl.when(part // 4 != place_ref[0])
            def _():
                other_ref[part % 4, 0] = value[:, 0:256]
                other_ref[part % 4, 1] = value[:, 256:512]

    def whole(*shape):
        return pl.BlockSpec(shape, lambda i, c: (0,) * len(shape))

    def rows_at(count, index):
        return pl.BlockSpec((count, 512), lambda i, c: (index, 0))

    out_block, below, above, pair, up, down, over, low, mid, high = blocks
    return call(
        body,
        (place,),
        (1,),
        [whole(2, 128, 512)] * 3
        + [rows_at(512, 0), rows_at(512, 1), rows_at(512, 1), rows_at(512, 0)]
        + [rows_at(256, 1), rows_at(256, 2)] * 2
        + [rows_at(512, 0), rows_at(128, 0), rows_at(128, 0), rows_at(256, 0)],
        [whole(4, 2, 256, 256)] * 2,
        [jax.ShapeDtypeStruct((4, 2, 256, 256), BF16)] * 2,
    )(
        place,
        mixed,
        z_near,
        z_far,
        out_block,
        below,
        above,
        pair,
        up,
        up,
        down,
        down,
        over,
        low,
        mid,
        high,
    )


def tables_of(routes_t):
    expert = lax.broadcasted_iota(jnp.int32, (8, 256), 0)
    picks = [(expert == routes_t[k : k + 1]) for k in range(2)]
    counts = (picks[0] | picks[1]).astype(BF16)
    earlier = (
        lax.broadcasted_iota(jnp.int32, (256, 256), 0)
        < lax.broadcasted_iota(jnp.int32, (256, 256), 1)
    ).astype(BF16)
    before = jnp.dot(counts, earlier, preferred_element_type=F32)
    place = before + 96.0 * expert.astype(F32)
    slot_row = lax.broadcasted_iota(jnp.int32, (768, 256), 0)
    hit = None
    for pick in picks:
        slot = jnp.sum(jnp.where(pick, place, 0.0), axis=0, keepdims=True).astype(jnp.int32)
        mine = slot_row == slot
        hit = mine if hit is None else hit | mine
    return hit.astype(BF16)


def hidden_dispatch(block, parts, x_rows, gain, routes_t):
    def body(block_ref, parts_ref, x_ref, gain_ref, routes_ref, hidden_ref, out_ref):
        mixer = jnp.sum(parts_ref[...].astype(F32), axis=0)
        hidden = (x_ref[...].astype(F32) + mixer).astype(BF16)
        hidden_ref[...] = hidden
        scaled = (hidden.astype(F32) * gain_ref[...]).astype(BF16)
        out_ref[...] = jnp.dot(
            tables_of(routes_ref[...]), scaled, preferred_element_type=F32
        ).astype(BF16)

    return call(
        body,
        (block,),
        (1,),
        [
            pl.BlockSpec((8, 256, 256), lambda i, b: (0, 0, 0)),
            pl.BlockSpec((256, 256), lambda i, b: (0, b[0])),
            pl.BlockSpec((1, 256), lambda i, b: (0, b[0])),
            pl.BlockSpec((2, 256), lambda i, b: (0, 0)),
        ],
        [
            pl.BlockSpec((256, 256), lambda i, b: (0, 0)),
            pl.BlockSpec((768, 256), lambda i, b: (0, 0)),
        ],
        [
            jax.ShapeDtypeStruct((256, 256), BF16),
            jax.ShapeDtypeStruct((768, 256), BF16),
        ],
    )(block, parts, x_rows, gain, routes_t)


def block_places(core_at, x_at, far_at):
    near = [far_at * 4 + (x_at + step) % 4 for step in (0, 3, 1)]
    cross = [(1 - far_at) * 4 + (x_at + step) % 4 for step in (0, 3, 1, 2)]
    two = far_at * 4 + (x_at + 2) % 4
    order = near + cross[0:1] + [two] + cross[1:4]
    return jnp.stack([core_at * 8 + at for at in order] + [(1 - core_at) * 8 + at for at in order])


def gate_up(places, first, rows, inverse, router_row, w_gate, w_up, held=None):
    def body(places_ref, *refs):
        rows_refs, inverse_refs, router_refs = refs[0:8], refs[8:16], refs[16:24]
        gate_refs, up_refs = refs[24:32], refs[32:40]

        def stats():
            squares, logits = None, None
            for piece in range(8):
                value = rows_refs[piece][...].astype(F32)
                square = value * inverse_refs[piece][...]
                square = square * square
                square = square[:, 0:128] + square[:, 128:256]
                squares = square if squares is None else squares + square
                logit = value * router_refs[piece][...]
                logit = logit[:, 0:128] + logit[:, 128:256]
                logits = logit if logits is None else logits + logit
            return squares, logits

        gate_w = jnp.concatenate([ref[...] for ref in gate_refs], axis=0)
        up_w = jnp.concatenate([ref[...] for ref in up_refs], axis=0)
        if held is None:
            gate_out, up_out, squares_out, logits_out = refs[40:]

            @pl.when(pl.program_id(0) == 0)
            def _():
                squares_out[...], logits_out[...] = stats()

        else:
            gate_in, up_in, squares_in, logits_in, active_out, scale_s, weight_s = refs[40:]

            @pl.when(pl.program_id(0) == 0)
            def _():
                squares, logits = stats()
                squares = jnp.sum(squares_in[...] + squares, axis=1, keepdims=True)
                logits = jnp.sum(logits_in[...] + logits, axis=1, keepdims=True)
                scale = lax.rsqrt(squares * (1.0 / 4096.0) + EPS)
                scale_s[...] = jnp.broadcast_to(scale, (768, 128))
                weight_s[...] = jnp.broadcast_to(scale * sigmoid(logits * scale), (768, 128))

        for begin in range(0, 768, 256):
            at = slice(begin, begin + 256)
            units = jnp.concatenate([ref[at, :] for ref in rows_refs], axis=1)
            gate = jnp.dot(units, gate_w, preferred_element_type=F32)
            up = jnp.dot(units, up_w, preferred_element_type=F32)
            if held is None:
                gate_out[at, :] = gate
                up_out[at, :] = up
            else:
                gate = (gate + gate_in[at, :]) * scale_s[at, 0:1]
                up = (up + up_in[at, :]) * weight_s[at, 0:1]
                active_out[at, :] = (silu(gate) * up).astype(BF16)

    def at(piece):
        return first + piece % 4 + 8 * (piece // 4)

    def row_spec(piece):
        return pl.BlockSpec((1, 256), lambda n, p: (0, p[at(piece)]))

    def weight_spec(piece):
        return pl.BlockSpec((256, 256), lambda n, p: (p[at(piece)], n))

    def whole(*shape):
        return pl.BlockSpec(shape, lambda n, p: (0, 0))

    tile = pl.BlockSpec((768, 256), lambda n, p: (0, n))
    kept = [tile, tile, whole(768, 128), whole(768, 128)]
    if held is None:
        outs = kept
        shapes = [jax.ShapeDtypeStruct((768, 768), F32)] * 2 + [
            jax.ShapeDtypeStruct((768, 128), F32)
        ] * 2
    else:
        outs, shapes = tile, jax.ShapeDtypeStruct((768, 768), BF16)
    return call(
        body,
        (places,),
        (3,),
        [whole(768, 256)] * 8
        + [row_spec(piece) for piece in range(8)] * 2
        + [weight_spec(piece) for piece in range(8)] * 2
        + ([] if held is None else kept),
        outs,
        shapes,
        () if held is None else (pltpu.VMEM((768, 128), F32),) * 2,
        cost=pl.CostEstimate(flops=2 * 768 * 2048 * 1536, bytes_accessed=20 << 20, transcendentals=0),
        megabytes=40,
    )(
        places,
        *rows,
        *([inverse] * 8),
        *([router_row] * 8),
        *([w_gate] * 8),
        *([w_up] * 8),
        *(() if held is None else held),
    )


def down_product(places, first, active, w_down, received=None):
    def body(places_ref, rows_ref, *refs):
        out_ref = refs[-1]
        for side in range(2):
            value = jnp.dot(rows_ref[...], refs[side][...], preferred_element_type=F32)
            if received is not None:
                value = value + refs[2][side].astype(F32)
            out_ref[side] = value.astype(BF16)

    def weight_spec(side):
        return pl.BlockSpec((768, 256), lambda i, p: (0, p[first + 2 * i + side]))

    blocks = pl.BlockSpec((2, 768, 256), lambda i, p: (i, 0, 0))
    return call(
        body,
        (places,),
        (2,),
        [pl.BlockSpec((768, 768), lambda i, p: (0, 0)), weight_spec(0), weight_spec(1)]
        + ([] if received is None else [blocks]),
        blocks,
        jax.ShapeDtypeStruct((4, 768, 256), BF16),
        cost=pl.CostEstimate(flops=2 * 768 * 768 * 1024, bytes_accessed=5 << 20, transcendentals=0),
        megabytes=24,
    )(places, active, w_down, w_down, *(() if received is None else (received,)))


def whole_call(body, shapes, operands):
    def spec(shape):
        return pl.BlockSpec(shape, lambda i: (0,) * len(shape))

    outs = [jax.ShapeDtypeStruct(shape, BF16) for shape in shapes]
    return call(
        body,
        (),
        (1,),
        [spec(value.shape) for value in operands],
        [spec(shape) for shape in shapes],
        outs,
    )(*operands)


def fold_far(far, corner):
    def body(far_ref, low_ref, mid_ref, high_ref, up_ref, down_ref, cross_ref):
        def add(block, begin, end, ref, at):
            return (
                far_ref[block, begin:end].astype(F32) + ref[at : at + end - begin].astype(F32)
            ).astype(BF16)

        up_ref[0:384] = far_ref[0, 0:384]
        up_ref[384:640] = add(2, 0, 256, low_ref, 0)
        up_ref[640:768] = far_ref[2, 256:384]
        down_ref[0:128] = far_ref[0, 384:512]
        down_ref[128:384] = add(0, 512, 768, high_ref, 0)
        down_ref[384:512] = add(1, 384, 512, mid_ref, 128)
        down_ref[512:768] = far_ref[1, 512:768]
        cross_ref[0:384] = far_ref[2, 384:768]
        cross_ref[384:640] = far_ref[1, 0:256]
        cross_ref[640:768] = add(1, 256, 384, mid_ref, 0)

    return whole_call(body, [(768, 256)] * 3, (far,) + corner)


def fold_near(near, up, down, cross):
    def body(near_ref, up_ref, down_ref, cross_ref, left_ref, right_ref, row_ref):
        for out_ref, block, top, bottom in (
            (right_ref, 2, up_ref[0:384], cross_ref[0:384]),
            (left_ref, 1, cross_ref[384:768], down_ref[0:384]),
            (row_ref, 3, up_ref[384:768], down_ref[384:768]),
        ):
            out_ref[0:384] = (near_ref[block, 0:384].astype(F32) + top.astype(F32)).astype(BF16)
            out_ref[384:768] = (near_ref[block, 384:768].astype(F32) + bottom.astype(F32)).astype(
                BF16
            )

    return whole_call(body, [(768, 256)] * 3, (near, up, down, cross))


def fold_own(near, parts):
    def body(near_ref, a_ref, b_ref, c_ref, out_ref):
        total = near_ref[0].astype(F32) + a_ref[...].astype(F32)
        out_ref[...] = (total + b_ref[...].astype(F32) + c_ref[...].astype(F32)).astype(BF16)

    return whole_call(body, [(768, 256)], (near,) + parts)[0]


def combine(hidden, back, routes_t):
    def body(hidden_ref, back_ref, routes_ref, out_ref):
        mixed = lax.dot_general(
            tables_of(routes_ref[...]),
            back_ref[...],
            (((0,), (0,)), ((), ())),
            preferred_element_type=F32,
        )
        out_ref[...] = (hidden_ref[...].astype(F32) + mixed).astype(BF16)

    return call(
        body,
        (),
        (1,),
        [
            pl.BlockSpec((256, 256), lambda i: (0, 0)),
            pl.BlockSpec((768, 256), lambda i: (0, 0)),
            pl.BlockSpec((2, 256), lambda i: (0, 0)),
        ],
        pl.BlockSpec((256, 256), lambda i: (0, 0)),
        jax.ShapeDtypeStruct((256, 256), BF16),
    )(hidden, back, routes_t)


def assemble(target, parts, base=None):
    def body(target_ref, parts_ref, *refs):
        for piece in range(4):
            refs[-1][:, piece * 256 : piece * 256 + 256] = parts_ref[piece]

    return call(
        body,
        (target,),
        (2,),
        [pl.BlockSpec((4, 256, 256), lambda i, t: (i, 0, 0))]
        + ([] if base is None else [pl.BlockSpec(memory_space=pl.ANY)]),
        pl.BlockSpec((256, 1024), lambda i, t: (0, t[0] * 2 + i)),
        jax.ShapeDtypeStruct((256, 4096), BF16),
        alias=None if base is None else {2: 0},
    )(target, parts, *(() if base is None else (base,)))


def per_device(
    x_rows,
    lengths,
    routes,
    conv_state,
    ssm_state,
    norm1_gain,
    in_x,
    in_z,
    conv_w,
    conv_b,
    x_dt,
    x_bc,
    dt_proj,
    dt_bias,
    decay_rate,
    skip,
    out_w,
    norm2_gain,
    router,
    w_gate,
    w_up,
    w_down,
):
    core_at = lax.axis_index("core").astype(jnp.int32)
    core = core_at.reshape(1)
    chip_at = lax.axis_index(CHIPS).astype(jnp.int32)
    block = (core_at * 8 + chip_at).reshape(1)
    expert_at = lax.axis_index(DP).astype(jnp.int32)

    place = jnp.stack(
        [core_at, lax.axis_index("z").astype(jnp.int32), lax.axis_index("ylo").astype(jnp.int32)]
    )
    low_weight = jnp.concatenate([x_dt, x_bc, jnp.zeros((512, 96), BF16)], axis=1)
    history = jnp.pad(conv_state.astype(F32), ((0, 0), (5, 0), (0, 0)))
    routes_t = routes.T
    router_row = lax.dynamic_slice(router, (0, expert_at), (4096, 1)).astype(F32).reshape(1, 4096)

    rows_mine, rows_send = norm_split(place, x_rows, norm1_gain.reshape(1, 4096))
    pair_own = swap_pair(rows_send)
    x_below, x_above = from_below(in_x), from_above(in_x)
    x_halves = (x_below[:256], x_above[256:])
    x_blocks = gather_ring(in_x, x_below, x_above, x_halves)
    pair_other = swap_core(after(pair_own, *x_halves))
    both = after(jnp.concatenate([in_z, out_w]), pair_other, *x_blocks[3:5])
    both_below, both_above = from_below(both), from_above(both)
    out_pair = swap_pair(after(out_w, pair_own))
    x_far = swap_pair(pair_product(place, pair_own, pair_other, x_blocks))
    sends = second_round(both_below, both_above, out_pair)
    x_near = own_product(rows_mine, x_blocks)
    conv, low = conv_project(
        core, x_near, x_far, history, conv_w, conv_b.reshape(1, 512), low_weight
    )
    low_pair = add_half(low[0], swap_core(low[1]))
    inverse = 1.0 / norm2_gain.reshape(1, 4096)
    low_pair = after(low_pair, router_row, inverse, *sends)
    low_two = add_half(low_pair, swap_far(low_pair))
    low_four = add_half(low_two, lax.ppermute(low_two, "x", [(i, i ^ 1) for i in range(4)]))
    up, down, over = from_below(sends[0]), from_above(sends[1]), swap_pair(sends[2])
    low_own = add_half(low_four, lax.ppermute(low_four, "x", [(i, i ^ 2) for i in range(4)]))
    low_other = swap_core(low_own)
    mixed, final = scan_block(
        core,
        lengths,
        low_own,
        low_other,
        conv,
        dt_proj,
        dt_bias.reshape(1, 512),
        decay_rate,
        skip.reshape(1, 512),
        ssm_state,
    )
    z_blocks = (in_z, both_below, both_above, up, down)
    z_far = swap_pair(pair_product(place, pair_own, pair_other, z_blocks))
    corner = third_round(up, down, over)
    z_near = own_product(rows_mine, z_blocks)
    out_blocks = (out_w, both_below, both_above, out_pair, up, down, over) + corner
    mixer_own, mixer_other = mixer_product(place, mixed, z_near, z_far, out_blocks)
    mixer_pair = (mixer_own.astype(F32) + swap_core(mixer_other).astype(F32)).astype(BF16)
    mixer_parts = exchange(mixer_pair.reshape(8, 256, 256), CHIPS)
    places = block_places(
        core_at, lax.axis_index("x").astype(jnp.int32), lax.axis_index("yhi").astype(jnp.int32)
    )
    gain = norm2_gain.reshape(1, 4096)
    hidden, outgoing = hidden_dispatch(block, mixer_parts, x_rows, gain, routes_t)
    rows = exchange(outgoing.reshape(8, 96, 256), DP).reshape(768, 256)
    left, right, cross = from_left(rows), from_right(rows), swap_far(rows)
    near = (rows, left, right, cross)
    near_other = tuple(swap_core(value) for value in near)
    top, bottom = slice(0, 384), slice(384, 768)
    up = from_left(jnp.concatenate([left[top], cross[top]]))
    down = from_right(jnp.concatenate([right[bottom], cross[bottom]]))
    over = swap_far(jnp.concatenate([right[top], left[bottom]]))
    held = gate_up(places, 0, near + near_other, inverse, router_row, w_gate[0], w_up[0])
    up, down, over = (after(value, held[2]) for value in (up, down, over))
    two = jnp.concatenate([up[top], down[top]])
    cross_left = jnp.concatenate([up[bottom], over[bottom]])
    cross_right = jnp.concatenate([over[top], down[bottom]])
    cross_two = jnp.concatenate(
        [from_left(cross_left[0:256]), from_right(cross_right[256:512]), swap_far(two[512:768])]
    )
    far = (two, cross_left, cross_right, cross_two)
    far_other = tuple(swap_core(value) for value in far)
    active = gate_up(places, 4, far + far_other, inverse, router_row, w_gate[0], w_up[0], held)
    far_sent = swap_core(down_product(places, 12, active, w_down[0]))
    near_sent = swap_core(down_product(places, 8, active, w_down[0]))
    far_sum = down_product(places, 4, active, w_down[0], far_sent)
    corner = (
        from_left(far_sum[3, 0:256]),
        from_right(far_sum[3, 256:512]),
        swap_far(far_sum[3, 512:768]),
    )
    near_sum = down_product(places, 0, active, w_down[0], near_sent)
    up_send, down_send, cross_send = fold_far(far_sum, corner)
    to_left, to_right, to_row = fold_near(
        near_sum, from_left(up_send), from_right(down_send), swap_far(cross_send)
    )
    total = fold_own(near_sum, (from_left(to_right), from_right(to_left), swap_far(to_row)))
    back = exchange(total.reshape(8, 96, 256), DP).reshape(768, 256)
    out_own = spread(combine(hidden, back, routes_t))
    out_other = swap_core(out_own)
    out_rows = assemble((1 - core_at).reshape(1), out_other, assemble(core, out_own))
    return (out_rows, final)


def solution(mesh):
    wide = Mesh(mesh.devices.reshape(4, 2, 2, 4, 2), ("z", "ylo", "yhi", "x", "core"))
    return jax.shard_map(
        per_device,
        mesh=wide,
        in_specs=(
            P(DP, None),
            P(DP),
            P(DP, None),
            P(DP, None, TENSOR),
            P(DP, None, TENSOR),
            P(),
            P(DP, TENSOR),
            P(DP, TENSOR),
            P(None, TENSOR),
            P(TENSOR),
            P(TENSOR, None),
            P(TENSOR, None),
            P(None, TENSOR),
            P(TENSOR),
            P(None, TENSOR),
            P(TENSOR),
            P(TENSOR, DP),
            P(),
            P(),
            P(DP, None, TENSOR),
            P(DP, None, TENSOR),
            P(DP, TENSOR, None),
        ),
        out_specs=(P(DP, None), P(DP, None, TENSOR)),
        check_vma=False,
    )
```
